128 devices in a mesh: dp: 32 (over y, z_hi, x), mp: 4 (over z_lo, core).
Axes of the slice: x: 4, y: 4, z: 4 (z_hi: 2, z_lo: 2; z = z_hi * 2 + z_lo), core: 2. Of those that a mesh axis runs over, the one named last changes fastest.
Arguments:
- tokens: bfloat16 [32768, 1024], P('dp'), may hold values from -6 to 6
- lengths: int32 [32, 8], P('dp'), may hold values from 1 to 768, 1024 in all within a row
- norm_gain_one: float32 [1024], replicated, may hold values from 0.5 to 1.5
- w_query: bfloat16 [1024, 512], P(None, 'mp'), may hold values from -0.1875 to 0.1875
- w_key: bfloat16 [1024, 512], P(None, 'mp'), may hold values from -0.1875 to 0.1875
- w_value: bfloat16 [1024, 1024], P(None, 'mp'), may hold values from -0.1875 to 0.1875
- w_gate_down: bfloat16 [1024, 16], replicated, may hold values from -0.1875 to 0.1875
- w_gate_up: bfloat16 [16, 512], P(None, 'mp'), may hold values from -1.5 to 1.5
- gate_bias: float32 [512], P('mp'), may hold values from -4.5 to 4.5
- w_out: bfloat16 [1024, 1024], P('mp'), may hold values from -0.09375 to 0.09375
- norm_gain_two: float32 [1024], replicated, may hold values from 0.5 to 1.5
- w_mlp_gate: bfloat16 [1024, 2816], P(None, 'mp'), may hold values from -0.1875 to 0.1875
- w_mlp_up: bfloat16 [1024, 2816], P(None, 'mp'), may hold values from -0.1875 to 0.1875
- w_mlp_down: bfloat16 [2816, 1024], P('mp'), may hold values from -0.109375 to 0.109375
- cotangent: bfloat16 [32768, 1024], P('dp'), may hold values from -6 to 6
Outputs:
- result: bfloat16 [32768, 1024], P('dp')
- grad_tokens: float32 [32768, 1024], P('dp')
- grad_gain_one: float32 [1024], replicated
- grad_query: float32 [1024, 512], P('dp', 'mp')
- grad_key: float32 [1024, 512], P('dp', 'mp')
- grad_value: float32 [1024, 1024], P('dp', 'mp')
- grad_gate_down: float32 [1024, 16], replicated
- grad_gate_up: float32 [16, 512], P(None, 'mp')
- grad_gate_bias: float32 [512], P('mp')
- grad_out: float32 [1024, 1024], P('mp', 'dp')
- grad_gain_two: float32 [1024], replicated
- grad_mlp_gate: float32 [1024, 2816], P('dp', 'mp')
- grad_mlp_up: float32 [1024, 2816], P('dp', 'mp')
- grad_mlp_down: float32 [2816, 1024], P('mp', 'dp')
The draws below stay inside these ranges and needn't reach their ends.
Inputs may be any that keep to these rules, and one draw needn't show every extreme that they name: `lengths`: each row sums to 1024, and its largest length is exactly 768.
All inputs are finite; a program needn't handle non-finite values.
Results may differ from the reference program's by a relative error of at most 0.02.
Values sent between devices are 32-bit elements; how exact they have to be, the bound alone decides.
No kernel may reach another device: no remote copies, remote signals or barrier semaphores. Data moves between devices by JAX's collectives and lax.ppermute only.
A program may use at most 128 MiB of HBM per device.

```python
import math
import jax
import jax.numpy as jnp
import numpy as np
from jax import lax

D = 1024
H = 4
DK = 128
DV = 256
R = 16
FF = 2816
BLK = 64
ITEMS = 8
TOK_GRP = 1024
MOST = 768
TOKENS = 32768
N_DP = 32


def block_levels(key, extent, cuts, smallest, top_value):
    def one(position, parts):
        steps = jax.random.uniform(jax.random.fold_in(jax.random.fold_in(key, 6), position), (parts,), jnp.float32, smallest / len(cuts), top_value / len(cuts))
        return jnp.repeat(jnp.exp(steps), extent[position] // parts).reshape((-1,) + (1,) * (len(extent) - position - 1))

    level = one(*cuts[0])
    for cut in cuts[1:]:
        level = level * one(*cut)
    return level


def profile(amount, total, limit, skew):
    portions = [(1 << 20) // math.isqrt(rank ** skew) + 1 for rank in range(2, amount + 1)]
    spare, holding = total - limit - (amount - 1), [1] * (amount - 1)
    while spare > 0:
        candidates = [i for i in range(amount - 1) if holding[i] < limit]
        mass, remaining = sum([portions[i] for i in candidates]), spare
        for i in candidates:
            more = min(limit - holding[i], max(1, remaining * portions[i] // mass), spare)
            holding[i] = holding[i] + more
            spare = spare - more
    return np.array([limit] + holding)


def uneven_parts(own_key, number_of, total, reach, lean):
    if number_of == 2:
        one = jax.random.randint(own_key, (), max(1, total - reach), min(reach, total - 1) + 1)
        return jnp.stack([one, total - one])
    tallies = jnp.asarray(profile(number_of, total, reach, lean), jnp.int32)
    twos = (number_of - 1) // 2
    source_of, receiver = tallies[1:1 + 2 * twos:2], tallies[2:2 + 2 * twos:2]
    margin = jnp.minimum(source_of - 1, reach - receiver)
    moved = jax.random.randint(jax.random.fold_in(own_key, 1), (twos,), 0, 1 << 20) % (margin + 1)
    tallies = tallies.at[1:1 + 2 * twos:2].set(source_of - moved).at[2:2 + 2 * twos:2].set(receiver + moved)
    return tallies[jax.random.permutation(jax.random.fold_in(own_key, 2), number_of)]


def noise(key, extent, scale, limit, shards=(), kind=jnp.bfloat16):
    level = block_levels(key, extent, shards, -0.22, 0.18) if shards else 1.0
    entries = jax.random.normal(key, extent, jnp.float32) * scale * level
    return jnp.minimum(jnp.maximum(entries, -limit), limit).astype(kind)


def setup_inputs(seed: int = 0) -> dict:
    streams_of = jax.random.split(jax.random.key(seed), 16)
    return {
        "tokens": noise(streams_of[0], (TOKENS, D), 1.0, 6.0, ((0, 32),)),
        "lengths": jax.vmap(lambda own: uneven_parts(own, ITEMS, TOK_GRP, MOST, 2))(jax.random.split(streams_of[1], N_DP)).reshape((N_DP, ITEMS)).astype(jnp.int32),
        "norm_gain_one": jnp.clip(1.0 + 0.1 * jax.random.normal(streams_of[2], (D,), jnp.float32), 0.5, 1.5),
        "w_query": noise(streams_of[3], (D, H * DK), D ** -0.5, 0.1875, ((1, 4),)),
        "w_key": noise(streams_of[4], (D, H * DK), D ** -0.5, 0.1875, ((1, 4),)),
        "w_value": noise(streams_of[5], (D, H * DV), D ** -0.5, 0.1875, ((1, 4),)),
        "w_gate_down": noise(streams_of[6], (D, R), D ** -0.5, 0.1875),
        "w_gate_up": noise(streams_of[7], (R, H * DK), R ** -0.5, 1.5, ((1, 4),)),
        "gate_bias": noise(streams_of[8], (H * DK,), 1.5, 4.5, ((0, 4),), jnp.float32),
        "w_out": noise(streams_of[9], (H * DV, D), (4 * H * DV) ** -0.5, 0.09375, ((0, 4),)),
        "norm_gain_two": jnp.clip(1.0 + 0.1 * jax.random.normal(streams_of[10], (D,), jnp.float32), 0.5, 1.5),
        "w_mlp_gate": noise(streams_of[11], (D, FF), D ** -0.5, 0.1875, ((1, 4),)),
        "w_mlp_up": noise(streams_of[12], (D, FF), D ** -0.5, 0.1875, ((1, 4),)),
        "w_mlp_down": noise(streams_of[13], (FF, D), FF ** -0.5, 0.109375, ((0, 4),)),
        "cotangent": noise(streams_of[14], (TOKENS, D), 1.0, 6.0, ((0, 32),)),
    }


gate_normalizer = 16.0
norm_epsilon = 1e-06

@jax.custom_vjp
def low(v):
    return lax.optimization_barrier(v.astype(jnp.bfloat16)).astype(jnp.float32)

@jax.custom_vjp
def low_back(v):
    return v

def low_keep(v):
    return (low(v), None)

def low_pass(kept, grad):
    return (grad,)

def back_keep(v):
    return (v, None)

def back_low(kept, grad):
    return (low(grad),)
low.defvjp(low_keep, low_pass)
low_back.defvjp(back_keep, back_low)

def exact_dot(left_side, right_side):
    return jnp.dot(left_side, right_side, precision=lax.Precision.HIGHEST)

def norm_apply(values, gains):
    inverse_rms = lax.rsqrt(lax.optimization_barrier(jnp.mean(values * values, axis=-1, keepdims=True)) + norm_epsilon)
    return values * inverse_rms * gains

def item_index(item_lengths):
    places = jnp.arange(TOK_GRP, dtype=jnp.int32)
    starts = jnp.cumsum(item_lengths) - item_lengths
    return lax.optimization_barrier(jnp.sum((places[:, None] >= starts[None, :]).astype(jnp.int32), axis=1)) - 1

def span_step(carry_state, pieces):
    query_rows, key_rows, value_rows, decay_rows, item_ids, before = pieces
    cumulative = jnp.cumsum(decay_rows, axis=0)
    block_end = cumulative[-1]
    q_scaled = low(query_rows * query_rows.shape[-1] ** (-0.5) * jnp.exp(cumulative))
    k_scaled = low(key_rows * jnp.exp(-cumulative))
    k_final = low(key_rows * jnp.exp(block_end - cumulative))
    places = jnp.arange(item_ids.shape[0])
    visible = (item_ids[:, None] == item_ids[None, :]) & (places[:, None] >= places[None, :])
    scores = low(jnp.where(visible, exact_dot(q_scaled, k_scaled.T), 0.0))
    carried = (item_ids == before)[:, None]
    outputs = exact_dot(scores, value_rows) + jnp.where(carried, exact_dot(q_scaled, low(carry_state)), 0.0)
    keep_state = jnp.where(item_ids[-1] == before, 1.0, 0.0)
    tail_keys = jnp.where((item_ids == item_ids[-1])[:, None], k_final, 0.0)
    new_state = keep_state * jnp.exp(block_end)[:, None] * carry_state + exact_dot(tail_keys.T, value_rows)
    return (new_state, outputs)

def gla_head(queries, keysets, valueset, decays, item_ids):
    blocks = item_ids.shape[0] // BLK
    before = jnp.concatenate([jnp.full((1,), -1, dtype=jnp.int32), item_ids[BLK - 1::BLK][:-1].astype(jnp.int32)])
    start_state = jnp.zeros((keysets.shape[1], valueset.shape[1]), jnp.float32)
    pieces = (queries.reshape(blocks, BLK, -1), keysets.reshape(blocks, BLK, -1), valueset.reshape(blocks, BLK, -1), decays.reshape(blocks, BLK, -1), item_ids.reshape(blocks, BLK), before)
    unused, outputs = lax.scan(jax.checkpoint(span_step), start_state, pieces)
    return outputs.reshape(-1, valueset.shape[1])

def gla_heads(queries, keysets, valueset, decays, item_ids):
    row_count = queries.shape[0]
    heads = queries.shape[1] // DK
    mapped = jax.vmap(gla_head, in_axes=(1, 1, 1, 1, None), out_axes=1)
    mixed_heads = mapped(queries.reshape(row_count, heads, DK), keysets.reshape(row_count, heads, DK), valueset.reshape(row_count, heads, DV), decays.reshape(row_count, heads, DK), item_ids)
    return mixed_heads.reshape(row_count, heads * DV)

def layer(inputs, gain_one, query_w, key_w, value_w, gate_down_w, gate_up_w, bias_gate, out_w, gain_two, mlp_gate_w, mlp_up_w, mlp_down_w, item_ids):
    normed_one = low(norm_apply(inputs, gain_one))
    queries = low_back(low(exact_dot(normed_one, query_w)))
    keysets = low_back(low(exact_dot(normed_one, key_w)))
    valueset = low_back(low(exact_dot(normed_one, value_w)))
    low_rank = low(exact_dot(normed_one, gate_down_w))
    logits = exact_dot(low_rank, gate_up_w) + bias_gate
    decays = jax.nn.log_sigmoid(logits) / gate_normalizer
    mixed_low = low_back(low(gla_heads(queries, keysets, valueset, decays, item_ids)))
    attention = low_back(exact_dot(mixed_low, out_w))
    middle = inputs + attention
    normed_two = low(norm_apply(middle, gain_two))
    gate_pre = low_back(exact_dot(normed_two, mlp_gate_w))
    up_pre = low_back(exact_dot(normed_two, mlp_up_w))
    hidden = low(jax.nn.silu(gate_pre) * up_pre)
    return middle + exact_dot(hidden, mlp_down_w)

def reference(tokens, lengths, norm_gain_one, w_query, w_key, w_value, w_gate_down, w_gate_up, gate_bias, w_out, norm_gain_two, w_mlp_gate, w_mlp_up, w_mlp_down, cotangent):
    params = tuple((p.astype(jnp.float32) for p in (norm_gain_one, w_query, w_key, w_value, w_gate_down, w_gate_up, gate_bias, w_out, norm_gain_two, w_mlp_gate, w_mlp_up, w_mlp_down)))
    group_tokens = tokens.astype(jnp.float32).reshape(N_DP, TOK_GRP, D)
    group_cots = cotangent.astype(jnp.float32).reshape(N_DP, TOK_GRP, D)

    def group_step(totals, pieces):
        inputs, cots, item_lengths = pieces
        item_ids = item_index(item_lengths)

        def forward(inputs, *weights):
            return layer(inputs, *weights, item_ids)
        outputs, backward = jax.vjp(forward, inputs, *params)
        grads = backward(cots)
        totals = tuple((total + grad for total, grad in zip(totals, grads[1:])))
        return (totals, (outputs, grads[0]))
    start_totals = tuple((jnp.zeros_like(p) for p in params))
    totals, (outputs, input_grads) = lax.scan(group_step, start_totals, (group_tokens, group_cots, lengths))
    return (outputs.reshape(TOKENS, D).astype(jnp.bfloat16), input_grads.reshape(TOKENS, D), totals[0], totals[1], totals[2], totals[3], totals[4], totals[5], totals[6], totals[7], totals[8], totals[9], totals[10], totals[11])
```

```python
import jax
import jax.numpy as jnp
from jax import lax
from jax.experimental import pallas as pl
from jax.experimental.pallas import tpu as pltpu
from jax.sharding import PartitionSpec as P

BLK = 64
CH = 256
EPS = 1e-6
SCALE = 128 ** -0.5
F32 = jnp.float32
BF16 = jnp.bfloat16
VMEM_BYTES = 56 * 1024 * 1024


def nn(a, b, **kw):
    return lax.dot_general(a, b, (((1,), (0,)), ((), ())), preferred_element_type=F32, **kw)


def nt(a, b, **kw):
    return lax.dot_general(a, b, (((1,), (1,)), ((), ())), preferred_element_type=F32, **kw)


def tn(a, b, **kw):
    return lax.dot_general(a, b, (((0,), (0,)), ((), ())), preferred_element_type=F32, **kw)


HIGH = dict(precision=lax.Precision.HIGHEST)


CORE = [(0, 1), (1, 0), (2, 3), (3, 2)]
ZLO = [(0, 2), (2, 0), (1, 3), (3, 1)]


def dp_perm(dy, dz, dx):
    out = []
    for y in range(4):
        for z in range(2):
            for x in range(4):
                out.append(((y * 2 + z) * 4 + x, (((y + dy) % 4) * 2 + (z + dz) % 2) * 4 + (x + dx) % 4))
    return out


XS = {1: dp_perm(0, 0, 1), 3: dp_perm(0, 0, -1), 2: dp_perm(0, 0, 2)}
YS = {1: dp_perm(1, 0, 0), 3: dp_perm(-1, 0, 0), 2: dp_perm(2, 0, 0)}
ZH = dp_perm(0, 1, 0)


def core_swap(v):
    return lax.ppermute(v, "mp", CORE)


def z_swap(v):
    return lax.ppermute(v, "mp", ZLO)


def rows_of(v, start, size):
    return lax.dynamic_slice_in_dim(v, start, size, 0)


def item_starts(len_ref):
    starts, total = [], jnp.int32(0)
    for j in range(8):
        starts.append(total)
        total = total + len_ref[0, j]
    return starts


def start_at(starts, place):
    best = jnp.int32(0)
    for s in starts[1:]:
        best = jnp.where(s <= place, jnp.maximum(best, s), best)
    return best


def chunk_masks(starts, base):
    row = lax.broadcasted_iota(jnp.int32, (CH, CH), 0)
    col = lax.broadcasted_iota(jnp.int32, (CH, CH), 1)
    blk = jnp.bitwise_and(row, -BLK)
    row1 = lax.broadcasted_iota(jnp.int32, (CH, 128), 0)
    place = row1 + base
    low = jnp.zeros_like(place)
    for s in starts[1:]:
        low = jnp.where(place >= s, jnp.maximum(low, s), low)
    low = low - base
    blk1 = jnp.bitwise_and(row1, -BLK)
    carried = low < blk1
    low_wide = jnp.concatenate([low, low], axis=1)
    causal = (col <= row) & (col >= blk)
    visible = causal & (col >= low_wide)
    return causal, visible, carried


def block_scalars(starts, base, b):
    first = base + b * BLK
    origin = start_at(starts, first + BLK - 1)
    keep = jnp.where(origin < first, 1.0, 0.0).astype(F32)
    place = lax.broadcasted_iota(jnp.int32, (BLK, 128), 0) + first
    return keep, place >= origin


def scaled_parts(q, k, cum):
    last = jnp.broadcast_to(cum.reshape(CH // BLK, BLK, 128)[:, BLK - 1 :, :], (CH // BLK, BLK, 128))
    last = last.reshape(CH, 128)
    e, en, ef = jnp.exp(cum), jnp.exp(-cum), jnp.exp(last - cum)
    qf = q.astype(F32) * SCALE * e
    ks = k.astype(F32) * en
    kf = k.astype(F32) * ef
    return last, e, en, ef, qf, ks, kf


def mixer_forward(
    len_ref, tok_ref, g1_ref, wq_ref, wk_ref, wv_ref, wgd_ref, wgu_ref, bias_ref,
    n_ref, q_ref, k_ref, v_ref, low_ref, logit_ref, cum_ref, mixed_ref, st_ref, state,
):
    step = pl.program_id(0)
    base = step * CH
    starts = item_starts(len_ref)

    @pl.when(step == 0)
    def _():
        state[...] = jnp.zeros_like(state)

    x = tok_ref[...].astype(F32)
    r = lax.rsqrt(jnp.mean(x * x, axis=-1, keepdims=True) + EPS)
    n = (x * r * g1_ref[...]).astype(BF16)
    n_ref[...] = n
    q = nn(n, wq_ref[...]).astype(BF16)
    k = nn(n, wk_ref[...]).astype(BF16)
    v = nn(n, wv_ref[...]).astype(BF16)
    low = nn(n, wgd_ref[...]).astype(BF16)
    q_ref[...] = q
    k_ref[...] = k
    v_ref[...] = v
    low_ref[...] = low
    logits = nn(low, wgu_ref[...]) + bias_ref[...]
    logit_ref[...] = logits
    decays = (jnp.minimum(logits, 0.0) - jnp.log1p(jnp.exp(-jnp.abs(logits)))) * (1.0 / 16.0)
    causal, visible, carried = chunk_masks(starts, base)
    cum = nn(jnp.where(causal, 1.0, 0.0).astype(F32), decays, **HIGH)
    cum_ref[...] = cum
    last, e, en, ef, qf, ks, kf = scaled_parts(q, k, cum)
    qs, ks, kf = qf.astype(BF16), ks.astype(BF16), kf.astype(BF16)
    scores = jnp.where(visible, nt(qs, ks), 0.0).astype(BF16)
    out = nn(scores, v)
    q_carried = jnp.where(carried, qf, 0.0).astype(BF16)
    for b in range(CH // BLK):
        sl = slice(b * BLK, (b + 1) * BLK)
        keep, tail = block_scalars(starts, base, b)
        s = state[...]
        st_ref[b] = s
        inter = nt(q_carried[sl], s.astype(BF16))
        mixed_ref[sl, :] = (out[sl] + inter).astype(BF16).astype(F32)
        k_tail = jnp.where(tail, kf[sl].astype(F32), 0.0).astype(BF16)
        state[...] = keep * jnp.exp(last[b * BLK : b * BLK + 1]) * s + tn(v[sl], k_tail)


def run_mixer_forward(lengths, tokens, g1, wq, wk, wv, wgd, wgu, bias):
    t = tokens.shape[0]
    whole = lambda a: pl.BlockSpec(a.shape, lambda i: (0,) * a.ndim)
    rows = lambda c: pl.BlockSpec((CH, c), lambda i: (i, 0))
    nb = CH // BLK
    outs = [
        ((t, 1024), BF16), ((t, 128), BF16), ((t, 128), BF16), ((t, 256), BF16), ((t, 16), BF16),
        ((t, 128), F32), ((t, 128), F32), ((t, 256), F32),
    ]
    return pl.pallas_call(
        mixer_forward,
        grid=(t // CH,),
        in_specs=[pl.BlockSpec(memory_space=pltpu.SMEM), rows(1024), whole(g1), whole(wq), whole(wk), whole(wv),
                  whole(wgd), whole(wgu), whole(bias)],
        out_specs=[rows(s[1]) for s, _ in outs] + [pl.BlockSpec((nb, 256, 128), lambda i: (i, 0, 0))],
        out_shape=[jax.ShapeDtypeStruct(s, d) for s, d in outs] + [jax.ShapeDtypeStruct((t // BLK, 256, 128), F32)],
        scratch_shapes=[pltpu.VMEM((256, 128), F32)],
        compiler_params=pltpu.CompilerParams(vmem_limit_bytes=VMEM_BYTES),
        cost_estimate=pl.CostEstimate(flops=2 * t * 1024 * 600, bytes_accessed=12 << 20, transcendentals=t * 700),
        name="mixer_forward",
    )(lengths, tokens, g1, wq, wk, wv, wgd, wgu, bias)


def feed_kernel(
    tok_ref, cot_ref, m0_ref, m1_ref, m2_ref, m3_ref, w0_ref, w1_ref, w2_ref, w3_ref, g2_ref, wg_ref, wu_ref, wd_ref,
    mid_ref, n_ref, hid_ref, gg_ref, feed_ref, part_ref, wo,
):
    @pl.when(pl.program_id(0) == 0)
    def _():
        wo[0:256] = w0_ref[...]
        wo[256:512] = w1_ref[...].astype(BF16)
        wo[512:768] = w2_ref[...].astype(BF16)
        wo[768:1024] = w3_ref[...].astype(BF16)

    mixed = jnp.concatenate([m0_ref[...], m1_ref[...], m2_ref[...], m3_ref[...]], axis=1).astype(BF16)
    mid = tok_ref[...].astype(F32) + nn(mixed, wo[...])
    mid_ref[...] = mid
    r = lax.rsqrt(jnp.mean(mid * mid, axis=-1, keepdims=True) + EPS)
    n = (mid * r * g2_ref[...]).astype(BF16)
    n_ref[...] = n
    pre = nn(n, wg_ref[...])
    up = nn(n, wu_ref[...])
    sg = jax.nn.sigmoid(pre)
    act = pre * sg
    hid = (act * up).astype(BF16)
    hid_ref[...] = hid
    feed_ref[...] = nn(hid, wd_ref[...])
    gh = nt(cot_ref[...], wd_ref[...])
    gg = (gh * up * sg * (1.0 + pre * (1.0 - sg))).astype(BF16)
    gu = (gh * act).astype(BF16)
    gg_ref[:, 0:704] = gg
    gg_ref[:, 704:1408] = gu
    part_ref[...] = nt(gg, wg_ref[...]) + nt(gu, wu_ref[...])


def run_feed(start, count, tokens, cot, mixed, wo, g2, wg, wu, wd):
    first = start // CH
    whole = lambda a: pl.BlockSpec(a.shape, lambda i: (0,) * a.ndim)
    rows = lambda c: pl.BlockSpec((CH, c), lambda i: (first + i, 0))
    outr = lambda c: pl.BlockSpec((CH, c), lambda i: (i, 0))
    outs = [((count, 1024), F32), ((count, 1024), BF16), ((count, 704), BF16), ((count, 1408), BF16),
            ((count, 1024), F32), ((count, 1024), F32)]
    return pl.pallas_call(
        feed_kernel,
        grid=(count // CH,),
        in_specs=[rows(1024), rows(1024)] + [rows(256)] * 4 + [whole(w) for w in wo] + [whole(g2), whole(wg), whole(wu), whole(wd)],
        out_specs=[outr(s[1]) for s, _ in outs],
        out_shape=[jax.ShapeDtypeStruct(s, d) for s, d in outs],
        scratch_shapes=[pltpu.VMEM((1024, 1024), BF16)],
        compiler_params=pltpu.CompilerParams(vmem_limit_bytes=VMEM_BYTES),
        cost_estimate=pl.CostEstimate(flops=2 * count * 1024 * 5300, bytes_accessed=count * 22000, transcendentals=count * 704),
        name="feed_both_ways",
    )(tokens, cot, *mixed, *wo, g2, wg, wu, wd)


def mixer_backward(
    len_ref, gm_ref, tok_ref, n_ref, q_ref, k_ref, v_ref, low_ref, logit_ref, cum_ref, st_ref,
    wo_ref, wq_ref, wk_ref, wv_ref, wgd_ref, wgu_ref,
    dqkv_ref, part_ref, ga_ref, small_ref, gup_ref, bias_ref, dstate, dq_s, dv_s, dk_s, dl_s,
):
    step = pl.program_id(0)
    steps = pl.num_programs(0)
    base = (steps - 1 - step) * CH
    starts = item_starts(len_ref)

    @pl.when(step == 0)
    def _():
        dstate[...] = jnp.zeros_like(dstate)
        small_ref[...] = jnp.zeros_like(small_ref)
        gup_ref[...] = jnp.zeros_like(gup_ref)
        bias_ref[...] = jnp.zeros_like(bias_ref)

    ga = gm_ref[...].astype(BF16)
    ga_ref[...] = ga
    g = nt(ga, wo_ref[...]).astype(BF16)
    q, k, v, cum = q_ref[...], k_ref[...], v_ref[...], cum_ref[...]
    causal, visible, carried = chunk_masks(starts, base)
    last, e, en, ef, qf, ksf, kff = scaled_parts(q, k, cum)
    qs, ks, kf = qf.astype(BF16), ksf.astype(BF16), kff.astype(BF16)
    scores = jnp.where(visible, nt(qs, ks), 0.0).astype(BF16)
    dscores = jnp.where(visible, nt(g, v), 0.0).astype(BF16)
    dv = tn(scores, g)
    dqs = nn(dscores, ks)
    dks = tn(dscores, qs)
    q_carried = jnp.where(carried, qf, 0.0).astype(BF16)
    for b in reversed(range(CH // BLK)):
        sl = slice(b * BLK, (b + 1) * BLK)
        keep, tail = block_scalars(starts, base, b)
        ds = dstate[...]
        dsb = ds.astype(BF16)
        s = st_ref[b]
        k_tail = jnp.where(tail, kff[sl], 0.0).astype(BF16)
        dv_s[sl, :] = dv[sl] + nt(k_tail, dsb)
        dkf = jnp.where(tail, nn(v[sl], dsb), 0.0)
        dk_s[sl, :] = dkf
        dq_s[sl, :] = dqs[sl] + jnp.where(carried[sl], nn(g[sl], s.astype(BF16)), 0.0)
        grow = keep * jnp.exp(last[b * BLK : b * BLK + 1])
        dlast = grow * jnp.sum(s * ds, axis=0, keepdims=True) + jnp.sum(dkf * kff[sl], axis=0, keepdims=True)
        dl_s[sl, :] = jnp.broadcast_to(dlast, (BLK, 128))
        dstate[...] = grow * ds + tn(g[sl], q_carried[sl])
    dqs = dq_s[...]
    dkf = dk_s[...]
    dq = (dqs * (SCALE * e)).astype(BF16)
    dk = (dks * en + dkf * ef).astype(BF16)
    dv = dv_s[...].astype(BF16)
    dqkv_ref[:, 0:128] = dq
    dqkv_ref[:, 128:256] = dk
    dqkv_ref[:, 256:512] = dv
    dcum = dqs * qf - dks * ksf - dkf * kff
    ddec = tn(jnp.where(causal, 1.0, 0.0).astype(F32), dcum, **HIGH) + dl_s[...]
    glog = ddec * jax.nn.sigmoid(-logit_ref[...]) * (1.0 / 16.0)
    bias_ref[0:1, :] += jnp.sum(glog, axis=0, keepdims=True)
    gup_ref[...] += tn(low_ref[...].astype(F32), glog, **HIGH)
    glr = nt(glog, wgu_ref[...].astype(F32), **HIGH).astype(BF16)
    part = nt(dq, wq_ref[...]) + nt(dk, wk_ref[...]) + nt(dv, wv_ref[...]) + nt(glr, wgd_ref[...])
    part_ref[...] = part
    small_ref[0:16, :] += tn(glr, n_ref[...])
    x = tok_ref[...].astype(F32)
    r = lax.rsqrt(jnp.mean(x * x, axis=-1, keepdims=True) + EPS)
    small_ref[16:17, :] += jnp.sum(part * x * r, axis=0, keepdims=True)


def run_mixer_backward(lengths, gm, tokens, n, q, k, v, low, logits, cum, st, wo, wq, wk, wv, wgd, wgu):
    t = tokens.shape[0]
    steps = t // CH
    whole = lambda a: pl.BlockSpec(a.shape, lambda i: (0,) * a.ndim)
    rows = lambda c: pl.BlockSpec((CH, c), lambda i: (steps - 1 - i, 0))
    nb = CH // BLK
    fixed = lambda s: pl.BlockSpec(s, lambda i: (0, 0))
    return pl.pallas_call(
        mixer_backward,
        grid=(steps,),
        in_specs=[pl.BlockSpec(memory_space=pltpu.SMEM), rows(1024), rows(1024), rows(1024), rows(128), rows(128), rows(256),
                  rows(16), rows(128), rows(128), pl.BlockSpec((nb, 256, 128), lambda i: (steps - 1 - i, 0, 0)),
                  whole(wo), whole(wq), whole(wk), whole(wv), whole(wgd), whole(wgu)],
        out_specs=[rows(512), rows(1024), rows(1024), fixed((24, 1024)), fixed((16, 128)), fixed((8, 128))],
        out_shape=[jax.ShapeDtypeStruct((t, 512), BF16), jax.ShapeDtypeStruct((t, 1024), F32),
                   jax.ShapeDtypeStruct((t, 1024), BF16), jax.ShapeDtypeStruct((24, 1024), F32),
                   jax.ShapeDtypeStruct((16, 128), F32), jax.ShapeDtypeStruct((8, 128), F32)],
        scratch_shapes=[pltpu.VMEM((256, 128), F32), pltpu.VMEM((CH, 128), F32), pltpu.VMEM((CH, 256), F32),
                        pltpu.VMEM((CH, 128), F32), pltpu.VMEM((CH, 128), F32)],
        compiler_params=pltpu.CompilerParams(vmem_limit_bytes=VMEM_BYTES),
        cost_estimate=pl.CostEstimate(flops=2 * t * 1024 * 1200, bytes_accessed=20 << 20, transcendentals=t * 600),
        name="mixer_backward",
    )(lengths, gm, tokens, n, q, k, v, low, logits, cum, st, wo, wq, wk, wv, wgd, wgu)


def mp_scatter(part, core, z):
    half, quarter = part.shape[0] // 2, part.shape[0] // 4
    acc = rows_of(part, core * half, half) + core_swap(rows_of(part, (1 - core) * half, half))
    return rows_of(acc, z * quarter, quarter) + z_swap(rows_of(acc, (1 - z) * quarter, quarter))


def paired(own, other, bit):
    first = jnp.where(bit == 0, own, other)
    second = jnp.where(bit == 0, other, own)
    return jnp.concatenate([first, second], axis=0)


def mp_join(own, core, z):
    half = paired(own, z_swap(own), z)
    return paired(half, core_swap(half), core)


def norm_back(y, gain, dn):
    r = lax.rsqrt(jnp.mean(y * y, axis=-1, keepdims=True) + EPS)
    gd = dn * gain
    dy = r * gd - r * r * r * y * jnp.mean(gd * y, axis=-1, keepdims=True)
    return dy, jnp.sum(dn * y * r, axis=0)


def direct_scatter(chunk, at, shifts):
    total = chunk(at)
    for d in (2, 1, 3):
        total = total + lax.ppermute(chunk((at + d) % 4), "dp", shifts[d])
    return total


def dp_scatter(grads, y, zh, x):
    cut = [g.reshape(4, 2, 4, 2, 16, g.shape[1]) for g in grads]

    def take_x(i, h):
        return jnp.concatenate([lax.dynamic_index_in_dim(g, i, 2, False)[:, :, h] for g in cut], axis=-1)

    def take_y(i, h):
        return jnp.concatenate([lax.dynamic_index_in_dim(g, i, 0, False)[:, :, h] for g in cut], axis=-1)

    a = direct_scatter(lambda i: take_x(i, 0), x, XS)
    b = direct_scatter(lambda i: take_y(i, 1), y, YS)
    a = direct_scatter(lambda i: lax.dynamic_index_in_dim(a, i, 0, False), y, YS)
    b = direct_scatter(lambda i: lax.dynamic_index_in_dim(b, i, 1, False), x, XS)
    ab = jnp.concatenate([a, b], axis=1)
    mine = lax.dynamic_index_in_dim(ab, zh, 0, False)
    return mine + lax.ppermute(lax.dynamic_index_in_dim(ab, 1 - zh, 0, False), "dp", ZH)


def dp_total(v):
    for perm in (XS[1], XS[2], YS[1], YS[2], ZH):
        pass
    v = v + lax.ppermute(v, "dp", XS[2])
    v = v + lax.ppermute(v, "dp", XS[1])
    v = v + lax.ppermute(v, "dp", YS[2])
    v = v + lax.ppermute(v, "dp", YS[1])
    return v + lax.ppermute(v, "dp", ZH)


FEED_CHUNKS = 2


def local(tokens, lengths, g1, wq, wk, wv, wgd, wgu, bias, wout, g2, wg, wu, wd, cot):
    mp, dp = lax.axis_index("mp"), lax.axis_index("dp")
    core, z = mp % 2, mp // 2
    x, zh, y = dp % 4, (dp // 4) % 2, dp // 8
    t = tokens.shape[0]
    g1r, g2r, biasr = g1.reshape(1, -1), g2.reshape(1, -1), bias.reshape(1, -1)

    wide = wout.astype(F32)
    wout_z = z_swap(wide)
    wout_c = core_swap(wide)
    wout_cz = core_swap(wout_z)
    wo = (wout, wout_z, wout_c, wout_cz)

    n1, q, k, v, low, logits, cum, mixed, st = run_mixer_forward(lengths, tokens, g1r, wq, wk, wv, wgd, wgu, biasr)
    mixed_z = z_swap(mixed)
    mixed_c = core_swap(mixed)
    mixed_cz = core_swap(mixed_z)
    mixed_all = (mixed, mixed_z, mixed_c, mixed_cz)

    size = t // FEED_CHUNKS
    quarter = size // 4
    parts = {}
    for c in reversed(range(FEED_CHUNKS)):
        parts[c] = run_feed(c * size, size, tokens, cot, mixed_all, wo, g2r, wg, wu, wd)
    joined = [jnp.concatenate([parts[c][j] for c in range(FEED_CHUNKS)], axis=0) for j in range(4)]
    middle, n2, hid, gg = joined

    own_at = [c * size + core * (size // 2) + z * quarter for c in range(FEED_CHUNKS)]
    gm_own, gm_full = [None] * FEED_CHUNKS, [None] * FEED_CHUNKS
    gain2 = 0.0
    dns = {c: mp_scatter(parts[c][5], core, z) for c in reversed(range(FEED_CHUNKS))}
    for c in reversed(range(FEED_CHUNKS)):
        dmid, gain = norm_back(rows_of(middle, own_at[c], quarter), g2, dns[c])
        gain2 = gain2 + gain
        gm_own[c] = rows_of(cot, own_at[c], quarter).astype(F32) + dmid
        gm_full[c] = mp_join(gm_own[c], core, z)
    grad_middle = jnp.concatenate(gm_full, axis=0)

    grad_gate_up_t = tn(n2, gg)
    grad_down_t = tn(cot, hid)
    mlp_rows = dp_scatter([grad_gate_up_t, grad_down_t], y, zh, x)

    dqkv, part1, ga, small, gup, gbias = run_mixer_backward(
        lengths, grad_middle, tokens, n1, q, k, v, low, logits, cum, st, wout, wq, wk, wv, wgd, wgu)

    feed = jnp.concatenate([mp_join(mp_scatter(parts[c][4], core, z), core, z) for c in range(FEED_CHUNKS)], axis=0)
    result = (middle + feed).astype(BF16)

    own1 = core * (t // 2) + z * (t // 4)
    dn1 = mp_scatter(part1, core, z)
    dx, _ = norm_back(rows_of(tokens, own1, t // 4).astype(F32), g1, dn1)
    grad_tokens = mp_join(dx, core, z) + grad_middle

    grad_qkv = tn(n1, dqkv)
    grad_out_t = tn(ga, mixed.astype(BF16))
    att_rows = dp_scatter([grad_qkv, grad_out_t], y, zh, x)

    shared = jnp.concatenate([small[0:17], gain2.reshape(1, 1024), jnp.zeros((6, 1024), F32)], axis=0)
    shared = shared + core_swap(shared)
    shared = shared + z_swap(shared)
    rest = jnp.concatenate([gup.reshape(2, 1024), jnp.pad(gbias[0:1], ((0, 5), (0, 896)))], axis=0)
    total = dp_total(jnp.concatenate([shared, rest], axis=0))

    return (
        result,
        grad_tokens,
        total[16],
        att_rows[:, 0:128],
        att_rows[:, 128:256],
        att_rows[:, 256:512],
        total[0:16].T,
        total[24:26].reshape(16, 128),
        total[26, 0:128],
        att_rows[:, 512:768].T,
        total[17],
        mlp_rows[:, 0:704],
        mlp_rows[:, 704:1408],
        mlp_rows[:, 1408:2112].T,
    )


def solution(mesh):
    placed = (
        P("dp", None), P("dp", None), P(), P(None, "mp"), P(None, "mp"), P(None, "mp"), P(), P(None, "mp"),
        P("mp"), P("mp", None), P(), P(None, "mp"), P(None, "mp"), P("mp", None), P("dp", None),
    )
    outs = (
        P("dp", None), P("dp", None), P(), P("dp", "mp"), P("dp", "mp"), P("dp", "mp"), P(), P(None, "mp"),
        P("mp"), P("mp", "dp"), P(), P("dp", "mp"), P("dp", "mp"), P("mp", "dp"),
    )
    return jax.shard_map(local, mesh=mesh, in_specs=placed, out_specs=outs, check_vma=False)
```

```python
import functools

import jax
import jax.numpy as jnp
from jax import lax
from jax.experimental import pallas as pl
from jax.experimental.pallas import tpu as pltpu
from jax.sharding import PartitionSpec as P

BLK = 64
CH = 256
EPS = 1e-6
SCALE = 128 ** -0.5
F32 = jnp.float32
BF16 = jnp.bfloat16
VMEM_BYTES = 63_400_000
BACK_US = 8
FWD_ROWS = 256
BWD_ROWS = 256


def weight(us):
    return pl.CostEstimate(flops=int(us * 1.0e4), bytes_accessed=1024, transcendentals=0)


def nn(a, b, **kw):
    return lax.dot_general(a, b, (((1,), (0,)), ((), ())), preferred_element_type=F32, **kw)


def nt(a, b, **kw):
    return lax.dot_general(a, b, (((1,), (1,)), ((), ())), preferred_element_type=F32, **kw)


def tn(a, b, **kw):
    return lax.dot_general(a, b, (((0,), (0,)), ((), ())), preferred_element_type=F32, **kw)


HIGH = dict(precision=lax.Precision.HIGHEST)


CORE = [(0, 1), (1, 0), (2, 3), (3, 2)]
ZLO = [(0, 2), (2, 0), (1, 3), (3, 1)]


def dp_perm(dy, dz, dx):
    out = []
    for y in range(4):
        for z in range(2):
            for x in range(4):
                out.append(((y * 2 + z) * 4 + x, (((y + dy) % 4) * 2 + (z + dz) % 2) * 4 + (x + dx) % 4))
    return out


XS = {1: dp_perm(0, 0, 1), 3: dp_perm(0, 0, -1), 2: dp_perm(0, 0, 2)}
YS = {1: dp_perm(1, 0, 0), 3: dp_perm(-1, 0, 0), 2: dp_perm(2, 0, 0)}
ZH = dp_perm(0, 1, 0)


def core_swap(v):
    return lax.ppermute(v, "mp", CORE)


def z_swap(v):
    return lax.ppermute(v, "mp", ZLO)


def rows_of(v, start, size):
    return lax.dynamic_slice_in_dim(v, start, size, 0)


def item_starts(len_ref):
    starts, total = [], jnp.int32(0)
    for j in range(8):
        starts.append(total)
        total = total + len_ref[0, j]
    return starts


def start_at(starts, place):
    best = jnp.int32(0)
    for s in starts[1:]:
        best = jnp.where(s <= place, jnp.maximum(best, s), best)
    return best


def chunk_masks(starts, base):
    row = lax.broadcasted_iota(jnp.int32, (CH, CH), 0)
    col = lax.broadcasted_iota(jnp.int32, (CH, CH), 1)
    blk = jnp.bitwise_and(row, -BLK)
    row1 = lax.broadcasted_iota(jnp.int32, (CH, 128), 0)
    place = row1 + base
    low = jnp.zeros_like(place)
    for s in starts[1:]:
        low = jnp.where(place >= s, jnp.maximum(low, s), low)
    low = low - base
    blk1 = jnp.bitwise_and(row1, -BLK)
    carried = low < blk1
    low_wide = jnp.concatenate([low, low], axis=1)
    causal = (col <= row) & (col >= blk)
    visible = causal & (col >= low_wide)
    return visible, carried


def causal_ones():
    row = lax.broadcasted_iota(jnp.int32, (CH, CH), 0)
    col = lax.broadcasted_iota(jnp.int32, (CH, CH), 1)
    return jnp.where((col <= row) & (col >= jnp.bitwise_and(row, -BLK)), 1.0, 0.0).astype(BF16)


def two_parts(v):
    high = v.astype(BF16)
    return high, (v - high.astype(F32)).astype(BF16)


def block_scalars(starts, base, b):
    first = base + b * BLK
    origin = start_at(starts, first + BLK - 1)
    keep = jnp.where(origin < first, 1.0, 0.0).astype(F32)
    place = lax.broadcasted_iota(jnp.int32, (BLK, 128), 0) + first
    return keep, place >= origin


def scaled_parts(q, k, cum):
    last = jnp.broadcast_to(cum.reshape(CH // BLK, BLK, 128)[:, BLK - 1 :, :], (CH // BLK, BLK, 128))
    last = last.reshape(CH, 128)
    e, en, ef = jnp.exp(cum), jnp.exp(-cum), jnp.exp(last - cum)
    qf = q.astype(F32) * SCALE * e
    ks = k.astype(F32) * en
    kf = k.astype(F32) * ef
    return last, e, en, ef, qf, ks, kf


def mixer_forward(
    len_ref, tok_ref, g1_ref, wq_ref, wk_ref, wv_ref, wgd_ref, wgu_ref, bias_ref,
    n_ref, q_ref, k_ref, v_ref, low_ref, logit_ref, cum_ref, mixed_lo_ref, mixed_hi_ref, st_ref, state,
):
    step = pl.program_id(0)
    rows = tok_ref.shape[0]
    starts = item_starts(len_ref)

    @pl.when(step == 0)
    def _():
        state[...] = jnp.zeros_like(state)

    ones = causal_ones()
    s = state[...]
    for c in range(rows // CH):
        base = step * rows + c * CH
        at = slice(c * CH, (c + 1) * CH)
        x = tok_ref[at, :].astype(F32)
        r = lax.rsqrt(jnp.mean(x * x, axis=-1, keepdims=True) + EPS)
        n = (x * r * g1_ref[...]).astype(BF16)
        n_ref[at, :] = n
        low = nt(n, wgd_ref[...]).astype(BF16)
        low_ref[at, :] = low
        logits = nn(low, wgu_ref[...]) + bias_ref[...]
        logit_ref[at, :] = logits
        decays = (jnp.minimum(logits, 0.0) - jnp.log1p(jnp.exp(-jnp.abs(logits)))) * (1.0 / 16.0)
        high, rest = two_parts(decays)
        cum = nn(ones, high) + nn(ones, rest)
        cum_ref[at, :] = cum
        q = nn(n, wq_ref[...]).astype(BF16)
        k = nn(n, wk_ref[...]).astype(BF16)
        v = nn(n, wv_ref[...]).astype(BF16)
        q_ref[at, :] = q
        k_ref[at, :] = k
        v_ref[at, :] = v
        visible, carried = chunk_masks(starts, base)
        last, e, en, ef, qf, ks, kf = scaled_parts(q, k, cum)
        scores = jnp.where(visible, nt(qf.astype(BF16), ks.astype(BF16)), 0.0).astype(BF16)
        out = nn(scores, v)
        q_carried = jnp.where(carried, qf, 0.0).astype(BF16)
        mixed_parts = []
        for b in range(CH // BLK):
            sl = slice(b * BLK, (b + 1) * BLK)
            keep, tail = block_scalars(starts, base, b)
            st_ref[c * (CH // BLK) + b] = s
            inter = nt(q_carried[sl], s.astype(BF16))
            mixed_parts.append((out[sl] + inter).astype(BF16).astype(F32))
            k_tail = jnp.where(tail, kf[sl], 0.0).astype(BF16)
            s = keep * jnp.exp(last[b * BLK : b * BLK + 1]) * s + tn(v[sl], k_tail)
        mixed = jnp.concatenate(mixed_parts, axis=0)

        @pl.when(step < 2)
        def _(mixed=mixed):
            mixed_lo_ref[...] = mixed

        @pl.when(step >= 2)
        def _(mixed=mixed):
            mixed_hi_ref[...] = mixed

    state[...] = s


def run_mixer_forward(lengths, tokens, g1, wq, wk, wv, wgd, wgu, bias):
    t = tokens.shape[0]
    whole = lambda a: pl.BlockSpec(a.shape, lambda i: (0,) * a.ndim)
    rows = lambda c: pl.BlockSpec((CH, c), lambda i: (i, 0))
    nb = CH // BLK
    outs = [
        ((t, 1024), BF16), ((t, 128), BF16), ((t, 128), BF16), ((t, 256), BF16), ((t, 16), BF16), ((t, 128), F32), ((t, 128), F32),
    ]
    sds = jax.ShapeDtypeStruct
    return pl.pallas_call(
        mixer_forward,
        grid=(t // CH,),
        in_specs=[pl.BlockSpec(memory_space=pltpu.SMEM), rows(1024), whole(g1), whole(wq), whole(wk), whole(wv),
                  whole(wgd), whole(wgu), whole(bias)],
        out_specs=[rows(s[1]) for s, _ in outs]
        + [pl.BlockSpec((CH, 256), lambda i: (jnp.minimum(i, 1), 0)), pl.BlockSpec((CH, 256), lambda i: (jnp.maximum(i - 2, 0), 0)),
           pl.BlockSpec((nb, 256, 128), lambda i: (i, 0, 0))],
        out_shape=[sds(s, d) for s, d in outs] + [sds((t // 2, 256), F32)] * 2 + [sds((t // BLK, 256, 128), F32)],
        scratch_shapes=[pltpu.VMEM((256, 128), F32)],
        compiler_params=pltpu.CompilerParams(vmem_limit_bytes=VMEM_BYTES),
        cost_estimate=weight(10),
        name="mixer_forward",
    )(lengths, tokens, g1, wq, wk, wv, wgd, wgu, bias)


def before_feed_kernel(w0_ref, w1_ref, w2_ref, w3_ref, cot_ref, wd_ref, wo_ref, gh_ref):
    for j, w_ref in enumerate((w0_ref, w1_ref, w2_ref, w3_ref)):

        @pl.when(pl.program_id(0) == j)
        def _(w_ref=w_ref):
            wo_ref[...] = w_ref[...].astype(BF16)

    gh_ref[...] = nt(cot_ref[...], wd_ref[...])


def run_before_feed(wo, cot, wd):
    t = cot.shape[0]
    whole = lambda a: pl.BlockSpec(a.shape, lambda s: (0,) * a.ndim)
    rows = lambda c: pl.BlockSpec((CH, c), lambda s: (s, 0))
    return pl.pallas_call(
        before_feed_kernel,
        grid=(t // CH,),
        in_specs=[whole(w) for w in wo] + [rows(1024), whole(wd)],
        out_specs=[rows(1024), rows(704)],
        out_shape=[jax.ShapeDtypeStruct((t, 1024), BF16), jax.ShapeDtypeStruct((t, 704), F32)],
        compiler_params=pltpu.CompilerParams(vmem_limit_bytes=VMEM_BYTES),
        cost_estimate=weight(1),
        name="before_feed",
    )(*wo, cot, wd)


def feed_kernel(
    at_ref, tok_ref, gh_ref, m0_ref, m1_ref, m2_ref, m3_ref, wo_ref, g2_ref, wg_ref, wu_ref, wd_ref,
    mid_ref, n_ref, hid_ref, gg_ref, feed_out_ref, feed_keep_ref, part_out_ref, part_keep_ref,
):
    step = pl.program_id(0)

    mixed = jnp.concatenate([m0_ref[...], m1_ref[...], m2_ref[...], m3_ref[...]], axis=1).astype(BF16)
    mid = tok_ref[...].astype(F32) + nn(mixed, wo_ref[...])
    mid_ref[...] = mid
    r = lax.rsqrt(jnp.mean(mid * mid, axis=-1, keepdims=True) + EPS)
    n = (mid * r * g2_ref[...]).astype(BF16)
    n_ref[...] = n
    pre = nt(n, wg_ref[...])
    up = nt(n, wu_ref[...])
    sg = jax.nn.sigmoid(pre)
    act = pre * sg
    hid = (act * up).astype(BF16)
    hid_ref[...] = hid
    gh = gh_ref[...]
    gg = (gh * up * sg * (1.0 + pre * (1.0 - sg))).astype(BF16)
    gu = (gh * act).astype(BF16)
    gg_ref[:, 0:704] = gg
    gg_ref[:, 704:1408] = gu
    feed = nn(hid, wd_ref[...])
    part = nn(gg, wg_ref[...]) + nn(gu, wu_ref[...])

    @pl.when(step == 0)
    def _():
        feed_out_ref[...] = feed
        part_out_ref[...] = part

    @pl.when(step == 1)
    def _():
        feed_keep_ref[...] = feed
        part_keep_ref[...] = part


def run_feed(at, chunk, tokens, gh, mixed, wo, g2, wg, wu, wd):
    t = tokens.shape[0] // 2
    whole = lambda a: pl.BlockSpec(a.shape, lambda s, at: (0,) * a.ndim)
    half = lambda s, at: jnp.bitwise_xor(1 - at[2], s)
    rows = lambda c: pl.BlockSpec((CH, c), lambda s, at: (half(s, at), 0))
    from_all = lambda c: pl.BlockSpec((CH, c), lambda s, at: (2 * chunk + half(s, at), 0))
    once = pl.BlockSpec((CH, 1024), lambda s, at: (0, 0))
    sds = jax.ShapeDtypeStruct
    return pl.pallas_call(
        feed_kernel,
        grid_spec=pltpu.PrefetchScalarGridSpec(
            num_scalar_prefetch=1,
            grid=(t // CH,),
            in_specs=[from_all(1024), from_all(704)] + [rows(256)] * 4 + [whole(wo), whole(g2), whole(wg), whole(wu), whole(wd)],
            out_specs=[rows(1024), rows(1024), rows(704), rows(1408), once, once, once, once],
        ),
        out_shape=[sds((t, 1024), F32), sds((t, 1024), BF16), sds((t, 704), BF16), sds((t, 1408), BF16)] + [sds((CH, 1024), F32)] * 4,
        compiler_params=pltpu.CompilerParams(vmem_limit_bytes=VMEM_BYTES),
        cost_estimate=weight(10),
        name="feed_both_ways",
    )(at, tokens, gh, *mixed, wo, g2, wg, wu, wd)


def mixer_backward(
    at_ref, len_ref, *refs,
):
    gm_refs, gain_refs, refs = refs[:8], refs[8:10], refs[10:]
    (tok_ref, n_ref, q_ref, k_ref, v_ref, low_ref, logit_ref, cum_ref,
     st_ref, wo_ref, wq_ref, wk_ref, wv_ref, wgd_ref, wgu_ref,
     dqkv_ref, part_out_ref, part_keep_ref, ga_ref, small_ref, gup_ref, bias_ref, dstate) = refs
    step = pl.program_id(0)
    steps = pl.num_programs(0)
    rows = tok_ref.shape[0]
    starts = item_starts(len_ref)

    core, z = at_ref[2], at_ref[3]
    here = steps - 1 - step
    mine = jnp.equal(lax.rem(here, 2), core)

    @pl.when(step == 0)
    def _():
        dstate[...] = jnp.zeros_like(dstate)
        small_ref[...] = jnp.zeros_like(small_ref)
        small_ref[17:18, :] = gain_refs[0][0:1, :] + gain_refs[1][0:1, :]
        gup_ref[...] = jnp.zeros_like(gup_ref)
        bias_ref[...] = jnp.zeros_like(bias_ref)

    first = pl.multiple_of(z * 128, 128)
    second = pl.multiple_of((1 - z) * 128, 128)
    for chunk in range(2):
        for other in range(2):
            wanted = jnp.logical_not(mine) if other else mine

            @pl.when(jnp.logical_and(jnp.equal(lax.div(here, 2), chunk), wanted))
            def _(chunk=chunk, other=other):
                ga_ref[pl.ds(first, 128), :] = gm_refs[4 * chunk + 2 * other][...].astype(BF16)
                ga_ref[pl.ds(second, 128), :] = gm_refs[4 * chunk + 2 * other + 1][...].astype(BF16)

    ones = causal_ones()
    ds = dstate[...]
    for c in reversed(range(rows // CH)):
        base = here * rows + c * CH
        at = slice(c * CH, (c + 1) * CH)
        g = nt(ga_ref[at, :], wo_ref[...]).astype(BF16)
        q, k, v, cum = q_ref[at, :], k_ref[at, :], v_ref[at, :], cum_ref[at, :]
        visible, carried = chunk_masks(starts, base)
        last, e, en, ef, qf, ksf, kff = scaled_parts(q, k, cum)
        qs, ks = qf.astype(BF16), ksf.astype(BF16)
        scores = jnp.where(visible, nt(qs, ks), 0.0).astype(BF16)
        dscores = jnp.where(visible, nt(g, v), 0.0).astype(BF16)
        dv = tn(scores, g)
        dqs = nn(dscores, ks)
        dks = tn(dscores, qs)
        q_carried = jnp.where(carried, qf, 0.0).astype(BF16)
        dvs, dkfs, dqss, dls = [], [], [], []
        for b in reversed(range(CH // BLK)):
            sl = slice(b * BLK, (b + 1) * BLK)
            keep, tail = block_scalars(starts, base, b)
            dsb = ds.astype(BF16)
            s = st_ref[c * (CH // BLK) + b]
            k_tail = jnp.where(tail, kff[sl], 0.0).astype(BF16)
            dvs.append(dv[sl] + nt(k_tail, dsb))
            dkf = jnp.where(tail, nn(v[sl], dsb), 0.0)
            dkfs.append(dkf)
            dqss.append(dqs[sl] + jnp.where(carried[sl], nn(g[sl], s.astype(BF16)), 0.0))
            grow = keep * jnp.exp(last[b * BLK : b * BLK + 1])
            dlast = grow * jnp.sum(s * ds, axis=0, keepdims=True) + jnp.sum(dkf * kff[sl], axis=0, keepdims=True)
            dls.append(jnp.broadcast_to(dlast, (BLK, 128)))
            ds = grow * ds + tn(g[sl], q_carried[sl])
        join = lambda parts: jnp.concatenate(parts[::-1], axis=0)
        dqs, dkf, dl = join(dqss), join(dkfs), join(dls)
        dq = (dqs * (SCALE * e)).astype(BF16)
        dk = (dks * en + dkf * ef).astype(BF16)
        dv = join(dvs).astype(BF16)
        dqkv_ref[at, 0:128] = dq
        dqkv_ref[at, 128:256] = dk
        dqkv_ref[at, 256:512] = dv
        high, rest = two_parts(dqs * qf - dks * ksf - dkf * kff)
        ddec = tn(ones, high) + tn(ones, rest) + dl
        glog = ddec * jax.nn.sigmoid(-logit_ref[at, :]) * (1.0 / 16.0)
        bias_ref[0:1, :] += jnp.sum(glog, axis=0, keepdims=True)
        high, rest = two_parts(glog)
        gup_ref[...] += tn(low_ref[at, :], high) + tn(low_ref[at, :], rest)
        glr = (nt(high, wgu_ref[...]) + nt(rest, wgu_ref[...])).astype(BF16)
        part = nt(dq, wq_ref[...]) + nt(dk, wk_ref[...]) + nt(dv, wv_ref[...]) + nn(glr, wgd_ref[...])
        @pl.when(mine)
        def _(part=part):
            part_keep_ref[...] = part

        @pl.when(jnp.logical_not(mine))
        def _(part=part):
            part_out_ref[...] = part

        small_ref[0:16, :] += tn(glr, n_ref[at, :])
        x = tok_ref[at, :].astype(F32)
        r = lax.rsqrt(jnp.mean(x * x, axis=-1, keepdims=True) + EPS)
        small_ref[16:17, :] += jnp.sum(part * x * r, axis=0, keepdims=True)
    dstate[...] = ds


def run_mixer_backward(at, lengths, gm, gains, tokens, n, q, k, v, low, logits, cum, st, wo, wq, wk, wv, wgd, wgu):
    t = tokens.shape[0]
    steps = t // CH
    whole = lambda a: pl.BlockSpec(a.shape, lambda i, at: (0,) * a.ndim)
    rows = lambda c: pl.BlockSpec((CH, c), lambda i, at: (steps - 1 - i, 0))
    split = pl.BlockSpec((CH, 1024), lambda i, at: (lax.div(steps - 1 - i, 2), 0))
    nb = CH // BLK
    fixed = lambda s: pl.BlockSpec(s, lambda i, at: (0, 0))
    sds = jax.ShapeDtypeStruct
    return pl.pallas_call(
        mixer_backward,
        grid_spec=pltpu.PrefetchScalarGridSpec(
            num_scalar_prefetch=1,
            grid=(steps,),
            in_specs=[pl.BlockSpec(memory_space=pltpu.SMEM)] + [whole(g) for g in (*gm, *gains)]
            + [rows(1024), rows(1024), rows(128), rows(128), rows(256), rows(16), rows(128), rows(128),
               pl.BlockSpec((nb, 256, 128), lambda i, at: (steps - 1 - i, 0, 0)),
               whole(wo), whole(wq), whole(wk), whole(wv), whole(wgd), whole(wgu)],
            out_specs=[rows(512), split, split, rows(1024), fixed((24, 1024)), fixed((16, 128)), fixed((8, 128))],
            scratch_shapes=[pltpu.VMEM((256, 128), F32)],
        ),
        out_shape=[sds((t, 512), BF16), sds((t // 2, 1024), F32), sds((t // 2, 1024), F32), sds((t, 1024), BF16),
                   sds((24, 1024), F32), sds((16, 128), F32), sds((8, 128), F32)],
        compiler_params=pltpu.CompilerParams(vmem_limit_bytes=VMEM_BYTES),
        cost_estimate=weight(BACK_US),
        name="mixer_backward",
    )(at, lengths, *gm, *gains, tokens, n, q, k, v, low, logits, cum, st, wo, wq, wk, wv, wgd, wgu)


SMALL = dict(
    compiler_params=pltpu.CompilerParams(vmem_limit_bytes=VMEM_BYTES),
    cost_estimate=weight(0.1),
)


def add_kernel(at_ref, *refs):
    out_ref = refs[-1]
    n = out_ref.shape[0] // (len(refs) // 2)
    for j in range(len(refs) // 2):
        out_ref[j * n : (j + 1) * n] = refs[2 * j][...] + refs[2 * j + 1][...]


def add_quarter(at, *pairs):
    ops, specs = [], []
    for pair in pairs:
        for j in range(pair[0].shape[0] // 256):
            ops += pair
            specs += [pl.BlockSpec((128, 1024), lambda s, at, j=j: (2 * j + 1 - at[3], 0))] * 2
    n = 64 * len(ops)
    return pl.pallas_call(
        add_kernel,
        grid_spec=pltpu.PrefetchScalarGridSpec(
            num_scalar_prefetch=1, grid=(1,), in_specs=specs, out_specs=pl.BlockSpec((n, 1024), lambda s, at: (0, 0))),
        out_shape=jax.ShapeDtypeStruct((n, 1024), F32),
        name="add_quarter",
        **SMALL,
    )(at, *ops)


def quarter_sum_kernel(at_ref, a0_ref, b0_ref, a1_ref, b1_ref, c_ref, o_ref):
    o_ref[0:128] = a0_ref[...] + b0_ref[...] + c_ref[0:128]
    o_ref[128:256] = a1_ref[...] + b1_ref[...] + c_ref[128:256]


def run_quarter_sum(at, pairs, c):
    of_half = pl.BlockSpec((128, 1024), lambda s, at: (at[3], 0))
    own = pl.BlockSpec((256, 1024), lambda s, at: (0, 0))
    return pl.pallas_call(
        quarter_sum_kernel,
        grid_spec=pltpu.PrefetchScalarGridSpec(
            num_scalar_prefetch=1, grid=(1,), in_specs=[of_half] * 4 + [own], out_specs=own),
        out_shape=jax.ShapeDtypeStruct((256, 1024), F32),
        name="quarter_sum",
        **SMALL,
    )(at, *pairs[0], *pairs[1], c)


def norm_gradient(dn, y, gain):
    r = lax.rsqrt(jnp.mean(y * y, axis=-1, keepdims=True) + EPS)
    gd = dn * gain
    dy = r * gd - (r * r * r) * y * jnp.mean(gd * y, axis=-1, keepdims=True)
    return dy, jnp.sum(dn * y * r, axis=0, keepdims=True)


def second_norm_kernel(at_ref, a_ref, b_ref, c_ref, y_ref, gain_ref, base_ref, o_ref, s_ref):
    dn = a_ref[...] + b_ref[...] + c_ref[...]
    dy, dgain = norm_gradient(dn, y_ref[...], gain_ref[...])
    o_ref[...] = base_ref[...].astype(F32) + dy
    s_ref[0:1, :] = dgain


def run_second_norm(at, chunk, a, b, c, middle, gain, cot):
    of_half = pl.BlockSpec((128, 1024), lambda s, at: (at[3], 0))
    of_chunk = pl.BlockSpec((128, 1024), lambda s, at: (2 * at[2] + at[3], 0))
    of_all = pl.BlockSpec((128, 1024), lambda s, at: (4 * chunk + 2 * at[2] + at[3], 0))
    fixed = lambda s: pl.BlockSpec(s, lambda s, at: (0, 0))
    return pl.pallas_call(
        second_norm_kernel,
        grid_spec=pltpu.PrefetchScalarGridSpec(
            num_scalar_prefetch=1, grid=(1,),
            in_specs=[of_half, of_half, fixed((128, 1024)), of_chunk, fixed((1, 1024)), of_all],
            out_specs=[fixed((128, 1024)), fixed((8, 1024))]),
        out_shape=[jax.ShapeDtypeStruct((128, 1024), F32), jax.ShapeDtypeStruct((8, 1024), F32)],
        name="second_norm_back",
        **SMALL,
    )(at, a, b, c, middle, gain, cot)


def first_norm_kernel(at_ref, a_ref, b_ref, c_ref, y_ref, gain_ref, o_ref):
    o_ref[...] = norm_gradient(a_ref[...] + b_ref[...] + c_ref[...], y_ref[...].astype(F32), gain_ref[...])[0]


def run_first_norm(at, a, b, c, tokens, gain):
    of_half = pl.BlockSpec((128, 1024), lambda s, at: (2 * s + at[3], 0))
    of_all = pl.BlockSpec((128, 1024), lambda s, at: (4 * s + 2 * at[2] + at[3], 0))
    own = pl.BlockSpec((128, 1024), lambda s, at: (s, 0))
    return pl.pallas_call(
        first_norm_kernel,
        grid_spec=pltpu.PrefetchScalarGridSpec(
            num_scalar_prefetch=1, grid=(2,),
            in_specs=[of_half, of_half, own, of_all, pl.BlockSpec((1, 1024), lambda s, at: (0, 0))], out_specs=own),
        out_shape=jax.ShapeDtypeStruct((256, 1024), F32),
        name="first_norm_back",
        **SMALL,
    )(at, a, b, c, tokens, gain)


def join_kernel(at_ref, *refs, pieces):
    step = pl.program_id(0)
    out_ref = refs[-1]
    for chunk in range(2):
        for j in range(2):

            @pl.when(step == chunk * 2 + j)
            def _(j=j, chunk=chunk):
                other = refs[2 + 2 * chunk + j] if pieces else refs[2 + chunk]
                out_ref[...] = (refs[j][...] + other[...]).astype(out_ref.dtype)


def run_join(at, odd, first, second, dtype, into=None):
    pieces = len(second) == 4
    chunk = lambda s: lax.div(s, 2)
    place = lambda s, at: jnp.bitwise_xor(2 * at[2] + at[3], 2 * lax.rem(s, 2) + odd)
    own = pl.BlockSpec((128, 1024), lambda s, at: (chunk(s), 0))
    whole = pl.BlockSpec((128, 1024), lambda s, at: (0, 0))
    low = pl.BlockSpec((128, 1024), lambda s, at: (place(jnp.minimum(s, 1), at), 0))
    high = pl.BlockSpec((128, 1024), lambda s, at: (place(jnp.maximum(s, 2), at), 0))
    placed = pl.BlockSpec((128, 1024), lambda s, at: (4 * chunk(s) + place(s, at), 0))
    more = [] if into is None else [into]
    ops = [*first, *second, *more]
    return pl.pallas_call(
        functools.partial(join_kernel, pieces=pieces),
        grid_spec=pltpu.PrefetchScalarGridSpec(
            num_scalar_prefetch=1, grid=(4,),
            in_specs=[own] * 2 + ([whole] * 4 if pieces else [low, high]) + [pl.BlockSpec(memory_space=pl.ANY)] * len(more),
            out_specs=placed),
        out_shape=jax.ShapeDtypeStruct((1024, 1024), dtype),
        input_output_aliases={len(ops): 0} if more else {},
        name="join_rows",
        **SMALL,
    )(at, *ops)


def feed_grads_kernel(at_ref, *refs):
    (l0_ref, l1_ref, r0_ref, r1_ref, c0_ref, c1_ref, h0_ref, h1_ref), outs = refs[:8], refs[8:]
    step = pl.program_id(0)
    w1 = r0_ref.shape[1]
    first = tn(l0_ref[...], r0_ref[...]) + tn(l1_ref[...], r1_ref[...])
    second = tn(c0_ref[...], h0_ref[...]) + tn(c1_ref[...], h1_ref[...])

    def write(ref, x):
        for zh in range(2):
            row = zh * 128 + x * 32
            ref[0, zh, :, 0:w1] = first[row : row + 32]
            ref[0, zh, :, w1:] = second[row : row + 32]

    for x in range(4):
        offset = lax.rem(x - at_ref[0] + 4, 4)
        for k, ref in ((0, outs[0]), (1, outs[1]), (3, outs[4])):

            @pl.when(offset == k)
            def _(x=x, ref=ref):
                write(ref, x)

        @pl.when(jnp.logical_and(offset == 2, step < 2))
        def _(x=x):
            write(outs[2], x)

        @pl.when(jnp.logical_and(offset == 2, step >= 2))
        def _(x=x):
            write(outs[3], x)


def run_feed_grads(at, n2, gg, cot, hid):
    t = cot.shape[0] // 2
    c = gg[0].shape[1] + hid[0].shape[1]
    cols = lambda j: pl.BlockSpec((t, CH), lambda s, at: (j, s))
    whole = lambda a: pl.BlockSpec(a.shape, lambda s, at: (0, 0))
    along = lambda f: pl.BlockSpec((1, 2, 32, c), lambda s, at: (f(s), 0, 0, 0))
    each = along(lambda s: s)
    return pl.pallas_call(
        feed_grads_kernel,
        grid_spec=pltpu.PrefetchScalarGridSpec(
            num_scalar_prefetch=1, grid=(4,),
            in_specs=[cols(0), cols(0), whole(gg[0]), whole(gg[1]), cols(0), cols(1), whole(hid[0]), whole(hid[1])],
            out_specs=[each, each, along(lambda s: jnp.minimum(s, 1)), along(lambda s: jnp.maximum(s - 2, 0)), each]),
        out_shape=[jax.ShapeDtypeStruct((n, 2, 32, c), F32) for n in (4, 4, 2, 2, 4)],
        compiler_params=pltpu.CompilerParams(vmem_limit_bytes=VMEM_BYTES),
        cost_estimate=weight(1),
        name="feed_weight_grads",
    )(at, n2[0], n2[1], gg[0], gg[1], cot, cot, hid[0], hid[1])


def mixer_grads_kernel(at_ref, l_ref, r0_ref, a0_ref, m0_ref, m1_ref, small_ref, core_ref, far_ref, gup_ref, bias_ref, *outs):
    step = pl.program_id(0)
    w1 = r0_ref.shape[1]

    @pl.when(step < 4)
    def _():
        n = m0_ref.shape[0]
        first = tn(l_ref[...], r0_ref[...])
        second = tn(a0_ref[0:n], m0_ref[...].astype(BF16)) + tn(a0_ref[n:], m1_ref[...].astype(BF16))

        def write(ref, x, to):
            for zh in range(2):
                row = zh * 128 + x * 32
                ref[2 * to + zh, :, 0:w1] = first[row : row + 32]
                ref[2 * to + zh, :, w1:] = second[row : row + 32]

        offset = lax.rem(step - at_ref[1] + 4, 4)
        for k, ref in ((0, outs[0]), (1, outs[1]), (3, outs[4])):

            @pl.when(offset == k)
            def _(ref=ref):
                for x in range(4):
                    write(ref, x, x)

        @pl.when(offset == 2)
        def _():
            for x in range(4):
                write(outs[2 if x < 2 else 3], x, x % 2)

    @pl.when(step == 4)
    def _():
        small = small_ref[...] + core_ref[...] + far_ref[...]
        for out in (outs[0], outs[1], outs[3], outs[4]):
            last = out.shape[0] - 1
            out[last] = jnp.zeros(out.shape[1:], F32)
            out[last, 0:16, :] = small[0:16, 0:768]
            for j in range(3):
                n = min(6, 16 - 6 * j)
                out[last, 16 : 16 + n, 256 * j : 256 * (j + 1)] = small[6 * j : 6 * j + n, 768:1024]
            for j in range(6):
                n = min(3, 16 - 3 * j)
                out[last, 22 : 22 + n, 128 * j : 128 * (j + 1)] = gup_ref[3 * j : 3 * j + n, :]
            out[last, 25:26, :] = small[16:17, 0:768]
            out[last, 26:27, :] = small[17:18, 0:768]
            out[last, 27:28, 0:256] = small[16:17, 768:1024]
            out[last, 27:28, 256:512] = small[17:18, 768:1024]
            out[last, 27:28, 512:640] = bias_ref[0:1, :]


def run_mixer_grads(at, n1, dqkv, ga, mixed, small, gup, bias):
    t, c = n1.shape[0], dqkv.shape[1] + mixed[0].shape[1]
    cols = pl.BlockSpec((t, CH), lambda s, at: (0, jnp.minimum(s, 3)))
    whole = lambda a: pl.BlockSpec(a.shape, lambda s, at: (0, 0))
    rest = [*small, gup, bias]
    counts = [9, 9, 4, 5, 9]
    return pl.pallas_call(
        mixer_grads_kernel,
        grid_spec=pltpu.PrefetchScalarGridSpec(
            num_scalar_prefetch=1, grid=(5,),
            in_specs=[cols, whole(dqkv), cols, whole(mixed[0]), whole(mixed[1])] + [whole(a) for a in rest],
            out_specs=[pl.BlockSpec((n, 32, c), lambda s, at: (0, 0, 0)) for n in counts]),
        out_shape=[jax.ShapeDtypeStruct((n, 32, c), F32) for n in counts],
        compiler_params=pltpu.CompilerParams(vmem_limit_bytes=VMEM_BYTES),
        cost_estimate=weight(1),
        name="mixer_weight_grads",
    )(at, n1, dqkv, ga, mixed[0], mixed[1], *rest)


def unpack_kernel(rows_ref, g1_ref, down_ref, up_ref, bias_ref, g2_ref, q_ref, k_ref, v_ref, o_ref):
    sums = rows_ref[1]
    wide = jnp.concatenate([sums[16:22, 0:256], sums[16:22, 256:512], sums[16:20, 512:768]], axis=0)
    down_ref[...] = jnp.concatenate([sums[0:16], wide], axis=1)
    for j in range(6):
        n = min(3, 16 - 3 * j)
        up_ref[3 * j : 3 * j + n, :] = sums[22 : 22 + n, 128 * j : 128 * (j + 1)]
    g1_ref[:, 0:768] = sums[25:26]
    g1_ref[:, 768:1024] = sums[27:28, 0:256]
    g2_ref[:, 0:768] = sums[26:27]
    g2_ref[:, 768:1024] = sums[27:28, 256:512]
    bias_ref[...] = sums[27:28, 512:640]
    q_ref[...] = rows_ref[0, :, 0:128]
    k_ref[...] = rows_ref[0, :, 128:256]
    v_ref[...] = rows_ref[0, :, 256:512]
    o_ref[...] = rows_ref[0, :, 512:768]


def unpack(rows):
    shapes = [(1, 1024), (16, 1024), (16, 128), (1, 128), (1, 1024), (32, 128), (32, 128), (32, 256), (32, 256)]
    return pl.pallas_call(
        unpack_kernel, out_shape=[jax.ShapeDtypeStruct(s, F32) for s in shapes], name="unpack", **SMALL,
    )(rows)


def after(value, *others):
    return lax.optimization_barrier((value, others))[0]


def send(v, shifts, d):
    return lax.ppermute(v, "dp", shifts[d])


def ring_one(v, shifts):
    return lax.ppermute(v[2], "dp", shifts[1]), lax.ppermute(v[3], "dp", shifts[3])


def ring_add(v, got):
    up, down = got
    return v[1].at[: up.shape[0]].add(up), v[4].at[v[4].shape[0] - down.shape[0] :].add(down)


def ring_two(v, shifts):
    return lax.ppermute(v[0], "dp", shifts[1]), lax.ppermute(v[1], "dp", shifts[3])


def pick(v, i, dim):
    return lax.dynamic_index_in_dim(v, i, dim, False)


def swap_zh(v, zh, dim):
    return pick(v, zh, dim) + lax.ppermute(pick(v, 1 - zh, dim), "dp", ZH)


def local(tokens, lengths, g1, wq, wk, wv, wgd, wgu, bias, wout, g2, wg, wu, wd, cot):
    mp, dp = lax.axis_index("mp"), lax.axis_index("dp")
    core, z = mp % 2, mp // 2
    ix, zh, iy = dp % 4, (dp // 4) % 2, dp // 8
    at = jnp.stack([ix, iy, core, z]).astype(jnp.int32)
    g1r, g2r, biasr = g1.reshape(1, -1), g2.reshape(1, -1), bias.reshape(1, -1)
    wgd_t, wg_t, wu_t = wgd.T, wg.T, wu.T

    with jax.named_scope("out_weights"):
        wide = wout.astype(F32)
        wout_z = z_swap(wide)
        wout_c = core_swap(wide)
    n1, q, k, v, low, logits, cum, mixed_lo, mixed_hi, st = run_mixer_forward(
        lengths, after(tokens, wide), g1r, wq, wk, wv, wgd_t, wgu, biasr)
    mixed = (mixed_lo, mixed_hi)
    with jax.named_scope("mixed_heads"):
        mixed_c = [core_swap(m) for m in mixed]
        wout_cz = core_swap(after(wout_z, mixed_hi))
        mixed_z = [None, z_swap(after(mixed_hi, wout_z))]
        mixed_z[0] = z_swap(after(mixed_lo, wout_z))
    wo, gh = run_before_feed((wout, wout_z, wout_c, wout_cz), cot, wd)

    middle, n2, hid, gg, feed_out, feed_keep, part_out, part_keep = [[None, None] for _ in range(8)]
    part_in, dn2_out, dn2_z, feed_in = [[None, None] for _ in range(4)]
    gm, gains = [None, None], [None, None]

    def feed_half(j, ready):
        with jax.named_scope("mixed_heads"):
            here = after(mixed_z[j], ready)
            pieces = (mixed[j], here, mixed_c[j], core_swap(here))
        (middle[j], n2[j], hid[j], gg[j], feed_out[j], feed_keep[j], part_out[j], part_keep[j]) = run_feed(
            at, j, tokens, gh, pieces, wo, g2r, wg_t, wu_t, wd)

    def norm_sum(j, ready):
        with jax.named_scope("second_norm_sum"):
            part_in[j] = core_swap(after(part_out[j], ready))
            dn2_out[j] = add_quarter(at, (part_keep[j], part_in[j]))
            dn2_z[j] = z_swap(dn2_out[j])

    def norm_join(j, ready):
        with jax.named_scope("second_norm_join"):
            gm0, gains[j] = run_second_norm(at, j, part_keep[j], part_in[j], after(dn2_z[j], ready), middle[j], g2r, cot)
            gm[j] = [gm0, z_swap(gm0), core_swap(gm0), None]

    feed_half(1, gh)
    norm_sum(1, mixed_z[0])
    feed_half(0, dn2_out[1])
    norm_sum(0, dn2_z[1])
    norm_join(1, dn2_out[0])

    a = run_feed_grads(at, *after((n2, gg), gm[1][0]), cot, hid)
    norm_join(0, (a[0], gm[1][1]))
    with jax.named_scope("feed_grads_one"):
        a = after(a, gm[1][1])
        a_on = ring_one(a, XS)

    with jax.named_scope("feed_sum"):
        feed_in = [core_swap(feed_out[j]) for j in range(2)]
        feed_pairs = [(feed_keep[j], feed_in[j]) for j in range(2)]
        feed_z_out = add_quarter(at, *after(feed_pairs, gm[0][0]))
        feed_z = z_swap(after(feed_z_out, gm[0][1]))

    with jax.named_scope("second_norm_join"):
        for j in range(2):
            gm[j][3] = core_swap(after(gm[j][1], (gm[0][1], feed_z_out, a_on)))

    dqkv, part1_out, part1_keep, ga, small, gup, gbias = run_mixer_backward(
        at, lengths, gm[0] + gm[1], gains, tokens, n1, q, k, v, low, logits, cum, st, wout, wq, wk, wv, wgd_t, wgu)

    with jax.named_scope("first_norm_sum"):
        part1_in = core_swap(after(part1_out, feed_z))
    with jax.named_scope("small_sums"):
        small_core = core_swap(small)
        small_far = z_swap(small + small_core)
    with jax.named_scope("feed_grads_one"):
        a_on = ring_add(a, after(a_on, part1_out))
    with jax.named_scope("first_norm_sum"):
        dn1_out = add_quarter(at, after((part1_keep, part1_in), a_on))
        dn1_z = z_swap(dn1_out)
    with jax.named_scope("feed_grads_one"):
        a_in = ring_two(a_on, XS)

    c = run_mixer_grads(at, n1, dqkv, ga, after(mixed, dn1_out), (small, small_core, small_far), gup, gbias)
    with jax.named_scope("mixer_grads_one"):
        c_on = ring_one(c, YS)

    with jax.named_scope("feed_join"):
        feed_own = run_quarter_sum(at, feed_pairs, after(feed_z, c))
        feed1 = z_swap(after(feed_own, dn1_z))
        feed2 = core_swap(feed_own)

    with jax.named_scope("mixer_grads_one"):
        c_on = ring_add(c, after(c_on, feed_own))
        c_in = ring_two(c_on, YS)

    with jax.named_scope("first_norm_join"):
        dx0 = run_first_norm(at, part1_keep, part1_in, after(dn1_z, c_on), tokens, g1r)
        dx1 = z_swap(after(dx0, feed1))
        dx2 = core_swap(dx0)

    def across(v, at_here, shifts, take):
        return take(v, at_here) + send(take(v, (at_here + 1) % 4), shifts, 1) + send(take(v, (at_here + 3) % 4), shifts, 3) \
            + send(take(v, (at_here + 2) % 4), shifts, 2)

    with jax.named_scope("mixer_grads_two"):
        c, c_in = after((c, c_in), dx0)
        c = c_sum = c[0] + c_in[0] + c_in[1]

        def with_small(v, i):
            return jnp.concatenate([lax.dynamic_slice_in_dim(v, 2 * i, 2, 0), v[8:9]], axis=0)

        c = across(c, ix, XS, with_small)

    with jax.named_scope("feed_grads_two"):
        a, a_in = after((a, a_in), c_sum)
        a = a_sum = a[0] + a_in[0] + a_in[1]
        a = across(a, iy, YS, lambda v, i: pick(v, i, 0))

    with jax.named_scope("first_norm_join"):
        grad_tokens = run_join(at, 0, after((dx0, dx2), a_sum), (gm[0][0], gm[0][2], gm[1][0], gm[1][2]), F32)

    with jax.named_scope("mixer_grads_two"):
        c = after(c, grad_tokens)
        turned = lambda i: jnp.stack([pick(c, i, 0), c[2]])
        rows = turned(zh) + lax.ppermute(turned(1 - zh), "dp", ZH)

    with jax.named_scope("feed_join"):
        result = run_join(at, 0, (feed_own, feed2), after(middle, c), BF16)

    with jax.named_scope("feed_grads_two"):
        mlp_rows = swap_zh(after(a, result), zh, 0)

    with jax.named_scope("feed_join"):
        feed3 = core_swap(after(feed1, a))
        result = run_join(at, 1, (feed1, feed3), middle, BF16, result)

    with jax.named_scope("small_sums"):
        gain_one, gate_down, gate_up, gate_bias, gain_two, d_query, d_key, d_value, d_out = unpack(rows)

    with jax.named_scope("first_norm_join"):
        dx3 = core_swap(dx1)
        grad_tokens = run_join(at, 1, (dx1, dx3), (gm[0][1], gm[0][3], gm[1][1], gm[1][3]), F32, grad_tokens)

    return (
        result,
        grad_tokens,
        gain_one.reshape(1024),
        d_query,
        d_key,
        d_value,
        gate_down.T,
        gate_up,
        gate_bias.reshape(128),
        d_out.T,
        gain_two.reshape(1024),
        mlp_rows[:, 0:704],
        mlp_rows[:, 704:1408],
        mlp_rows[:, 1408:2112].T,
    )


def solution(mesh):
    placed = (
        P("dp", None), P("dp", None), P(), P(None, "mp"), P(None, "mp"), P(None, "mp"), P(), P(None, "mp"),
        P("mp"), P("mp", None), P(), P(None, "mp"), P(None, "mp"), P("mp", None), P("dp", None),
    )
    outs = (
        P("dp", None), P("dp", None), P(), P("dp", "mp"), P("dp", "mp"), P("dp", "mp"), P(), P(None, "mp"),
        P("mp"), P("mp", "dp"), P(), P("dp", "mp"), P("dp", "mp"), P("mp", "dp"),
    )
    return jax.shard_map(local, mesh=mesh, in_specs=placed, out_specs=outs, check_vma=False)
```

```python
import functools

import jax
import jax.numpy as jnp
from jax import lax
from jax.experimental import pallas as pl
from jax.experimental.pallas import tpu as pltpu
from jax.sharding import PartitionSpec as P

BLK = 64
CH = 256
EPS = 1e-6
SCALE = 128 ** -0.5
F32 = jnp.float32
BF16 = jnp.bfloat16
VMEM_BYTES = 63_400_000
BACK_US = 16
FWD_ROWS = 256
BWD_ROWS = 256


def weight(us):
    return pl.CostEstimate(flops=int(us * 1.0e9), bytes_accessed=1024, transcendentals=0)


def nn(a, b, **kw):
    return lax.dot_general(a, b, (((1,), (0,)), ((), ())), preferred_element_type=F32, **kw)


def nt(a, b, **kw):
    return lax.dot_general(a, b, (((1,), (1,)), ((), ())), preferred_element_type=F32, **kw)


def tn(a, b, **kw):
    return lax.dot_general(a, b, (((0,), (0,)), ((), ())), preferred_element_type=F32, **kw)


HIGH = dict(precision=lax.Precision.HIGHEST)


CORE = [(0, 1), (1, 0), (2, 3), (3, 2)]
ZLO = [(0, 2), (2, 0), (1, 3), (3, 1)]


def dp_perm(dy, dz, dx):
    out = []
    for y in range(4):
        for z in range(2):
            for x in range(4):
                out.append(((y * 2 + z) * 4 + x, (((y + dy) % 4) * 2 + (z + dz) % 2) * 4 + (x + dx) % 4))
    return out


XS = {1: dp_perm(0, 0, 1), 3: dp_perm(0, 0, -1), 2: dp_perm(0, 0, 2)}
YS = {1: dp_perm(1, 0, 0), 3: dp_perm(-1, 0, 0), 2: dp_perm(2, 0, 0)}
ZH = dp_perm(0, 1, 0)
Y_PAIR = [((y * 2 + z) * 4 + x, ((y ^ 1) * 2 + z) * 4 + x) for y in range(4) for z in range(2) for x in range(4)]
X_PAIR = [((y * 2 + z) * 4 + x, (y * 2 + z) * 4 + (x ^ 1)) for y in range(4) for z in range(2) for x in range(4)]


def core_swap(v):
    return lax.ppermute(v, "mp", CORE)


def z_swap(v):
    return lax.ppermute(v, "mp", ZLO)


def rows_of(v, start, size):
    return lax.dynamic_slice_in_dim(v, start, size, 0)


def item_starts(len_ref):
    starts, total = [], jnp.int32(0)
    for j in range(8):
        starts.append(total)
        total = total + len_ref[0, j]
    return starts


def start_at(starts, place):
    best = jnp.int32(0)
    for s in starts[1:]:
        best = jnp.where(s <= place, jnp.maximum(best, s), best)
    return best


def chunk_masks(starts, base):
    row = lax.broadcasted_iota(jnp.int32, (CH, CH), 0)
    col = lax.broadcasted_iota(jnp.int32, (CH, CH), 1)
    blk = jnp.bitwise_and(row, -BLK)
    row1 = lax.broadcasted_iota(jnp.int32, (CH, 128), 0)
    place = row1 + base
    low = jnp.zeros_like(place)
    for s in starts[1:]:
        low = jnp.where(place >= s, jnp.maximum(low, s), low)
    low = low - base
    blk1 = jnp.bitwise_and(row1, -BLK)
    carried = low < blk1
    low_wide = jnp.concatenate([low, low], axis=1)
    causal = (col <= row) & (col >= blk)
    visible = causal & (col >= low_wide)
    return visible, carried


def causal_ones():
    row = lax.broadcasted_iota(jnp.int32, (CH, CH), 0)
    col = lax.broadcasted_iota(jnp.int32, (CH, CH), 1)
    return jnp.where((col <= row) & (col >= jnp.bitwise_and(row, -BLK)), 1.0, 0.0).astype(BF16)


def two_parts(v):
    high = v.astype(BF16)
    return high, (v - high.astype(F32)).astype(BF16)


def block_scalars(starts, base, b):
    first = base + b * BLK
    origin = start_at(starts, first + BLK - 1)
    keep = jnp.where(origin < first, 1.0, 0.0).astype(F32)
    place = lax.broadcasted_iota(jnp.int32, (BLK, 128), 0) + first
    return keep, place >= origin


def scaled_parts(q, k, cum):
    last = jnp.broadcast_to(cum.reshape(CH // BLK, BLK, 128)[:, BLK - 1 :, :], (CH // BLK, BLK, 128))
    last = last.reshape(CH, 128)
    e, en, ef = jnp.exp(cum), jnp.exp(-cum), jnp.exp(last - cum)
    qf = q.astype(F32) * SCALE * e
    ks = k.astype(F32) * en
    kf = k.astype(F32) * ef
    return last, e, en, ef, qf, ks, kf


def mixer_forward(
    len_ref, tok_ref, g1_ref, wq_ref, wk_ref, wv_ref, wgd_ref, wgu_ref, bias_ref,
    n_ref, q_ref, k_ref, v_ref, low_ref, logit_ref, cum_ref, mixed_lo_ref, mixed_hi_ref, st_ref, state,
):
    step = pl.program_id(0)
    rows = tok_ref.shape[0]
    starts = item_starts(len_ref)

    @pl.when(step == 0)
    def _():
        state[...] = jnp.zeros_like(state)

    ones = causal_ones()
    s = state[...]
    for c in range(rows // CH):
        base = step * rows + c * CH
        at = slice(c * CH, (c + 1) * CH)
        x = tok_ref[at, :].astype(F32)
        r = lax.rsqrt(jnp.mean(x * x, axis=-1, keepdims=True) + EPS)
        n = (x * r * g1_ref[...]).astype(BF16)
        n_ref[at, :] = n
        low = nt(n, wgd_ref[...]).astype(BF16)
        low_ref[at, :] = low
        logits = nn(low, wgu_ref[...]) + bias_ref[...]
        logit_ref[at, :] = logits
        decays = (jnp.minimum(logits, 0.0) - jnp.log1p(jnp.exp(-jnp.abs(logits)))) * (1.0 / 16.0)
        high, rest = two_parts(decays)
        cum = nn(ones, high) + nn(ones, rest)
        cum_ref[at, :] = cum
        q = nn(n, wq_ref[...]).astype(BF16)
        k = nn(n, wk_ref[...]).astype(BF16)
        v = nn(n, wv_ref[...]).astype(BF16)
        q_ref[at, :] = q
        k_ref[at, :] = k
        v_ref[at, :] = v
        visible, carried = chunk_masks(starts, base)
        last, e, en, ef, qf, ks, kf = scaled_parts(q, k, cum)
        scores = jnp.where(visible, nt(qf.astype(BF16), ks.astype(BF16)), 0.0).astype(BF16)
        out = nn(scores, v)
        q_carried = jnp.where(carried, qf, 0.0).astype(BF16)
        mixed_parts = []
        for b in range(CH // BLK):
            sl = slice(b * BLK, (b + 1) * BLK)
            keep, tail = block_scalars(starts, base, b)
            st_ref[c * (CH // BLK) + b] = s
            inter = nt(q_carried[sl], s.astype(BF16))
            mixed_parts.append((out[sl] + inter).astype(BF16).astype(F32))
            k_tail = jnp.where(tail, kf[sl], 0.0).astype(BF16)
            s = keep * jnp.exp(last[b * BLK : b * BLK + 1]) * s + tn(v[sl], k_tail)
        mixed = jnp.concatenate(mixed_parts, axis=0)

        @pl.when(step < 2)
        def _(mixed=mixed):
            mixed_lo_ref[...] = mixed

        @pl.when(step >= 2)
        def _(mixed=mixed):
            mixed_hi_ref[...] = mixed

    state[...] = s


def run_mixer_forward(lengths, tokens, g1, wq, wk, wv, wgd, wgu, bias):
    t = tokens.shape[0]
    whole = lambda a: pl.BlockSpec(a.shape, lambda i: (0,) * a.ndim)
    rows = lambda c: pl.BlockSpec((CH, c), lambda i: (i, 0))
    nb = CH // BLK
    outs = [
        ((t, 1024), BF16), ((t, 128), BF16), ((t, 128), BF16), ((t, 256), BF16), ((t, 16), BF16), ((t, 128), F32), ((t, 128), F32),
    ]
    sds = jax.ShapeDtypeStruct
    return pl.pallas_call(
        mixer_forward,
        grid=(t // CH,),
        in_specs=[pl.BlockSpec(memory_space=pltpu.SMEM), rows(1024), whole(g1), whole(wq), whole(wk), whole(wv),
                  whole(wgd), whole(wgu), whole(bias)],
        out_specs=[rows(s[1]) for s, _ in outs]
        + [pl.BlockSpec((CH, 256), lambda i: (jnp.minimum(i, 1), 0)), pl.BlockSpec((CH, 256), lambda i: (jnp.maximum(i - 2, 0), 0)),
           pl.BlockSpec((nb, 256, 128), lambda i: (i, 0, 0))],
        out_shape=[sds(s, d) for s, d in outs] + [sds((t // 2, 256), F32)] * 2 + [sds((t // BLK, 256, 128), F32)],
        scratch_shapes=[pltpu.VMEM((256, 128), F32)],
        compiler_params=pltpu.CompilerParams(vmem_limit_bytes=VMEM_BYTES),
        cost_estimate=weight(10),
        name="mixer_forward",
    )(lengths, tokens, g1, wq, wk, wv, wgd, wgu, bias)


def before_feed_kernel(w0_ref, w1_ref, w2_ref, w3_ref, cot_ref, wd_ref, wo_ref, gh_ref):
    for j, w_ref in enumerate((w0_ref, w1_ref, w2_ref, w3_ref)):

        @pl.when(pl.program_id(0) == j)
        def _(w_ref=w_ref):
            wo_ref[...] = w_ref[...].astype(BF16)

    gh_ref[...] = nt(cot_ref[...], wd_ref[...])


def run_before_feed(wo, cot, wd):
    t = cot.shape[0]
    whole = lambda a: pl.BlockSpec(a.shape, lambda s: (0,) * a.ndim)
    rows = lambda c: pl.BlockSpec((CH, c), lambda s: (s, 0))
    return pl.pallas_call(
        before_feed_kernel,
        grid=(t // CH,),
        in_specs=[whole(w) for w in wo] + [rows(1024), whole(wd)],
        out_specs=[rows(1024), rows(704)],
        out_shape=[jax.ShapeDtypeStruct((t, 1024), BF16), jax.ShapeDtypeStruct((t, 704), F32)],
        compiler_params=pltpu.CompilerParams(vmem_limit_bytes=VMEM_BYTES),
        cost_estimate=weight(7),
        name="before_feed",
    )(*wo, cot, wd)


def feed_kernel(
    at_ref, tok_ref, gh_ref, m0_ref, m1_ref, m2_ref, m3_ref, wo_ref, g2_ref, wg_ref, wu_ref, wd_ref,
    mid_ref, n_ref, hid_ref, gg_ref, feed_out_ref, feed_keep_ref, part_out_ref, part_keep_ref,
):
    step = pl.program_id(0)

    mixed = jnp.concatenate([m0_ref[...], m1_ref[...], m2_ref[...], m3_ref[...]], axis=1).astype(BF16)
    mid = tok_ref[...].astype(F32) + nn(mixed, wo_ref[...])
    mid_ref[...] = mid
    r = lax.rsqrt(jnp.mean(mid * mid, axis=-1, keepdims=True) + EPS)
    n = (mid * r * g2_ref[...]).astype(BF16)
    n_ref[...] = n
    pre = nt(n, wg_ref[...])
    up = nt(n, wu_ref[...])
    sg = jax.nn.sigmoid(pre)
    act = pre * sg
    hid = (act * up).astype(BF16)
    hid_ref[...] = hid
    gh = gh_ref[...]
    gg = (gh * up * sg * (1.0 + pre * (1.0 - sg))).astype(BF16)
    gu = (gh * act).astype(BF16)
    gg_ref[:, 0:704] = gg
    gg_ref[:, 704:1408] = gu
    feed = nn(hid, wd_ref[...])
    part = nn(gg, wg_ref[...]) + nn(gu, wu_ref[...])

    @pl.when(step == 0)
    def _():
        feed_out_ref[...] = feed
        part_out_ref[...] = part

    @pl.when(step == 1)
    def _():
        feed_keep_ref[...] = feed
        part_keep_ref[...] = part


def run_feed(at, chunk, tokens, gh, mixed, wo, g2, wg, wu, wd):
    t = tokens.shape[0] // 2
    whole = lambda a: pl.BlockSpec(a.shape, lambda s, at: (0,) * a.ndim)
    half = lambda s, at: jnp.bitwise_xor(1 - at[2], s)
    rows = lambda c: pl.BlockSpec((CH, c), lambda s, at: (half(s, at), 0))
    from_all = lambda c: pl.BlockSpec((CH, c), lambda s, at: (2 * chunk + half(s, at), 0))
    once = pl.BlockSpec((CH, 1024), lambda s, at: (0, 0))
    sds = jax.ShapeDtypeStruct
    return pl.pallas_call(
        feed_kernel,
        grid_spec=pltpu.PrefetchScalarGridSpec(
            num_scalar_prefetch=1,
            grid=(t // CH,),
            in_specs=[from_all(1024), from_all(704)] + [rows(256)] * 4 + [whole(wo), whole(g2), whole(wg), whole(wu), whole(wd)],
            out_specs=[rows(1024), rows(1024), rows(704), rows(1408), once, once, once, once],
        ),
        out_shape=[sds((t, 1024), F32), sds((t, 1024), BF16), sds((t, 704), BF16), sds((t, 1408), BF16)] + [sds((CH, 1024), F32)] * 4,
        compiler_params=pltpu.CompilerParams(vmem_limit_bytes=VMEM_BYTES),
        cost_estimate=weight(14),
        name="feed_both_ways",
    )(at, tokens, gh, *mixed, wo, g2, wg, wu, wd)


def mixer_backward(
    at_ref, len_ref, *refs,
):
    gm_refs, gain_ref, refs = refs[:4], refs[4], refs[5:]
    (tok_ref, n_ref, q_ref, k_ref, v_ref, low_ref, logit_ref, cum_ref,
     st_ref, wo_ref, wq_ref, wk_ref, wv_ref, wgd_ref, wgu_ref,
     dqkv_ref, far0_ref, far1_ref, near0_ref, near1_ref, part_keep_ref, ga_ref, small_ref, gup_ref, bias_ref, dstate, whole) = refs
    step = pl.program_id(0)
    steps = pl.num_programs(0)
    rows = tok_ref.shape[0]
    starts = item_starts(len_ref)

    core, z = at_ref[2], at_ref[3]
    here = steps - 1 - step
    mine = jnp.equal(lax.rem(here, 2), core)

    @pl.when(step == 0)
    def _():
        dstate[...] = jnp.zeros_like(dstate)
        small_ref[...] = jnp.zeros_like(small_ref)
        small_ref[17:18, :] = gain_ref[0:1, :]
        gup_ref[...] = jnp.zeros_like(gup_ref)
        bias_ref[...] = jnp.zeros_like(bias_ref)

    first = pl.multiple_of(z * 128, 128)
    second = pl.multiple_of((1 - z) * 128, 128)
    for other in range(2):

        @pl.when(jnp.logical_not(mine) if other else mine)
        def _(other=other):
            ga_ref[pl.ds(first, 128), :] = gm_refs[2 * other][...].astype(BF16)
            ga_ref[pl.ds(second, 128), :] = gm_refs[2 * other + 1][...].astype(BF16)

    ones = causal_ones()
    ds = dstate[...]
    for c in reversed(range(rows // CH)):
        base = here * rows + c * CH
        at = slice(c * CH, (c + 1) * CH)
        g = nt(ga_ref[at, :], wo_ref[...]).astype(BF16)
        q, k, v, cum = q_ref[at, :], k_ref[at, :], v_ref[at, :], cum_ref[at, :]
        visible, carried = chunk_masks(starts, base)
        last, e, en, ef, qf, ksf, kff = scaled_parts(q, k, cum)
        qs, ks = qf.astype(BF16), ksf.astype(BF16)
        scores = jnp.where(visible, nt(qs, ks), 0.0).astype(BF16)
        dscores = jnp.where(visible, nt(g, v), 0.0).astype(BF16)
        dv = tn(scores, g)
        dqs = nn(dscores, ks)
        dks = tn(dscores, qs)
        q_carried = jnp.where(carried, qf, 0.0).astype(BF16)
        dvs, dkfs, dqss, dls = [], [], [], []
        for b in reversed(range(CH // BLK)):
            sl = slice(b * BLK, (b + 1) * BLK)
            keep, tail = block_scalars(starts, base, b)
            dsb = ds.astype(BF16)
            s = st_ref[c * (CH // BLK) + b]
            k_tail = jnp.where(tail, kff[sl], 0.0).astype(BF16)
            dvs.append(dv[sl] + nt(k_tail, dsb))
            dkf = jnp.where(tail, nn(v[sl], dsb), 0.0)
            dkfs.append(dkf)
            dqss.append(dqs[sl] + jnp.where(carried[sl], nn(g[sl], s.astype(BF16)), 0.0))
            grow = keep * jnp.exp(last[b * BLK : b * BLK + 1])
            dlast = grow * jnp.sum(s * ds, axis=0, keepdims=True) + jnp.sum(dkf * kff[sl], axis=0, keepdims=True)
            dls.append(jnp.broadcast_to(dlast, (BLK, 128)))
            ds = grow * ds + tn(g[sl], q_carried[sl])
        join = lambda parts: jnp.concatenate(parts[::-1], axis=0)
        dqs, dkf, dl = join(dqss), join(dkfs), join(dls)
        dq = (dqs * (SCALE * e)).astype(BF16)
        dk = (dks * en + dkf * ef).astype(BF16)
        dv = join(dvs).astype(BF16)
        dqkv_ref[at, 0:128] = dq
        dqkv_ref[at, 128:256] = dk
        dqkv_ref[at, 256:512] = dv
        high, rest = two_parts(dqs * qf - dks * ksf - dkf * kff)
        ddec = tn(ones, high) + tn(ones, rest) + dl
        glog = ddec * jax.nn.sigmoid(-logit_ref[at, :]) * (1.0 / 16.0)
        bias_ref[0:1, :] += jnp.sum(glog, axis=0, keepdims=True)
        high, rest = two_parts(glog)
        gup_ref[...] += tn(low_ref[at, :], high) + tn(low_ref[at, :], rest)
        glr = (nt(high, wgu_ref[...]) + nt(rest, wgu_ref[...])).astype(BF16)
        part = nt(dq, wq_ref[...]) + nt(dk, wk_ref[...]) + nt(dv, wv_ref[...]) + nn(glr, wgd_ref[...])
        @pl.when(mine)
        def _(part=part):
            part_keep_ref[...] = part

        for chunk, (far_ref, near_ref) in enumerate(((far0_ref, near0_ref), (far1_ref, near1_ref))):

            @pl.when(jnp.logical_and(jnp.logical_not(mine), jnp.equal(lax.div(here, 2), chunk)))
            def _(part=part, far_ref=far_ref, near_ref=near_ref):
                whole[...] = part
                far_ref[...] = whole[pl.ds(second, 128), :]
                near_ref[...] = whole[pl.ds(first, 128), :]

        small_ref[0:16, :] += tn(glr, n_ref[at, :])
        x = tok_ref[at, :].astype(F32)
        r = lax.rsqrt(jnp.mean(x * x, axis=-1, keepdims=True) + EPS)
        small_ref[16:17, :] += jnp.sum(part * x * r, axis=0, keepdims=True)
    dstate[...] = ds


def run_mixer_backward(at, lengths, gm, gain, tokens, n, q, k, v, low, logits, cum, st, wo, wq, wk, wv, wgd, wgu):
    t = tokens.shape[0]
    steps = t // CH
    whole = lambda a: pl.BlockSpec(a.shape, lambda i, at: (0,) * a.ndim)
    rows = lambda c: pl.BlockSpec((CH, c), lambda i, at: (steps - 1 - i, 0))
    split = pl.BlockSpec((CH, 1024), lambda i, at: (lax.div(steps - 1 - i, 2), 0))
    nb = CH // BLK
    fixed = lambda s: pl.BlockSpec(s, lambda i, at: (0, 0))
    sds = jax.ShapeDtypeStruct
    return pl.pallas_call(
        mixer_backward,
        grid_spec=pltpu.PrefetchScalarGridSpec(
            num_scalar_prefetch=1,
            grid=(steps,),
            in_specs=[pl.BlockSpec(memory_space=pltpu.SMEM)] + [pl.BlockSpec((128, 1024), lambda i, at: (lax.div(steps - 1 - i, 2), 0))] * 4 + [whole(gain)]
            + [rows(1024), rows(1024), rows(128), rows(128), rows(256), rows(16), rows(128), rows(128),
               pl.BlockSpec((nb, 256, 128), lambda i, at: (steps - 1 - i, 0, 0)),
               whole(wo), whole(wq), whole(wk), whole(wv), whole(wgd), whole(wgu)],
            out_specs=[rows(512)] + [fixed((128, 1024))] * 4 + [split, rows(1024), fixed((24, 1024)), fixed((16, 128)), fixed((8, 128))],
            scratch_shapes=[pltpu.VMEM((256, 128), F32), pltpu.VMEM((CH, 1024), F32)],
        ),
        out_shape=[sds((t, 512), BF16)] + [sds((128, 1024), F32)] * 4 + [sds((t // 2, 1024), F32), sds((t, 1024), BF16),
                   sds((24, 1024), F32), sds((16, 128), F32), sds((8, 128), F32)],
        compiler_params=pltpu.CompilerParams(vmem_limit_bytes=VMEM_BYTES),
        cost_estimate=weight(BACK_US),
        name="mixer_backward",
    )(at, lengths, *gm, gain, tokens, n, q, k, v, low, logits, cum, st, wo, wq, wk, wv, wgd, wgu)


SMALL = dict(
    compiler_params=pltpu.CompilerParams(vmem_limit_bytes=VMEM_BYTES),
    cost_estimate=weight(3),
)


def add_kernel(at_ref, *refs):
    out_ref = refs[-1]
    n = out_ref.shape[0] // (len(refs) // 2)
    for j in range(len(refs) // 2):
        out_ref[j * n : (j + 1) * n] = refs[2 * j][...] + refs[2 * j + 1][...]


def add_quarter(at, *pairs):
    ops, specs = [], []
    for pair in pairs:
        for j in range(pair[0].shape[0] // 256):
            ops += pair
            specs += [pl.BlockSpec((128, 1024), lambda s, at, j=j: (2 * j + 1 - at[3], 0))] * 2
    n = 64 * len(ops)
    return pl.pallas_call(
        add_kernel,
        grid_spec=pltpu.PrefetchScalarGridSpec(
            num_scalar_prefetch=1, grid=(1,), in_specs=specs, out_specs=pl.BlockSpec((n, 1024), lambda s, at: (0, 0))),
        out_shape=jax.ShapeDtypeStruct((n, 1024), F32),
        name="add_quarter",
        **SMALL,
    )(at, *ops)


def quarter_sum_kernel(at_ref, a0_ref, b0_ref, y0_ref, a1_ref, b1_ref, y1_ref, c_ref, o_ref):
    o_ref[0:128] = a0_ref[...] + b0_ref[...] + c_ref[0:128] + y0_ref[...]
    o_ref[128:256] = a1_ref[...] + b1_ref[...] + c_ref[128:256] + y1_ref[...]


def run_quarter_sum(at, keep, got, far, middle):
    of_half = pl.BlockSpec((128, 1024), lambda s, at: (at[3], 0))
    of_chunk = pl.BlockSpec((128, 1024), lambda s, at: (2 * at[2] + at[3], 0))
    own = pl.BlockSpec((256, 1024), lambda s, at: (0, 0))
    return pl.pallas_call(
        quarter_sum_kernel,
        grid_spec=pltpu.PrefetchScalarGridSpec(
            num_scalar_prefetch=1, grid=(1,), in_specs=[of_half, of_half, of_chunk] * 2 + [own], out_specs=own),
        out_shape=jax.ShapeDtypeStruct((256, 1024), F32),
        name="quarter_sum",
        **SMALL,
    )(at, keep[0], got[0], middle[0], keep[1], got[1], middle[1], far)


def norm_gradient(dn, y, gain):
    r = lax.rsqrt(jnp.mean(y * y, axis=-1, keepdims=True) + EPS)
    gd = dn * gain
    dy = r * gd - (r * r * r) * y * jnp.mean(gd * y, axis=-1, keepdims=True)
    return dy, jnp.sum(dn * y * r, axis=0, keepdims=True)


def second_norm_kernel(at_ref, a0_ref, b0_ref, c0_ref, y0_ref, a1_ref, b1_ref, c1_ref, y1_ref, gain_ref, base0_ref, base1_ref, o_ref, s_ref):
    halves = ((a0_ref, b0_ref, c0_ref, y0_ref, base0_ref), (a1_ref, b1_ref, c1_ref, y1_ref, base1_ref))
    total = jnp.zeros((1, 1024), F32)
    for j, (a_ref, b_ref, c_ref, y_ref, base_ref) in enumerate(halves):
        dy, dgain = norm_gradient(a_ref[...] + b_ref[...] + c_ref[...], y_ref[...], gain_ref[...])
        o_ref[128 * j : 128 * (j + 1)] = base_ref[...].astype(F32) + dy
        total = total + dgain
    s_ref[0:1, :] = total


def run_second_norm(at, keep, got, far, middle, gain, cot):
    of_half = pl.BlockSpec((128, 1024), lambda s, at: (at[3], 0))
    of_chunk = pl.BlockSpec((128, 1024), lambda s, at: (2 * at[2] + at[3], 0))
    of_all = lambda j: pl.BlockSpec((128, 1024), lambda s, at: (4 * j + 2 * at[2] + at[3], 0))
    fixed = lambda *s: pl.BlockSpec(s, lambda s, at: (0, 0))
    ops = [v for j in range(2) for v in (keep[j], got[j], far[j], middle[j])]
    return pl.pallas_call(
        second_norm_kernel,
        grid_spec=pltpu.PrefetchScalarGridSpec(
            num_scalar_prefetch=1, grid=(1,),
            in_specs=[of_half, of_half, fixed(128, 1024), of_chunk] * 2 + [fixed(1, 1024), of_all(0), of_all(1)],
            out_specs=[fixed(256, 1024), fixed(8, 1024)]),
        out_shape=[jax.ShapeDtypeStruct((256, 1024), F32), jax.ShapeDtypeStruct((8, 1024), F32)],
        name="second_norm_back",
        **SMALL,
    )(at, *ops, gain, cot, cot)


def far_sum_kernel(at_ref, keep_ref, got0_ref, got1_ref, o_ref):
    for j, got_ref in enumerate((got0_ref, got1_ref)):

        @pl.when(pl.program_id(0) == j)
        def _(got_ref=got_ref):
            o_ref[...] = keep_ref[...] + got_ref[...]


def run_far_sum(at, keep, got):
    fixed = pl.BlockSpec((128, 1024), lambda s, at: (0, 0))
    return pl.pallas_call(
        far_sum_kernel,
        grid_spec=pltpu.PrefetchScalarGridSpec(
            num_scalar_prefetch=1, grid=(2,), in_specs=[pl.BlockSpec((128, 1024), lambda s, at: (2 * s + 1 - at[3], 0)), fixed, fixed],
            out_specs=pl.BlockSpec((128, 1024), lambda s, at: (s, 0))),
        out_shape=jax.ShapeDtypeStruct((256, 1024), F32),
        name="far_sum",
        **SMALL,
    )(at, keep, *got)


def first_norm_kernel(at_ref, a_ref, b0_ref, b1_ref, c_ref, y_ref, base_ref, gain_ref, own_ref):
    for j, b_ref in enumerate((b0_ref, b1_ref)):

        @pl.when(pl.program_id(0) == j)
        def _(b_ref=b_ref):
            dy, _ = norm_gradient(a_ref[...] + b_ref[...] + c_ref[...], y_ref[...].astype(F32), gain_ref[...])
            own_ref[...] = dy + base_ref[...]


def run_first_norm(at, keep, got, far, tokens, base, gain):
    of_half = pl.BlockSpec((128, 1024), lambda s, at: (2 * s + at[3], 0))
    of_all = pl.BlockSpec((128, 1024), lambda s, at: (4 * s + 2 * at[2] + at[3], 0))
    own = pl.BlockSpec((128, 1024), lambda s, at: (s, 0))
    fixed = lambda *n: pl.BlockSpec(n, lambda s, at: (0, 0))
    return pl.pallas_call(
        first_norm_kernel,
        grid_spec=pltpu.PrefetchScalarGridSpec(
            num_scalar_prefetch=1, grid=(2,),
            in_specs=[of_half, fixed(128, 1024), fixed(128, 1024), own, of_all, own, fixed(1, 1024)], out_specs=own),
        out_shape=jax.ShapeDtypeStruct((256, 1024), F32),
        name="first_norm_back",
        **SMALL,
    )(at, keep, *got, far, tokens, base, gain)


def place_kernel(at_ref, r0_ref, g0_ref, r1_ref, g1_ref, *rest):
    result_ref, grad_ref = rest[-2:]

    @pl.when(lax.rem(pl.program_id(0), 2) == 0)
    def _():
        result_ref[...] = r0_ref[...].astype(BF16)
        grad_ref[...] = g0_ref[...]

    @pl.when(lax.rem(pl.program_id(0), 2) == 1)
    def _():
        result_ref[...] = r1_ref[...].astype(BF16)
        grad_ref[...] = g1_ref[...]


def run_place(at, odd, pieces, into=()):
    chunk = lambda s: lax.div(s, 2)
    place = lambda s, at: jnp.bitwise_xor(2 * at[2] + at[3], 2 * lax.rem(s, 2) + odd)
    piece = pl.BlockSpec((128, 1024), lambda s, at: (chunk(s), 0))
    placed = pl.BlockSpec((128, 1024), lambda s, at: (4 * chunk(s) + place(s, at), 0))
    return pl.pallas_call(
        place_kernel,
        grid_spec=pltpu.PrefetchScalarGridSpec(
            num_scalar_prefetch=1, grid=(4,),
            in_specs=[piece] * 4 + [pl.BlockSpec(memory_space=pl.ANY)] * len(into),
            out_specs=[placed, placed]),
        out_shape=[jax.ShapeDtypeStruct((1024, 1024), BF16), jax.ShapeDtypeStruct((1024, 1024), F32)],
        input_output_aliases={5: 0, 6: 1} if into else {},
        name="place_rows",
        **SMALL,
    )(at, *pieces, *into)


def feed_grads_kernel(l0_ref, l1_ref, r0_ref, r1_ref, c0_ref, c1_ref, h0_ref, h1_ref, out):
    w1, w2 = r0_ref.shape[1], h0_ref.shape[1]
    first = tn(l0_ref[...], r0_ref[...]) + tn(l1_ref[...], r1_ref[...])
    second = tn(c0_ref[...], h0_ref[...]) + tn(c1_ref[...], h1_ref[...])
    for x in range(4):
        for zh in range(2):
            row = zh * 128 + x * 32
            out[x, 0, zh, :, 0:w1] = first[row : row + 32]
            out[x, 0, zh, :, w1 : w1 + w2] = second[row : row + 32]
            out[x, 0, zh, :, w1 + w2 :] = jnp.zeros((32, out.shape[-1] - w1 - w2), F32)


def run_feed_grads(n2, gg, cot, hid):
    t = cot.shape[0] // 2
    c = gg[0].shape[1] + hid[0].shape[1]
    wide = -(-c // 128) * 128
    cols = lambda j: pl.BlockSpec((t, CH), lambda s: (j, s))
    whole = lambda a: pl.BlockSpec(a.shape, lambda s: (0, 0))
    return pl.pallas_call(
        feed_grads_kernel,
        grid=(4,),
        in_specs=[cols(0), cols(0), whole(gg[0]), whole(gg[1]), cols(0), cols(1), whole(hid[0]), whole(hid[1])],
        out_specs=pl.BlockSpec((4, 1, 2, 32, wide), lambda s: (0, s, 0, 0, 0)),
        out_shape=jax.ShapeDtypeStruct((4, 4, 2, 32, wide), F32),
        compiler_params=pltpu.CompilerParams(vmem_limit_bytes=VMEM_BYTES),
        cost_estimate=weight(12),
        name="feed_weight_grads",
    )(n2[0], n2[1], gg[0], gg[1], cot, cot, hid[0], hid[1])


RING_OUTS = ((0, None, 0), (2, 0, 1), (1, 1, 1), (3, 0, 2), (2, 1, 2), (1, 0, 3), (3, 1, 4))


def mixer_grads_kernel(at_ref, l_ref, r0_ref, a0_ref, m0_ref, m1_ref, small_ref, gup_ref, bias_ref, *outs):
    step = pl.program_id(0)
    w1 = r0_ref.shape[1]

    @pl.when(step < 4)
    def _():
        n = m0_ref.shape[0]
        first = tn(l_ref[...], r0_ref[...])
        second = tn(a0_ref[0:n], m0_ref[...].astype(BF16)) + tn(a0_ref[n:], m1_ref[...].astype(BF16))

        def write(ref, x, to):
            for zh in range(2):
                row = zh * 128 + x * 32
                ref[2 * to + zh, :, 0:w1] = first[row : row + 32]
                ref[2 * to + zh, :, w1:] = second[row : row + 32]

        offset = lax.rem(step - at_ref[1] + 4, 4)

        for k, late, ref in RING_OUTS:

            @pl.when(offset == k)
            def _(late=late, ref=ref):
                for x in range(4):
                    if late is None or late == x // 2:
                        write(outs[ref], x, x if ref < 3 else x % 2)

    @pl.when(step == 4)
    def _():
        small = small_ref[...]
        for out in (outs[0], outs[1], outs[2], outs[4]):
            last = out.shape[0] - 1
            out[last] = jnp.zeros(out.shape[1:], F32)
            out[last, 0:16, :] = small[0:16, 0:768]
            for j in range(3):
                n = min(6, 16 - 6 * j)
                out[last, 16 : 16 + n, 256 * j : 256 * (j + 1)] = small[6 * j : 6 * j + n, 768:1024]
            for j in range(6):
                n = min(3, 16 - 3 * j)
                out[last, 22 : 22 + n, 128 * j : 128 * (j + 1)] = gup_ref[3 * j : 3 * j + n, :]
            out[last, 25:26, :] = small[16:17, 0:768]
            out[last, 26:27, :] = small[17:18, 0:768]
            out[last, 27:28, 0:256] = small[16:17, 768:1024]
            out[last, 27:28, 256:512] = small[17:18, 768:1024]
            out[last, 27:28, 512:640] = bias_ref[0:1, :]


def run_mixer_grads(at, n1, dqkv, ga, mixed, small, gup, bias):
    t, c = n1.shape[0], dqkv.shape[1] + mixed[0].shape[1]
    cols = pl.BlockSpec((t, CH), lambda s, at: (0, jnp.minimum(s, 3)))
    whole = lambda a: pl.BlockSpec(a.shape, lambda s, at: (0, 0))
    rest = [small, gup, bias]
    counts = [9, 9, 9, 4, 5]
    return pl.pallas_call(
        mixer_grads_kernel,
        grid_spec=pltpu.PrefetchScalarGridSpec(
            num_scalar_prefetch=1, grid=(5,),
            in_specs=[cols, whole(dqkv), cols, whole(mixed[0]), whole(mixed[1])] + [whole(a) for a in rest],
            out_specs=[pl.BlockSpec((n, 32, c), lambda s, at: (0, 0, 0)) for n in counts]),
        out_shape=[jax.ShapeDtypeStruct((n, 32, c), F32) for n in counts],
        compiler_params=pltpu.CompilerParams(vmem_limit_bytes=VMEM_BYTES),
        cost_estimate=weight(8),
        name="mixer_weight_grads",
    )(at, n1, dqkv, ga, mixed[0], mixed[1], *rest)


def unpack_kernel(
    own_ref, got_ref, a_ref, b_ref, sums_ref, far_ref,
    g1_ref, down_ref, up_ref, bias_ref, g2_ref, q_ref, k_ref, v_ref, o_ref, gate_ref, mup_ref, mdown_ref,
):
    rows = own_ref[...] + got_ref[...]
    feed = a_ref[...] + b_ref[...]
    own = rows[:, 768:1536]
    sums = sums_ref[...] + far_ref[...]
    wide = jnp.concatenate([sums[16:22, 0:256], sums[16:22, 256:512], sums[16:20, 512:768]], axis=0)
    down_ref[...] = jnp.concatenate([sums[0:16], wide], axis=1)
    for j in range(6):
        n = min(3, 16 - 3 * j)
        up_ref[3 * j : 3 * j + n, :] = own[22 : 22 + n, 128 * j : 128 * (j + 1)]
    g1_ref[:, 0:768] = sums[25:26]
    g1_ref[:, 768:1024] = sums[27:28, 0:256]
    g2_ref[:, 0:768] = sums[26:27]
    g2_ref[:, 768:1024] = sums[27:28, 256:512]
    bias_ref[...] = own[27:28, 512:640]
    q_ref[...] = rows[:, 0:128]
    k_ref[...] = rows[:, 128:256]
    v_ref[...] = rows[:, 256:512]
    o_ref[...] = rows[:, 512:768]
    gate_ref[...] = feed[:, 0:704]
    mup_ref[...] = feed[:, 704:1408]
    mdown_ref[...] = feed[:, 1408:2112]


def unpack(own, got, feed_own, feed_got, sums, far):
    shapes = [(1, 1024), (16, 1024), (16, 128), (1, 128), (1, 1024), (32, 128), (32, 128), (32, 256), (32, 256)] + [(32, 704)] * 3
    return pl.pallas_call(
        unpack_kernel, out_shape=[jax.ShapeDtypeStruct(s, F32) for s in shapes], name="unpack", **SMALL,
    )(own, got, feed_own, feed_got, sums, far)


def after(value, *others):
    return lax.optimization_barrier((value, others))[0]


def send(v, shifts, d):
    return lax.ppermute(v, "dp", shifts[d])


GX = [[(y * 2 + z) * 4 + x for x in range(4)] for y in range(4) for z in range(2)]
GY = [[(y * 2 + z) * 4 + x for y in range(4)] for x in range(4) for z in range(2)]


def scatter_rows(v, groups):
    return lax.psum_scatter(v, "dp", scatter_dimension=0, tiled=True, axis_index_groups=groups)


def ring_first(v, shifts):
    return lax.ppermute(v[1], "dp", shifts[1]), lax.ppermute(v[2], "dp", shifts[3])


def ring_on(v, got):
    n = v[3].shape[0]
    return v[3] + got[0][:n], v[4] + got[1][n:]


def ring_last(on, shifts):
    return lax.ppermute(on[0], "dp", shifts[1]), lax.ppermute(on[1], "dp", shifts[3])


def ring_total(v, got, last):
    n = last[0].shape[0]
    return jnp.concatenate([v[0][:n] + last[0] + got[1][:n], v[0][n:] + got[0][n:] + last[1]], axis=0)


def pick(v, i, dim):
    return lax.dynamic_index_in_dim(v, i, dim, False)


def swap_zh(v, zh, dim):
    return pick(v, zh, dim) + lax.ppermute(pick(v, 1 - zh, dim), "dp", ZH)


def local(tokens, lengths, g1, wq, wk, wv, wgd, wgu, bias, wout, g2, wg, wu, wd, cot):
    mp, dp = lax.axis_index("mp"), lax.axis_index("dp")
    core, z = mp % 2, mp // 2
    ix, zh, iy = dp % 4, (dp // 4) % 2, dp // 8
    at = jnp.stack([ix, iy, core, z]).astype(jnp.int32)
    g1r, g2r, biasr = g1.reshape(1, -1), g2.reshape(1, -1), bias.reshape(1, -1)
    wgd_t, wg_t, wu_t = wgd.T, wg.T, wu.T

    def phase(*values):
        return lax.optimization_barrier(values)

    def across(v, at_here, shifts, take):
        return [take(v, at_here)] + [send(take(v, (at_here + k) % 4), shifts, k) for k in (1, 3, 2)]

    with jax.named_scope("out_weights"):
        wide = wout.astype(F32)
        wout_z = z_swap(wide)
        wout_c = core_swap(wide)
    n1, q, k, v, low, logits, cum, mixed_lo, mixed_hi, st = run_mixer_forward(
        lengths, after(tokens, wide), g1r, wq, wk, wv, wgd_t, wgu, biasr)
    wout_z, wout_c, mixed_lo, mixed_hi = phase(wout_z, wout_c, mixed_lo, mixed_hi)

    with jax.named_scope("heads_one"):
        hi_z = z_swap(mixed_hi)
        hi_c = core_swap(mixed_hi)
        lo_c = core_swap(mixed_lo)
        wout_cz = core_swap(wout_z)
    wo, gh = run_before_feed((wout, wout_z, wout_c, wout_cz), cot, wd)
    hi_z, hi_c, lo_c, mixed_lo, wo, gh = phase(hi_z, hi_c, lo_c, mixed_lo, wo, gh)

    with jax.named_scope("heads_two"):
        lo_z = z_swap(mixed_lo)
        hi_cz = core_swap(hi_z)
    one = run_feed(at, 1, tokens, gh, (mixed_hi, hi_z, hi_c, hi_cz), wo, g2r, wg_t, wu_t, wd)
    lo_z, one = phase(lo_z, one)

    with jax.named_scope("second_norm_core"):
        part_in1 = core_swap(one[6])
        dn2_out1 = add_quarter(at, (one[7], part_in1))
    dn2_out1, part_in1, one, lo_z = phase(dn2_out1, part_in1, one, lo_z)

    with jax.named_scope("second_norm_z"):
        dn2_z1 = z_swap(dn2_out1)
        lo_cz = core_swap(lo_z)
    zero = run_feed(at, 0, tokens, gh, (mixed_lo, lo_z, lo_c, lo_cz), wo, g2r, wg_t, wu_t, wd)
    dn2_z1, zero = phase(dn2_z1, zero)

    with jax.named_scope("second_norm_core"):
        part_in0 = core_swap(zero[6])
        dn2_out0 = add_quarter(at, (zero[7], part_in0))
    dn2_out0, part_in0, one, zero = phase(dn2_out0, part_in0, one, zero)

    middle, n2, hid, gg, feed_out, feed_keep, _, part_keep = zip(zero, one)
    with jax.named_scope("second_norm_z"):
        dn2_z0 = z_swap(dn2_out0)
        feed_in = [core_swap(f) for f in feed_out]
    a = run_feed_grads(n2, gg, cot, hid)
    dn2_z0, feed_in, a = phase(dn2_z0, feed_in, a)

    gm0, gain2 = run_second_norm(at, part_keep, (part_in0, part_in1), (dn2_z0, dn2_z1), middle, g2r, cot)
    gm0, a, feed_in = phase(gm0, a, feed_in)
    with jax.named_scope("second_norm_join"):
        gm1 = z_swap(gm0)
        gm2 = core_swap(gm0)
    with jax.named_scope("feed_grads_x"):
        a = scatter_rows(a.reshape(1024, a.shape[-1]), GX)
    with jax.named_scope("feed_sum"):
        feed_z_out = add_quarter(at, (feed_keep[0], feed_in[0]), (feed_keep[1], feed_in[1]))
    gm1, gm2, feed_z_out = phase(gm1, gm2, feed_z_out)

    with jax.named_scope("second_norm_join"):
        gm3 = core_swap(gm1)
    gm3, gm1, feed_z_out = phase(gm3, gm1, feed_z_out)

    with jax.named_scope("feed_sum"):
        feed_z = z_swap(feed_z_out)
    gm = (gm0, gm1, gm2, gm3)
    dqkv, *part1_out, part1_keep, ga, small, gup, gbias = run_mixer_backward(
        at, lengths, gm, gain2, tokens, n1, q, k, v, low, logits, cum, st, wout, wq, wk, wv, wgd_t, wgu)
    with jax.named_scope("first_norm_core"):
        part1_in = [core_swap(p) for p in part1_out]
    c = run_mixer_grads(at, n1, dqkv, ga, (mixed_lo, mixed_hi), small, gup, gbias)
    feed_z, part1_in, part1_keep, c = phase(feed_z, part1_in, part1_keep, c)

    dn1_out = run_far_sum(at, part1_keep, part1_in[:2])
    dn1_out, c = phase(dn1_out, c)
    with jax.named_scope("first_norm_z"):
        dn1_z = z_swap(dn1_out)
    with jax.named_scope("mixer_grads_first"):
        c_got = ring_first(c, YS)
    feed_own = run_quarter_sum(at, feed_keep, feed_in, feed_z, middle)
    with jax.named_scope("result_join"):
        feed1 = z_swap(feed_own)
    grad0 = run_first_norm(at, part1_keep, part1_in[2:], dn1_z, tokens, gm0, g1r)
    with jax.named_scope("mixer_grads_last"):
        c_last = ring_last(ring_on(c, c_got), YS)
        c = ring_total(c, c_got, c_last)
    feed1, grad0, c, feed_own, a = phase(feed1, grad0, c, feed_own, a)

    with jax.named_scope("grad_join"):
        grad1 = z_swap(grad0)
        grad2 = core_swap(grad0)
    with jax.named_scope("result_join"):
        feed2 = core_swap(feed_own)
    with jax.named_scope("feed_grads_y"):
        a = scatter_rows(a, GY).reshape(2, 32, -1)
    with jax.named_scope("mixer_grads_two"):
        x_pair, x_one = ix // 2, ix % 2
        c_far = lax.ppermute(jnp.concatenate([rows_of(c, 4 * (1 - x_pair), 4), c[8:9]], axis=0), "dp", XS[2])
    placed = run_place(at, 0, after((feed_own, grad0, feed2, grad2), c))
    with jax.named_scope("mixer_grads_two"):
        c = jnp.concatenate([rows_of(c, 4 * x_pair, 4), c[8:9]], axis=0) + c_far
        c = after(c, placed)
        c_near = lax.ppermute(jnp.concatenate([rows_of(c, 2 * (1 - x_one), 2), c[4:5]], axis=0), "dp", X_PAIR)
        c = jnp.concatenate([rows_of(c, 2 * x_one, 2), c[4:5]], axis=0) + c_near
    with jax.named_scope("rows"):
        c = after(c, grad1)
        turned = lambda i: jnp.concatenate([pick(c, i, 0), c[2]], axis=1)
        own = turned(zh)
        got = lax.ppermute(turned(1 - zh), "dp", ZH)
        a_own = pick(a, zh, 0)
        a_got = lax.ppermute(after(pick(a, 1 - zh, 0), c), "dp", ZH)
    with jax.named_scope("result_join"):
        feed3 = core_swap(feed1)
    with jax.named_scope("grad_join"):
        grad3 = core_swap(grad1)
    result, grad_tokens = run_place(at, 1, (feed1, grad1, feed3, grad3), placed)
    with jax.named_scope("small_sums"):
        sums = own[:, 768:1536] + got[:, 768:1536]
        sums = sums + core_swap(sums)
        far = z_swap(sums)
        (gain_one, gate_down, gate_up, gate_bias, gain_two, d_query, d_key, d_value, d_out, d_gate, d_up, d_down) = unpack(
            own, got, a_own, a_got, sums, after(far, result))

    return (
        result,
        grad_tokens,
        gain_one.reshape(1024),
        d_query,
        d_key,
        d_value,
        gate_down.T,
        gate_up,
        gate_bias.reshape(128),
        d_out.T,
        gain_two.reshape(1024),
        d_gate,
        d_up,
        d_down.T,
    )


def solution(mesh):
    placed = (
        P("dp", None), P("dp", None), P(), P(None, "mp"), P(None, "mp"), P(None, "mp"), P(), P(None, "mp"),
        P("mp"), P("mp", None), P(), P(None, "mp"), P(None, "mp"), P("mp", None), P("dp", None),
    )
    outs = (
        P("dp", None), P("dp", None), P(), P("dp", "mp"), P("dp", "mp"), P("dp", "mp"), P(), P(None, "mp"),
        P("mp"), P("mp", "dp"), P(), P("dp", "mp"), P("dp", "mp"), P("mp", "dp"),
    )
    return jax.shard_map(local, mesh=mesh, in_specs=placed, out_specs=outs, check_vma=False)
```

```python
import functools

import jax
import jax.numpy as jnp
from jax import lax
from jax.experimental import pallas as pl
from jax.experimental.pallas import tpu as pltpu
from jax.sharding import PartitionSpec as P

BLK = 64
CH = 256
EPS = 1e-6
SCALE = 128 ** -0.5
F32 = jnp.float32
BF16 = jnp.bfloat16
VMEM_BYTES = 63_400_000
BACK_US = 16
FWD_ROWS = 256
BWD_ROWS = 256


def weight(us):
    return pl.CostEstimate(flops=int(us * 1.0e9), bytes_accessed=1024, transcendentals=0)


def nn(a, b, **kw):
    return lax.dot_general(a, b, (((1,), (0,)), ((), ())), preferred_element_type=F32, **kw)


def nt(a, b, **kw):
    return lax.dot_general(a, b, (((1,), (1,)), ((), ())), preferred_element_type=F32, **kw)


def tn(a, b, **kw):
    return lax.dot_general(a, b, (((0,), (0,)), ((), ())), preferred_element_type=F32, **kw)


HIGH = dict(precision=lax.Precision.HIGHEST)


CORE = [(0, 1), (1, 0), (2, 3), (3, 2)]
ZLO = [(0, 2), (2, 0), (1, 3), (3, 1)]


def dp_perm(dy, dz, dx):
    out = []
    for y in range(4):
        for z in range(2):
            for x in range(4):
                out.append(((y * 2 + z) * 4 + x, (((y + dy) % 4) * 2 + (z + dz) % 2) * 4 + (x + dx) % 4))
    return out


XS = {1: dp_perm(0, 0, 1), 3: dp_perm(0, 0, -1), 2: dp_perm(0, 0, 2)}
YS = {1: dp_perm(1, 0, 0), 3: dp_perm(-1, 0, 0), 2: dp_perm(2, 0, 0)}
ZH = dp_perm(0, 1, 0)
Y_PAIR = [((y * 2 + z) * 4 + x, ((y ^ 1) * 2 + z) * 4 + x) for y in range(4) for z in range(2) for x in range(4)]
X_PAIR = [((y * 2 + z) * 4 + x, (y * 2 + z) * 4 + (x ^ 1)) for y in range(4) for z in range(2) for x in range(4)]


def core_swap(v):
    return lax.ppermute(v, "mp", CORE)


def z_swap(v):
    return lax.ppermute(v, "mp", ZLO)


def rows_of(v, start, size):
    return lax.dynamic_slice_in_dim(v, start, size, 0)


def item_starts(len_ref):
    starts, total = [], jnp.int32(0)
    for j in range(8):
        starts.append(total)
        total = total + len_ref[0, j]
    return starts


def start_at(starts, place):
    best = jnp.int32(0)
    for s in starts[1:]:
        best = jnp.where(s <= place, jnp.maximum(best, s), best)
    return best


def chunk_masks(starts, base):
    row = lax.broadcasted_iota(jnp.int32, (CH, CH), 0)
    col = lax.broadcasted_iota(jnp.int32, (CH, CH), 1)
    blk = jnp.bitwise_and(row, -BLK)
    row1 = lax.broadcasted_iota(jnp.int32, (CH, 128), 0)
    place = row1 + base
    low = jnp.zeros_like(place)
    for s in starts[1:]:
        low = jnp.where(place >= s, jnp.maximum(low, s), low)
    low = low - base
    blk1 = jnp.bitwise_and(row1, -BLK)
    carried = low < blk1
    low_wide = jnp.concatenate([low, low], axis=1)
    causal = (col <= row) & (col >= blk)
    visible = causal & (col >= low_wide)
    return visible, carried


def causal_ones():
    row = lax.broadcasted_iota(jnp.int32, (CH, CH), 0)
    col = lax.broadcasted_iota(jnp.int32, (CH, CH), 1)
    return jnp.where((col <= row) & (col >= jnp.bitwise_and(row, -BLK)), 1.0, 0.0).astype(BF16)


def two_parts(v):
    high = v.astype(BF16)
    return high, (v - high.astype(F32)).astype(BF16)


def block_scalars(starts, base, b):
    first = base + b * BLK
    origin = start_at(starts, first + BLK - 1)
    keep = jnp.where(origin < first, 1.0, 0.0).astype(F32)
    place = lax.broadcasted_iota(jnp.int32, (BLK, 128), 0) + first
    return keep, place >= origin


def scaled_parts(q, k, cum):
    last = jnp.broadcast_to(cum.reshape(CH // BLK, BLK, 128)[:, BLK - 1 :, :], (CH // BLK, BLK, 128))
    last = last.reshape(CH, 128)
    e, en, ef = jnp.exp(cum), jnp.exp(-cum), jnp.exp(last - cum)
    qf = q.astype(F32) * SCALE * e
    ks = k.astype(F32) * en
    kf = k.astype(F32) * ef
    return last, e, en, ef, qf, ks, kf


def mixer_forward(
    len_ref, tok_ref, g1_ref, wq_ref, wk_ref, wv_ref, wgd_ref, wgu_ref, bias_ref,
    n_ref, q_ref, k_ref, v_ref, low_ref, logit_ref, cum_ref, mixed_lo_ref, mixed_hi_ref, st_ref, state,
):
    step = pl.program_id(0)
    rows = tok_ref.shape[0]
    starts = item_starts(len_ref)

    @pl.when(step == 0)
    def _():
        state[...] = jnp.zeros_like(state)

    ones = causal_ones()
    s = state[...]
    for c in range(rows // CH):
        base = step * rows + c * CH
        at = slice(c * CH, (c + 1) * CH)
        x = tok_ref[at, :].astype(F32)
        r = lax.rsqrt(jnp.mean(x * x, axis=-1, keepdims=True) + EPS)
        n = (x * r * g1_ref[...]).astype(BF16)
        n_ref[at, :] = n
        low = nt(n, wgd_ref[...]).astype(BF16)
        low_ref[at, :] = low
        logits = nn(low, wgu_ref[...]) + bias_ref[...]
        logit_ref[at, :] = logits
        decays = (jnp.minimum(logits, 0.0) - jnp.log1p(jnp.exp(-jnp.abs(logits)))) * (1.0 / 16.0)
        high, rest = two_parts(decays)
        cum = nn(ones, high) + nn(ones, rest)
        cum_ref[at, :] = cum
        q = nn(n, wq_ref[...]).astype(BF16)
        k = nn(n, wk_ref[...]).astype(BF16)
        v = nn(n, wv_ref[...]).astype(BF16)
        q_ref[at, :] = q
        k_ref[at, :] = k
        v_ref[at, :] = v
        visible, carried = chunk_masks(starts, base)
        last, e, en, ef, qf, ks, kf = scaled_parts(q, k, cum)
        scores = jnp.where(visible, nt(qf.astype(BF16), ks.astype(BF16)), 0.0).astype(BF16)
        out = nn(scores, v)
        q_carried = jnp.where(carried, qf, 0.0).astype(BF16)
        mixed_parts = []
        for b in range(CH // BLK):
            sl = slice(b * BLK, (b + 1) * BLK)
            keep, tail = block_scalars(starts, base, b)
            st_ref[c * (CH // BLK) + b] = s
            inter = nt(q_carried[sl], s.astype(BF16))
            mixed_parts.append((out[sl] + inter).astype(BF16).astype(F32))
            k_tail = jnp.where(tail, kf[sl], 0.0).astype(BF16)
            s = keep * jnp.exp(last[b * BLK : b * BLK + 1]) * s + tn(v[sl], k_tail)
        mixed = jnp.concatenate(mixed_parts, axis=0)

        @pl.when(step < 2)
        def _(mixed=mixed):
            mixed_lo_ref[...] = mixed

        @pl.when(step >= 2)
        def _(mixed=mixed):
            mixed_hi_ref[...] = mixed

    state[...] = s


def run_mixer_forward(lengths, tokens, g1, wq, wk, wv, wgd, wgu, bias):
    t = tokens.shape[0]
    whole = lambda a: pl.BlockSpec(a.shape, lambda i: (0,) * a.ndim)
    rows = lambda c: pl.BlockSpec((CH, c), lambda i: (i, 0))
    nb = CH // BLK
    outs = [
        ((t, 1024), BF16), ((t, 128), BF16), ((t, 128), BF16), ((t, 256), BF16), ((t, 16), BF16), ((t, 128), F32), ((t, 128), F32),
    ]
    sds = jax.ShapeDtypeStruct
    return pl.pallas_call(
        mixer_forward,
        grid=(t // CH,),
        in_specs=[pl.BlockSpec(memory_space=pltpu.SMEM), rows(1024), whole(g1), whole(wq), whole(wk), whole(wv),
                  whole(wgd), whole(wgu), whole(bias)],
        out_specs=[rows(s[1]) for s, _ in outs]
        + [pl.BlockSpec((CH, 256), lambda i: (jnp.minimum(i, 1), 0)), pl.BlockSpec((CH, 256), lambda i: (jnp.maximum(i - 2, 0), 0)),
           pl.BlockSpec((nb, 256, 128), lambda i: (i, 0, 0))],
        out_shape=[sds(s, d) for s, d in outs] + [sds((t // 2, 256), F32)] * 2 + [sds((t // BLK, 256, 128), F32)],
        scratch_shapes=[pltpu.VMEM((256, 128), F32)],
        compiler_params=pltpu.CompilerParams(vmem_limit_bytes=VMEM_BYTES),
        cost_estimate=weight(10),
        name="mixer_forward",
    )(lengths, tokens, g1, wq, wk, wv, wgd, wgu, bias)


def before_feed_kernel(w0_ref, w1_ref, w2_ref, w3_ref, cot_ref, wd_ref, wo_ref, gh_ref):
    for j, w_ref in enumerate((w0_ref, w1_ref, w2_ref, w3_ref)):

        @pl.when(pl.program_id(0) == j)
        def _(w_ref=w_ref):
            wo_ref[...] = w_ref[...].astype(BF16)

    gh_ref[...] = nt(cot_ref[...], wd_ref[...])


def run_before_feed(wo, cot, wd):
    t = cot.shape[0]
    whole = lambda a: pl.BlockSpec(a.shape, lambda s: (0,) * a.ndim)
    rows = lambda c: pl.BlockSpec((CH, c), lambda s: (s, 0))
    return pl.pallas_call(
        before_feed_kernel,
        grid=(t // CH,),
        in_specs=[whole(w) for w in wo] + [rows(1024), whole(wd)],
        out_specs=[rows(1024), rows(704)],
        out_shape=[jax.ShapeDtypeStruct((t, 1024), BF16), jax.ShapeDtypeStruct((t, 704), F32)],
        compiler_params=pltpu.CompilerParams(vmem_limit_bytes=VMEM_BYTES),
        cost_estimate=weight(7),
        name="before_feed",
    )(*wo, cot, wd)


def feed_kernel(
    at_ref, tok_ref, gh_ref, m0_ref, m1_ref, m2_ref, m3_ref, wo_ref, g2_ref, wg_ref, wu_ref, wd_ref,
    mid_ref, n_ref, hid_ref, gg_ref, feed_out_ref, feed_keep_ref, part_out_ref, part_keep_ref,
):
    step = pl.program_id(0)

    mixed = jnp.concatenate([m0_ref[...], m1_ref[...], m2_ref[...], m3_ref[...]], axis=1).astype(BF16)
    mid = tok_ref[...].astype(F32) + nn(mixed, wo_ref[...])
    mid_ref[...] = mid
    r = lax.rsqrt(jnp.mean(mid * mid, axis=-1, keepdims=True) + EPS)
    n = (mid * r * g2_ref[...]).astype(BF16)
    n_ref[...] = n
    pre = nt(n, wg_ref[...])
    up = nt(n, wu_ref[...])
    sg = jax.nn.sigmoid(pre)
    act = pre * sg
    hid = (act * up).astype(BF16)
    hid_ref[...] = hid
    gh = gh_ref[...]
    gg = (gh * up * sg * (1.0 + pre * (1.0 - sg))).astype(BF16)
    gu = (gh * act).astype(BF16)
    gg_ref[:, 0:704] = gg
    gg_ref[:, 704:1408] = gu
    feed = nn(hid, wd_ref[...])
    part = nn(gg, wg_ref[...]) + nn(gu, wu_ref[...])

    @pl.when(step == 0)
    def _():
        feed_out_ref[...] = feed
        part_out_ref[...] = part

    @pl.when(step == 1)
    def _():
        feed_keep_ref[...] = feed
        part_keep_ref[...] = part


def run_feed(at, chunk, tokens, gh, mixed, wo, g2, wg, wu, wd):
    t = tokens.shape[0] // 2
    whole = lambda a: pl.BlockSpec(a.shape, lambda s, at: (0,) * a.ndim)
    half = lambda s, at: jnp.bitwise_xor(1 - at[2], s)
    rows = lambda c: pl.BlockSpec((CH, c), lambda s, at: (half(s, at), 0))
    from_all = lambda c: pl.BlockSpec((CH, c), lambda s, at: (2 * chunk + half(s, at), 0))
    once = pl.BlockSpec((CH, 1024), lambda s, at: (0, 0))
    sds = jax.ShapeDtypeStruct
    return pl.pallas_call(
        feed_kernel,
        grid_spec=pltpu.PrefetchScalarGridSpec(
            num_scalar_prefetch=1,
            grid=(t // CH,),
            in_specs=[from_all(1024), from_all(704)] + [rows(256)] * 4 + [whole(wo), whole(g2), whole(wg), whole(wu), whole(wd)],
            out_specs=[rows(1024), rows(1024), rows(704), rows(1408), once, once, once, once],
        ),
        out_shape=[sds((t, 1024), F32), sds((t, 1024), BF16), sds((t, 704), BF16), sds((t, 1408), BF16)] + [sds((CH, 1024), F32)] * 4,
        compiler_params=pltpu.CompilerParams(vmem_limit_bytes=VMEM_BYTES),
        cost_estimate=weight(14),
        name="feed_both_ways",
    )(at, tokens, gh, *mixed, wo, g2, wg, wu, wd)


def mixer_backward(
    at_ref, len_ref, *refs,
):
    gm_refs, gain_ref, refs = refs[:4], refs[4], refs[5:]
    (tok_ref, n_ref, q_ref, k_ref, v_ref, low_ref, logit_ref, cum_ref,
     st_ref, wo_ref, wq_ref, wk_ref, wv_ref, wgd_ref, wgu_ref,
     dqkv_ref, far0_ref, far1_ref, near0_ref, near1_ref, part_keep_ref, ga_ref, small_ref, gup_ref, bias_ref, dstate, whole) = refs
    step = pl.program_id(0)
    steps = pl.num_programs(0)
    rows = tok_ref.shape[0]
    starts = item_starts(len_ref)

    core, z = at_ref[2], at_ref[3]
    here = steps - 1 - step
    mine = jnp.equal(lax.rem(here, 2), core)

    @pl.when(step == 0)
    def _():
        dstate[...] = jnp.zeros_like(dstate)
        small_ref[...] = jnp.zeros_like(small_ref)
        small_ref[17:18, :] = gain_ref[0:1, :]
        gup_ref[...] = jnp.zeros_like(gup_ref)
        bias_ref[...] = jnp.zeros_like(bias_ref)

    first = pl.multiple_of(z * 128, 128)
    second = pl.multiple_of((1 - z) * 128, 128)
    for other in range(2):

        @pl.when(jnp.logical_not(mine) if other else mine)
        def _(other=other):
            ga_ref[pl.ds(first, 128), :] = gm_refs[2 * other][...].astype(BF16)
            ga_ref[pl.ds(second, 128), :] = gm_refs[2 * other + 1][...].astype(BF16)

    ones = causal_ones()
    ds = dstate[...]
    for c in reversed(range(rows // CH)):
        base = here * rows + c * CH
        at = slice(c * CH, (c + 1) * CH)
        g = nt(ga_ref[at, :], wo_ref[...]).astype(BF16)
        q, k, v, cum = q_ref[at, :], k_ref[at, :], v_ref[at, :], cum_ref[at, :]
        visible, carried = chunk_masks(starts, base)
        last, e, en, ef, qf, ksf, kff = scaled_parts(q, k, cum)
        qs, ks = qf.astype(BF16), ksf.astype(BF16)
        scores = jnp.where(visible, nt(qs, ks), 0.0).astype(BF16)
        dscores = jnp.where(visible, nt(g, v), 0.0).astype(BF16)
        dv = tn(scores, g)
        dqs = nn(dscores, ks)
        dks = tn(dscores, qs)
        q_carried = jnp.where(carried, qf, 0.0).astype(BF16)
        dvs, dkfs, dqss, dls = [], [], [], []
        for b in reversed(range(CH // BLK)):
            sl = slice(b * BLK, (b + 1) * BLK)
            keep, tail = block_scalars(starts, base, b)
            dsb = ds.astype(BF16)
            s = st_ref[c * (CH // BLK) + b]
            k_tail = jnp.where(tail, kff[sl], 0.0).astype(BF16)
            dvs.append(dv[sl] + nt(k_tail, dsb))
            dkf = jnp.where(tail, nn(v[sl], dsb), 0.0)
            dkfs.append(dkf)
            dqss.append(dqs[sl] + jnp.where(carried[sl], nn(g[sl], s.astype(BF16)), 0.0))
            grow = keep * jnp.exp(last[b * BLK : b * BLK + 1])
            dlast = grow * jnp.sum(s * ds, axis=0, keepdims=True) + jnp.sum(dkf * kff[sl], axis=0, keepdims=True)
            dls.append(jnp.broadcast_to(dlast, (BLK, 128)))
            ds = grow * ds + tn(g[sl], q_carried[sl])
        join = lambda parts: jnp.concatenate(parts[::-1], axis=0)
        dqs, dkf, dl = join(dqss), join(dkfs), join(dls)
        dq = (dqs * (SCALE * e)).astype(BF16)
        dk = (dks * en + dkf * ef).astype(BF16)
        dv = join(dvs).astype(BF16)
        dqkv_ref[at, 0:128] = dq
        dqkv_ref[at, 128:256] = dk
        dqkv_ref[at, 256:512] = dv
        high, rest = two_parts(dqs * qf - dks * ksf - dkf * kff)
        ddec = tn(ones, high) + tn(ones, rest) + dl
        glog = ddec * jax.nn.sigmoid(-logit_ref[at, :]) * (1.0 / 16.0)
        bias_ref[0:1, :] += jnp.sum(glog, axis=0, keepdims=True)
        high, rest = two_parts(glog)
        gup_ref[...] += tn(low_ref[at, :], high) + tn(low_ref[at, :], rest)
        glr = (nt(high, wgu_ref[...]) + nt(rest, wgu_ref[...])).astype(BF16)
        part = nt(dq, wq_ref[...]) + nt(dk, wk_ref[...]) + nt(dv, wv_ref[...]) + nn(glr, wgd_ref[...])
        @pl.when(mine)
        def _(part=part):
            part_keep_ref[...] = part

        for chunk, (far_ref, near_ref) in enumerate(((far0_ref, near0_ref), (far1_ref, near1_ref))):

            @pl.when(jnp.logical_and(jnp.logical_not(mine), jnp.equal(lax.div(here, 2), chunk)))
            def _(part=part, far_ref=far_ref, near_ref=near_ref):
                whole[...] = part
                far_ref[...] = whole[pl.ds(second, 128), :]
                near_ref[...] = whole[pl.ds(first, 128), :]

        small_ref[0:16, :] += tn(glr, n_ref[at, :])
        x = tok_ref[at, :].astype(F32)
        r = lax.rsqrt(jnp.mean(x * x, axis=-1, keepdims=True) + EPS)
        small_ref[16:17, :] += jnp.sum(part * x * r, axis=0, keepdims=True)
    dstate[...] = ds


def run_mixer_backward(at, lengths, gm, gain, tokens, n, q, k, v, low, logits, cum, st, wo, wq, wk, wv, wgd, wgu):
    t = tokens.shape[0]
    steps = t // CH
    whole = lambda a: pl.BlockSpec(a.shape, lambda i, at: (0,) * a.ndim)
    rows = lambda c: pl.BlockSpec((CH, c), lambda i, at: (steps - 1 - i, 0))
    split = pl.BlockSpec((CH, 1024), lambda i, at: (lax.div(steps - 1 - i, 2), 0))
    nb = CH // BLK
    fixed = lambda s: pl.BlockSpec(s, lambda i, at: (0, 0))
    sds = jax.ShapeDtypeStruct
    return pl.pallas_call(
        mixer_backward,
        grid_spec=pltpu.PrefetchScalarGridSpec(
            num_scalar_prefetch=1,
            grid=(steps,),
            in_specs=[pl.BlockSpec(memory_space=pltpu.SMEM)] + [pl.BlockSpec((128, 1024), lambda i, at: (lax.div(steps - 1 - i, 2), 0))] * 4 + [whole(gain)]
            + [rows(1024), rows(1024), rows(128), rows(128), rows(256), rows(16), rows(128), rows(128),
               pl.BlockSpec((nb, 256, 128), lambda i, at: (steps - 1 - i, 0, 0)),
               whole(wo), whole(wq), whole(wk), whole(wv), whole(wgd), whole(wgu)],
            out_specs=[rows(512)] + [fixed((128, 1024))] * 4 + [split, rows(1024), fixed((24, 1024)), fixed((16, 128)), fixed((8, 128))],
            scratch_shapes=[pltpu.VMEM((256, 128), F32), pltpu.VMEM((CH, 1024), F32)],
        ),
        out_shape=[sds((t, 512), BF16)] + [sds((128, 1024), F32)] * 4 + [sds((t // 2, 1024), F32), sds((t, 1024), BF16),
                   sds((24, 1024), F32), sds((16, 128), F32), sds((8, 128), F32)],
        compiler_params=pltpu.CompilerParams(vmem_limit_bytes=VMEM_BYTES),
        cost_estimate=weight(BACK_US),
        name="mixer_backward",
    )(at, lengths, *gm, gain, tokens, n, q, k, v, low, logits, cum, st, wo, wq, wk, wv, wgd, wgu)


SMALL = dict(
    compiler_params=pltpu.CompilerParams(vmem_limit_bytes=VMEM_BYTES),
    cost_estimate=weight(3),
)


def quarter(v, j, which):
    return rows_of(v, 256 * j + 128 * which, 128)


def norm_gradient(dn, y, gain):
    r = lax.rsqrt(jnp.mean(y * y, axis=-1, keepdims=True) + EPS)
    gd = dn * gain
    dy = r * gd - (r * r * r) * y * jnp.mean(gd * y, axis=-1, keepdims=True)
    return dy, jnp.sum(dn * y * r, axis=0, keepdims=True)


def second_norm_kernel(at_ref, a0_ref, b0_ref, c0_ref, y0_ref, a1_ref, b1_ref, c1_ref, y1_ref, gain_ref, base0_ref, base1_ref, o_ref, s_ref):
    halves = ((a0_ref, b0_ref, c0_ref, y0_ref, base0_ref), (a1_ref, b1_ref, c1_ref, y1_ref, base1_ref))
    total = jnp.zeros((1, 1024), F32)
    for j, (a_ref, b_ref, c_ref, y_ref, base_ref) in enumerate(halves):
        dy, dgain = norm_gradient(a_ref[...] + b_ref[...] + c_ref[...], y_ref[...], gain_ref[...])
        o_ref[128 * j : 128 * (j + 1)] = base_ref[...].astype(F32) + dy
        total = total + dgain
    s_ref[0:1, :] = total


def run_second_norm(at, keep, got, far, middle, gain, cot):
    of_half = pl.BlockSpec((128, 1024), lambda s, at: (at[3], 0))
    of_chunk = pl.BlockSpec((128, 1024), lambda s, at: (2 * at[2] + at[3], 0))
    of_all = lambda j: pl.BlockSpec((128, 1024), lambda s, at: (4 * j + 2 * at[2] + at[3], 0))
    fixed = lambda *s: pl.BlockSpec(s, lambda s, at: (0, 0))
    ops = [v for j in range(2) for v in (keep[j], got[j], far[j], middle[j])]
    return pl.pallas_call(
        second_norm_kernel,
        grid_spec=pltpu.PrefetchScalarGridSpec(
            num_scalar_prefetch=1, grid=(1,),
            in_specs=[of_half, of_half, fixed(128, 1024), of_chunk] * 2 + [fixed(1, 1024), of_all(0), of_all(1)],
            out_specs=[fixed(256, 1024), fixed(8, 1024)]),
        out_shape=[jax.ShapeDtypeStruct((256, 1024), F32), jax.ShapeDtypeStruct((8, 1024), F32)],
        name="second_norm_back",
        **SMALL,
    )(at, *ops, gain, cot, cot)


def first_norm_kernel(at_ref, a_ref, b0_ref, b1_ref, c_ref, y_ref, base_ref, gain_ref, own_ref):
    for j, b_ref in enumerate((b0_ref, b1_ref)):

        @pl.when(pl.program_id(0) == j)
        def _(b_ref=b_ref):
            dy, _ = norm_gradient(a_ref[...] + b_ref[...] + c_ref[...], y_ref[...].astype(F32), gain_ref[...])
            own_ref[...] = dy + base_ref[...]


def run_first_norm(at, keep, got, far, tokens, base, gain):
    of_half = pl.BlockSpec((128, 1024), lambda s, at: (2 * s + at[3], 0))
    of_all = pl.BlockSpec((128, 1024), lambda s, at: (4 * s + 2 * at[2] + at[3], 0))
    own = pl.BlockSpec((128, 1024), lambda s, at: (s, 0))
    fixed = lambda *n: pl.BlockSpec(n, lambda s, at: (0, 0))
    return pl.pallas_call(
        first_norm_kernel,
        grid_spec=pltpu.PrefetchScalarGridSpec(
            num_scalar_prefetch=1, grid=(2,),
            in_specs=[of_half, fixed(128, 1024), fixed(128, 1024), own, of_all, own, fixed(1, 1024)], out_specs=own),
        out_shape=jax.ShapeDtypeStruct((256, 1024), F32),
        name="first_norm_back",
        **SMALL,
    )(at, keep, *got, far, tokens, base, gain)


def place_kernel(at_ref, r0_ref, g0_ref, r1_ref, g1_ref, *rest):
    result_ref, grad_ref = rest[-2:]

    @pl.when(lax.rem(pl.program_id(0), 2) == 0)
    def _():
        result_ref[...] = r0_ref[...].astype(BF16)
        grad_ref[...] = g0_ref[...]

    @pl.when(lax.rem(pl.program_id(0), 2) == 1)
    def _():
        result_ref[...] = r1_ref[...].astype(BF16)
        grad_ref[...] = g1_ref[...]


def run_place(at, odd, pieces, into=()):
    chunk = lambda s: lax.div(s, 2)
    place = lambda s, at: jnp.bitwise_xor(2 * at[2] + at[3], 2 * lax.rem(s, 2) + odd)
    piece = pl.BlockSpec((128, 1024), lambda s, at: (chunk(s), 0))
    placed = pl.BlockSpec((128, 1024), lambda s, at: (4 * chunk(s) + place(s, at), 0))
    return pl.pallas_call(
        place_kernel,
        grid_spec=pltpu.PrefetchScalarGridSpec(
            num_scalar_prefetch=1, grid=(4,),
            in_specs=[piece] * 4 + [pl.BlockSpec(memory_space=pl.ANY)] * len(into),
            out_specs=[placed, placed]),
        out_shape=[jax.ShapeDtypeStruct((1024, 1024), BF16), jax.ShapeDtypeStruct((1024, 1024), F32)],
        input_output_aliases={5: 0, 6: 1} if into else {},
        name="place_rows",
        **SMALL,
    )(at, *pieces, *into)


def feed_grads_kernel(l0_ref, l1_ref, r0_ref, r1_ref, c0_ref, c1_ref, h0_ref, h1_ref, out):
    w1, w2 = r0_ref.shape[1], h0_ref.shape[1]
    first = tn(l0_ref[...], r0_ref[...]) + tn(l1_ref[...], r1_ref[...])
    second = tn(c0_ref[...], h0_ref[...]) + tn(c1_ref[...], h1_ref[...])
    for x in range(4):
        for zh in range(2):
            row = zh * 128 + x * 32
            out[x, 0, zh, :, 0:w1] = first[row : row + 32]
            out[x, 0, zh, :, w1 : w1 + w2] = second[row : row + 32]
            out[x, 0, zh, :, w1 + w2 :] = jnp.zeros((32, out.shape[-1] - w1 - w2), F32)


def run_feed_grads(n2, gg, cot, hid):
    t = cot.shape[0] // 2
    c = gg[0].shape[1] + hid[0].shape[1]
    wide = -(-c // 128) * 128
    cols = lambda j: pl.BlockSpec((t, CH), lambda s: (j, s))
    whole = lambda a: pl.BlockSpec(a.shape, lambda s: (0, 0))
    return pl.pallas_call(
        feed_grads_kernel,
        grid=(4,),
        in_specs=[cols(0), cols(0), whole(gg[0]), whole(gg[1]), cols(0), cols(1), whole(hid[0]), whole(hid[1])],
        out_specs=pl.BlockSpec((4, 1, 2, 32, wide), lambda s: (0, s, 0, 0, 0)),
        out_shape=jax.ShapeDtypeStruct((4, 4, 2, 32, wide), F32),
        compiler_params=pltpu.CompilerParams(vmem_limit_bytes=VMEM_BYTES),
        cost_estimate=weight(12),
        name="feed_weight_grads",
    )(n2[0], n2[1], gg[0], gg[1], cot, cot, hid[0], hid[1])


RING_OUTS = ((0, None, 0), (2, 0, 1), (1, 1, 1), (3, 0, 2), (2, 1, 2), (1, 0, 3), (3, 1, 4))


def mixer_grads_kernel(at_ref, l_ref, r0_ref, a0_ref, m0_ref, m1_ref, small_ref, gup_ref, bias_ref, *outs):
    step = pl.program_id(0)
    w1 = r0_ref.shape[1]

    @pl.when(step < 4)
    def _():
        n = m0_ref.shape[0]
        first = tn(l_ref[...], r0_ref[...])
        second = tn(a0_ref[0:n], m0_ref[...].astype(BF16)) + tn(a0_ref[n:], m1_ref[...].astype(BF16))

        def write(ref, x, to):
            for zh in range(2):
                row = zh * 128 + x * 32
                ref[2 * to + zh, :, 0:w1] = first[row : row + 32]
                ref[2 * to + zh, :, w1:] = second[row : row + 32]

        offset = lax.rem(step - at_ref[1] + 4, 4)

        for k, late, ref in RING_OUTS:

            @pl.when(offset == k)
            def _(late=late, ref=ref):
                for x in range(4):
                    if late is None or late == x // 2:
                        write(outs[ref], x, x if ref < 3 else x % 2)

    @pl.when(step == 4)
    def _():
        small = small_ref[...]
        for out in (outs[0], outs[1], outs[2], outs[4]):
            last = out.shape[0] - 1
            out[last] = jnp.zeros(out.shape[1:], F32)
            out[last, 0:16, :] = small[0:16, 0:768]
            for j in range(3):
                n = min(6, 16 - 6 * j)
                out[last, 16 : 16 + n, 256 * j : 256 * (j + 1)] = small[6 * j : 6 * j + n, 768:1024]
            for j in range(6):
                n = min(3, 16 - 3 * j)
                out[last, 22 : 22 + n, 128 * j : 128 * (j + 1)] = gup_ref[3 * j : 3 * j + n, :]
            out[last, 25:26, :] = small[16:17, 0:768]
            out[last, 26:27, :] = small[17:18, 0:768]
            out[last, 27:28, 0:256] = small[16:17, 768:1024]
            out[last, 27:28, 256:512] = small[17:18, 768:1024]
            out[last, 27:28, 512:640] = bias_ref[0:1, :]


def run_mixer_grads(at, n1, dqkv, ga, mixed, small, gup, bias):
    t, c = n1.shape[0], dqkv.shape[1] + mixed[0].shape[1]
    cols = pl.BlockSpec((t, CH), lambda s, at: (0, jnp.minimum(s, 3)))
    whole = lambda a: pl.BlockSpec(a.shape, lambda s, at: (0, 0))
    rest = [small, gup, bias]
    counts = [9, 9, 9, 4, 5]
    return pl.pallas_call(
        mixer_grads_kernel,
        grid_spec=pltpu.PrefetchScalarGridSpec(
            num_scalar_prefetch=1, grid=(5,),
            in_specs=[cols, whole(dqkv), cols, whole(mixed[0]), whole(mixed[1])] + [whole(a) for a in rest],
            out_specs=[pl.BlockSpec((n, 32, c), lambda s, at: (0, 0, 0)) for n in counts]),
        out_shape=[jax.ShapeDtypeStruct((n, 32, c), F32) for n in counts],
        compiler_params=pltpu.CompilerParams(vmem_limit_bytes=VMEM_BYTES),
        cost_estimate=weight(8),
        name="mixer_weight_grads",
    )(at, n1, dqkv, ga, mixed[0], mixed[1], *rest)


def unpack_kernel(
    own_ref, got_ref, a_ref, b_ref, sums_ref, far_ref,
    g1_ref, down_ref, up_ref, bias_ref, g2_ref, q_ref, k_ref, v_ref, o_ref, gate_ref, mup_ref, mdown_ref,
):
    rows = own_ref[...] + got_ref[...]
    feed = a_ref[...] + b_ref[...]
    own = rows[:, 768:1536]
    sums = sums_ref[...] + far_ref[...]
    wide = jnp.concatenate([sums[16:22, 0:256], sums[16:22, 256:512], sums[16:20, 512:768]], axis=0)
    down_ref[...] = jnp.concatenate([sums[0:16], wide], axis=1)
    for j in range(6):
        n = min(3, 16 - 3 * j)
        up_ref[3 * j : 3 * j + n, :] = own[22 : 22 + n, 128 * j : 128 * (j + 1)]
    g1_ref[:, 0:768] = sums[25:26]
    g1_ref[:, 768:1024] = sums[27:28, 0:256]
    g2_ref[:, 0:768] = sums[26:27]
    g2_ref[:, 768:1024] = sums[27:28, 256:512]
    bias_ref[...] = own[27:28, 512:640]
    q_ref[...] = rows[:, 0:128]
    k_ref[...] = rows[:, 128:256]
    v_ref[...] = rows[:, 256:512]
    o_ref[...] = rows[:, 512:768]
    gate_ref[...] = feed[:, 0:704]
    mup_ref[...] = feed[:, 704:1408]
    mdown_ref[...] = feed[:, 1408:2112]


def unpack(own, got, feed_own, feed_got, sums, far):
    shapes = [(1, 1024), (16, 1024), (16, 128), (1, 128), (1, 1024), (32, 128), (32, 128), (32, 256), (32, 256)] + [(32, 704)] * 3
    return pl.pallas_call(
        unpack_kernel, out_shape=[jax.ShapeDtypeStruct(s, F32) for s in shapes], name="unpack", **SMALL,
    )(own, got, feed_own, feed_got, sums, far)


def after(value, *others):
    return lax.optimization_barrier((value, others))[0]


def send(v, shifts, d):
    return lax.ppermute(v, "dp", shifts[d])


GX = [[(y * 2 + z) * 4 + x for x in range(4)] for y in range(4) for z in range(2)]
GY = [[(y * 2 + z) * 4 + x for y in range(4)] for x in range(4) for z in range(2)]


def scatter_rows(v, groups):
    return lax.psum_scatter(v, "dp", scatter_dimension=0, tiled=True, axis_index_groups=groups)


def ring_first(v, shifts):
    return lax.ppermute(v[1], "dp", shifts[1]), lax.ppermute(v[2], "dp", shifts[3])


def ring_on(v, got):
    n = v[3].shape[0]
    return v[3] + got[0][:n], v[4] + got[1][n:]


def ring_last(on, shifts):
    return lax.ppermute(on[0], "dp", shifts[1]), lax.ppermute(on[1], "dp", shifts[3])


def ring_total(v, got, last):
    n = last[0].shape[0]
    return jnp.concatenate([v[0][:n] + last[0] + got[1][:n], v[0][n:] + got[0][n:] + last[1]], axis=0)


def pick(v, i, dim):
    return lax.dynamic_index_in_dim(v, i, dim, False)


def swap_zh(v, zh, dim):
    return pick(v, zh, dim) + lax.ppermute(pick(v, 1 - zh, dim), "dp", ZH)


def local(tokens, lengths, g1, wq, wk, wv, wgd, wgu, bias, wout, g2, wg, wu, wd, cot):
    mp, dp = lax.axis_index("mp"), lax.axis_index("dp")
    core, z = mp % 2, mp // 2
    ix, zh, iy = dp % 4, (dp // 4) % 2, dp // 8
    at = jnp.stack([ix, iy, core, z]).astype(jnp.int32)
    g1r, g2r, biasr = g1.reshape(1, -1), g2.reshape(1, -1), bias.reshape(1, -1)
    wgd_t, wg_t, wu_t = wgd.T, wg.T, wu.T

    def phase(*values):
        return lax.optimization_barrier(values)

    def across(v, at_here, shifts, take):
        return [take(v, at_here)] + [send(take(v, (at_here + k) % 4), shifts, k) for k in (1, 3, 2)]

    with jax.named_scope("out_weights"):
        wide = wout.astype(F32)
        wout_z = z_swap(wide)
        wout_c = core_swap(wide)
    n1, q, k, v, low, logits, cum, mixed_lo, mixed_hi, st = run_mixer_forward(
        lengths, after(tokens, wide), g1r, wq, wk, wv, wgd_t, wgu, biasr)
    wout_z, wout_c, mixed_lo, mixed_hi = phase(wout_z, wout_c, mixed_lo, mixed_hi)

    with jax.named_scope("heads_one"):
        hi_z = z_swap(mixed_hi)
        hi_c = core_swap(mixed_hi)
        lo_c = core_swap(mixed_lo)
        wout_cz = core_swap(wout_z)
    wo, gh = run_before_feed((wout, wout_z, wout_c, wout_cz), cot, wd)
    hi_z, hi_c, lo_c, mixed_lo, wo, gh = phase(hi_z, hi_c, lo_c, mixed_lo, wo, gh)

    with jax.named_scope("heads_two"):
        lo_z = z_swap(mixed_lo)
        hi_cz = core_swap(hi_z)
    one = run_feed(at, 1, tokens, gh, (mixed_hi, hi_z, hi_c, hi_cz), wo, g2r, wg_t, wu_t, wd)
    lo_z, one = phase(lo_z, one)

    with jax.named_scope("second_norm_core"):
        part_in1 = core_swap(one[6])
        dn2_out1 = quarter(one[7], 0, 1 - z) + quarter(part_in1, 0, 1 - z)
    dn2_out1, part_in1, one, lo_z = phase(dn2_out1, part_in1, one, lo_z)

    with jax.named_scope("second_norm_z"):
        dn2_z1 = z_swap(dn2_out1)
        lo_cz = core_swap(lo_z)
    zero = run_feed(at, 0, tokens, gh, (mixed_lo, lo_z, lo_c, lo_cz), wo, g2r, wg_t, wu_t, wd)
    dn2_z1, zero = phase(dn2_z1, zero)

    with jax.named_scope("second_norm_core"):
        part_in0 = core_swap(zero[6])
        dn2_out0 = quarter(zero[7], 0, 1 - z) + quarter(part_in0, 0, 1 - z)
    dn2_out0, part_in0, one, zero = phase(dn2_out0, part_in0, one, zero)

    middle, n2, hid, gg, feed_out, feed_keep, _, part_keep = zip(zero, one)
    with jax.named_scope("second_norm_z"):
        dn2_z0 = z_swap(dn2_out0)
        feed_in = [core_swap(f) for f in feed_out]
    a = run_feed_grads(n2, gg, cot, hid)
    dn2_z0, feed_in, a = phase(dn2_z0, feed_in, a)

    gm0, gain2 = run_second_norm(at, part_keep, (part_in0, part_in1), (dn2_z0, dn2_z1), middle, g2r, cot)
    gm0, a, feed_in = phase(gm0, a, feed_in)
    with jax.named_scope("second_norm_join"):
        gm1 = z_swap(gm0)
        gm2 = core_swap(gm0)
    with jax.named_scope("feed_grads_x"):
        a = scatter_rows(a.reshape(1024, a.shape[-1]), GX)
    with jax.named_scope("feed_sum"):
        feed_z_out = jnp.concatenate([quarter(feed_keep[j], 0, 1 - z) + quarter(feed_in[j], 0, 1 - z) for j in range(2)], axis=0)
    gm1, gm2, feed_z_out = phase(gm1, gm2, feed_z_out)

    with jax.named_scope("second_norm_join"):
        gm3 = core_swap(gm1)
    gm3, gm1, feed_z_out = phase(gm3, gm1, feed_z_out)

    with jax.named_scope("feed_sum"):
        feed_z = z_swap(feed_z_out)
    gm = (gm0, gm1, gm2, gm3)
    dqkv, *part1_out, part1_keep, ga, small, gup, gbias = run_mixer_backward(
        at, lengths, gm, gain2, tokens, n1, q, k, v, low, logits, cum, st, wout, wq, wk, wv, wgd_t, wgu)
    with jax.named_scope("first_norm_core"):
        part1_in = [core_swap(p) for p in part1_out]
    c = run_mixer_grads(at, n1, dqkv, ga, (mixed_lo, mixed_hi), small, gup, gbias)
    feed_z, part1_in, part1_keep, c = phase(feed_z, part1_in, part1_keep, c)

    dn1_out = jnp.concatenate([quarter(part1_keep, j, 1 - z) + part1_in[j] for j in range(2)], axis=0)
    dn1_out, c = phase(dn1_out, c)
    with jax.named_scope("first_norm_z"):
        dn1_z = z_swap(dn1_out)
    with jax.named_scope("mixer_grads_first"):
        c_got = ring_first(c, YS)
    feed_own = jnp.concatenate([
        quarter(feed_keep[j], 0, z) + quarter(feed_in[j], 0, z) + feed_z[128 * j : 128 * (j + 1)]
        + rows_of(middle[j], 256 * core + 128 * z, 128) for j in range(2)], axis=0)
    with jax.named_scope("result_join"):
        feed1 = z_swap(feed_own)
    grad0 = run_first_norm(at, part1_keep, part1_in[2:], dn1_z, tokens, gm0, g1r)
    with jax.named_scope("mixer_grads_last"):
        c_last = ring_last(ring_on(c, c_got), YS)
        c = ring_total(c, c_got, c_last)
    feed1, grad0, c, feed_own, a = phase(feed1, grad0, c, feed_own, a)

    with jax.named_scope("grad_join"):
        grad1 = z_swap(grad0)
        grad2 = core_swap(grad0)
    with jax.named_scope("result_join"):
        feed2 = core_swap(feed_own)
    with jax.named_scope("feed_grads_y"):
        a = scatter_rows(a, GY).reshape(2, 32, -1)
    with jax.named_scope("mixer_grads_two"):
        x_pair, x_one = ix // 2, ix % 2
        c_far = lax.ppermute(jnp.concatenate([rows_of(c, 4 * (1 - x_pair), 4), c[8:9]], axis=0), "dp", XS[2])
    placed = run_place(at, 0, after((feed_own, grad0, feed2, grad2), c))
    with jax.named_scope("mixer_grads_two"):
        c = jnp.concatenate([rows_of(c, 4 * x_pair, 4), c[8:9]], axis=0) + c_far
        c = after(c, placed)
        c_near = lax.ppermute(jnp.concatenate([rows_of(c, 2 * (1 - x_one), 2), c[4:5]], axis=0), "dp", X_PAIR)
        c = jnp.concatenate([rows_of(c, 2 * x_one, 2), c[4:5]], axis=0) + c_near
    with jax.named_scope("rows"):
        turned_c = after(c, grad1)
        c = turned_c
        turned = lambda i: jnp.concatenate([pick(c, i, 0), c[2]], axis=1)
        own = turned(zh)
        got = lax.ppermute(turned(1 - zh), "dp", ZH)
        a_own = pick(a, zh, 0)
        a_got = lax.ppermute(after(pick(a, 1 - zh, 0), c), "dp", ZH)
    with jax.named_scope("result_join"):
        feed3 = core_swap(feed1)
    with jax.named_scope("grad_join"):
        grad3 = core_swap(after(grad1, c))
    result, grad_tokens = run_place(at, 1, (feed1, grad1, feed3, grad3), placed)
    with jax.named_scope("small_sums"):
        got = after(got, result)
        sums = own[:, 768:1536] + got[:, 768:1536]
        sums = sums + core_swap(sums)
        far = z_swap(sums)
        (gain_one, gate_down, gate_up, gate_bias, gain_two, d_query, d_key, d_value, d_out, d_gate, d_up, d_down) = unpack(
            own, got, a_own, a_got, sums, far)

    return (
        result,
        grad_tokens,
        gain_one.reshape(1024),
        d_query,
        d_key,
        d_value,
        gate_down.T,
        gate_up,
        gate_bias.reshape(128),
        d_out.T,
        gain_two.reshape(1024),
        d_gate,
        d_up,
        d_down.T,
    )


def solution(mesh):
    placed = (
        P("dp", None), P("dp", None), P(), P(None, "mp"), P(None, "mp"), P(None, "mp"), P(), P(None, "mp"),
        P("mp"), P("mp", None), P(), P(None, "mp"), P(None, "mp"), P("mp", None), P("dp", None),
    )
    outs = (
        P("dp", None), P("dp", None), P(), P("dp", "mp"), P("dp", "mp"), P("dp", "mp"), P(), P(None, "mp"),
        P("mp"), P("mp", "dp"), P(), P("dp", "mp"), P("dp", "mp"), P("mp", "dp"),
    )
    return jax.shard_map(local, mesh=mesh, in_specs=placed, out_specs=outs, check_vma=False)
```

```python
import functools

import jax
import jax.numpy as jnp
from jax import lax
from jax.experimental import pallas as pl
from jax.experimental.pallas import tpu as pltpu
from jax.sharding import PartitionSpec as P

BLK = 64
CH = 256
EPS = 1e-6
SCALE = 128 ** -0.5
F32 = jnp.float32
BF16 = jnp.bfloat16
VMEM_BYTES = 63_400_000
BACK_US = 16
FWD_ROWS = 256
BWD_ROWS = 256


def weight(us):
    return pl.CostEstimate(flops=int(us * 1.0e9), bytes_accessed=1024, transcendentals=0)


def nn(a, b, **kw):
    return lax.dot_general(a, b, (((1,), (0,)), ((), ())), preferred_element_type=F32, **kw)


def nt(a, b, **kw):
    return lax.dot_general(a, b, (((1,), (1,)), ((), ())), preferred_element_type=F32, **kw)


def tn(a, b, **kw):
    return lax.dot_general(a, b, (((0,), (0,)), ((), ())), preferred_element_type=F32, **kw)


HIGH = dict(precision=lax.Precision.HIGHEST)


CORE = [(0, 1), (1, 0), (2, 3), (3, 2)]
ZLO = [(0, 2), (2, 0), (1, 3), (3, 1)]


def dp_perm(dy, dz, dx):
    out = []
    for y in range(4):
        for z in range(2):
            for x in range(4):
                out.append(((y * 2 + z) * 4 + x, (((y + dy) % 4) * 2 + (z + dz) % 2) * 4 + (x + dx) % 4))
    return out


XS = {1: dp_perm(0, 0, 1), 3: dp_perm(0, 0, -1), 2: dp_perm(0, 0, 2)}
YS = {1: dp_perm(1, 0, 0), 3: dp_perm(-1, 0, 0), 2: dp_perm(2, 0, 0)}
ZH = dp_perm(0, 1, 0)
Y_PAIR = [((y * 2 + z) * 4 + x, ((y ^ 1) * 2 + z) * 4 + x) for y in range(4) for z in range(2) for x in range(4)]
X_PAIR = [((y * 2 + z) * 4 + x, (y * 2 + z) * 4 + (x ^ 1)) for y in range(4) for z in range(2) for x in range(4)]


def core_swap(v):
    return lax.ppermute(v, "mp", CORE)


def z_swap(v):
    return lax.ppermute(v, "mp", ZLO)


def rows_of(v, start, size):
    return lax.dynamic_slice_in_dim(v, start, size, 0)


def item_starts(len_ref):
    starts, total = [], jnp.int32(0)
    for j in range(8):
        starts.append(total)
        total = total + len_ref[0, j]
    return starts


def start_at(starts, place):
    best = jnp.int32(0)
    for s in starts[1:]:
        best = jnp.where(s <= place, jnp.maximum(best, s), best)
    return best


def chunk_masks(starts, base):
    row = lax.broadcasted_iota(jnp.int32, (CH, CH), 0)
    col = lax.broadcasted_iota(jnp.int32, (CH, CH), 1)
    blk = jnp.bitwise_and(row, -BLK)
    row1 = lax.broadcasted_iota(jnp.int32, (CH, 128), 0)
    place = row1 + base
    low = jnp.zeros_like(place)
    for s in starts[1:]:
        low = jnp.where(place >= s, jnp.maximum(low, s), low)
    low = low - base
    blk1 = jnp.bitwise_and(row1, -BLK)
    carried = low < blk1
    low_wide = jnp.concatenate([low, low], axis=1)
    causal = (col <= row) & (col >= blk)
    visible = causal & (col >= low_wide)
    return visible, carried


def causal_ones():
    row = lax.broadcasted_iota(jnp.int32, (CH, CH), 0)
    col = lax.broadcasted_iota(jnp.int32, (CH, CH), 1)
    return jnp.where((col <= row) & (col >= jnp.bitwise_and(row, -BLK)), 1.0, 0.0).astype(BF16)


def two_parts(v):
    high = v.astype(BF16)
    return high, (v - high.astype(F32)).astype(BF16)


def block_scalars(starts, base, b):
    first = base + b * BLK
    origin = start_at(starts, first + BLK - 1)
    keep = jnp.where(origin < first, 1.0, 0.0).astype(F32)
    place = lax.broadcasted_iota(jnp.int32, (BLK, 128), 0) + first
    return keep, place >= origin


def scaled_parts(q, k, cum):
    last = jnp.broadcast_to(cum.reshape(CH // BLK, BLK, 128)[:, BLK - 1 :, :], (CH // BLK, BLK, 128))
    last = last.reshape(CH, 128)
    e, en, ef = jnp.exp(cum), jnp.exp(-cum), jnp.exp(last - cum)
    qf = q.astype(F32) * SCALE * e
    ks = k.astype(F32) * en
    kf = k.astype(F32) * ef
    return last, e, en, ef, qf, ks, kf


def mixer_forward(
    len_ref, tok_ref, g1_ref, wq_ref, wk_ref, wv_ref, wgd_ref, wgu_ref, bias_ref,
    n_ref, q_ref, k_ref, v_ref, low_ref, logit_ref, cum_ref, mixed_lo_ref, mixed_hi_ref, st_ref, state,
):
    step = pl.program_id(0)
    rows = tok_ref.shape[0]
    starts = item_starts(len_ref)

    @pl.when(step == 0)
    def _():
        state[...] = jnp.zeros_like(state)

    ones = causal_ones()
    s = state[...]
    for c in range(rows // CH):
        base = step * rows + c * CH
        at = slice(c * CH, (c + 1) * CH)
        x = tok_ref[at, :].astype(F32)
        r = lax.rsqrt(jnp.mean(x * x, axis=-1, keepdims=True) + EPS)
        n = (x * r * g1_ref[...]).astype(BF16)
        n_ref[at, :] = n
        low = nt(n, wgd_ref[...]).astype(BF16)
        low_ref[at, :] = low
        logits = nn(low, wgu_ref[...]) + bias_ref[...]
        logit_ref[at, :] = logits
        decays = (jnp.minimum(logits, 0.0) - jnp.log1p(jnp.exp(-jnp.abs(logits)))) * (1.0 / 16.0)
        high, rest = two_parts(decays)
        cum = nn(ones, high) + nn(ones, rest)
        cum_ref[at, :] = cum
        q = nn(n, wq_ref[...]).astype(BF16)
        k = nn(n, wk_ref[...]).astype(BF16)
        v = nn(n, wv_ref[...]).astype(BF16)
        q_ref[at, :] = q
        k_ref[at, :] = k
        v_ref[at, :] = v
        visible, carried = chunk_masks(starts, base)
        last, e, en, ef, qf, ks, kf = scaled_parts(q, k, cum)
        scores = jnp.where(visible, nt(qf.astype(BF16), ks.astype(BF16)), 0.0).astype(BF16)
        out = nn(scores, v)
        q_carried = jnp.where(carried, qf, 0.0).astype(BF16)
        mixed_parts = []
        for b in range(CH // BLK):
            sl = slice(b * BLK, (b + 1) * BLK)
            keep, tail = block_scalars(starts, base, b)
            st_ref[c * (CH // BLK) + b] = s
            inter = nt(q_carried[sl], s.astype(BF16))
            mixed_parts.append((out[sl] + inter).astype(BF16).astype(F32))
            k_tail = jnp.where(tail, kf[sl], 0.0).astype(BF16)
            s = keep * jnp.exp(last[b * BLK : b * BLK + 1]) * s + tn(v[sl], k_tail)
        mixed = jnp.concatenate(mixed_parts, axis=0)

        @pl.when(step < 2)
        def _(mixed=mixed):
            mixed_lo_ref[...] = mixed

        @pl.when(step >= 2)
        def _(mixed=mixed):
            mixed_hi_ref[...] = mixed

    state[...] = s


def run_mixer_forward(lengths, tokens, g1, wq, wk, wv, wgd, wgu, bias):
    t = tokens.shape[0]
    whole = lambda a: pl.BlockSpec(a.shape, lambda i: (0,) * a.ndim)
    rows = lambda c: pl.BlockSpec((CH, c), lambda i: (i, 0))
    nb = CH // BLK
    outs = [
        ((t, 1024), BF16), ((t, 128), BF16), ((t, 128), BF16), ((t, 256), BF16), ((t, 16), BF16), ((t, 128), F32), ((t, 128), F32),
    ]
    sds = jax.ShapeDtypeStruct
    return pl.pallas_call(
        mixer_forward,
        grid=(t // CH,),
        in_specs=[pl.BlockSpec(memory_space=pltpu.SMEM), rows(1024), whole(g1), whole(wq), whole(wk), whole(wv),
                  whole(wgd), whole(wgu), whole(bias)],
        out_specs=[rows(s[1]) for s, _ in outs]
        + [pl.BlockSpec((CH, 256), lambda i: (jnp.minimum(i, 1), 0)), pl.BlockSpec((CH, 256), lambda i: (jnp.maximum(i - 2, 0), 0)),
           pl.BlockSpec((nb, 256, 128), lambda i: (i, 0, 0))],
        out_shape=[sds(s, d) for s, d in outs] + [sds((t // 2, 256), F32)] * 2 + [sds((t // BLK, 256, 128), F32)],
        scratch_shapes=[pltpu.VMEM((256, 128), F32)],
        compiler_params=pltpu.CompilerParams(vmem_limit_bytes=VMEM_BYTES),
        cost_estimate=weight(10),
        name="mixer_forward",
    )(lengths, tokens, g1, wq, wk, wv, wgd, wgu, bias)


def before_feed_kernel(w0_ref, w1_ref, w2_ref, w3_ref, cot_ref, wd_ref, wo_ref, gh_ref):
    for j, w_ref in enumerate((w0_ref, w1_ref, w2_ref, w3_ref)):

        @pl.when(pl.program_id(0) == j)
        def _(w_ref=w_ref):
            wo_ref[...] = w_ref[...].astype(BF16)

    gh_ref[...] = nt(cot_ref[...], wd_ref[...])


def run_before_feed(wo, cot, wd):
    t = cot.shape[0]
    whole = lambda a: pl.BlockSpec(a.shape, lambda s: (0,) * a.ndim)
    rows = lambda c: pl.BlockSpec((CH, c), lambda s: (s, 0))
    return pl.pallas_call(
        before_feed_kernel,
        grid=(t // CH,),
        in_specs=[whole(w) for w in wo] + [rows(1024), whole(wd)],
        out_specs=[rows(1024), rows(704)],
        out_shape=[jax.ShapeDtypeStruct((t, 1024), BF16), jax.ShapeDtypeStruct((t, 704), F32)],
        compiler_params=pltpu.CompilerParams(vmem_limit_bytes=VMEM_BYTES),
        cost_estimate=weight(7),
        name="before_feed",
    )(*wo, cot, wd)


def feed_kernel(
    at_ref, tok_ref, gh_ref, m0_ref, m1_ref, m2_ref, m3_ref, wo_ref, g2_ref, wg_ref, wu_ref, wd_ref,
    mid_ref, n_ref, hid_ref, gg_ref, feed_out_ref, feed_keep_ref, part_out_ref, part_keep_ref,
):
    step = pl.program_id(0)

    mixed = jnp.concatenate([m0_ref[...], m1_ref[...], m2_ref[...], m3_ref[...]], axis=1).astype(BF16)
    mid = tok_ref[...].astype(F32) + nn(mixed, wo_ref[...])
    mid_ref[...] = mid
    r = lax.rsqrt(jnp.mean(mid * mid, axis=-1, keepdims=True) + EPS)
    n = (mid * r * g2_ref[...]).astype(BF16)
    n_ref[...] = n
    pre = nt(n, wg_ref[...])
    up = nt(n, wu_ref[...])
    sg = jax.nn.sigmoid(pre)
    act = pre * sg
    hid = (act * up).astype(BF16)
    hid_ref[...] = hid
    gh = gh_ref[...]
    gg = (gh * up * sg * (1.0 + pre * (1.0 - sg))).astype(BF16)
    gu = (gh * act).astype(BF16)
    gg_ref[:, 0:704] = gg
    gg_ref[:, 704:1408] = gu
    feed = nn(hid, wd_ref[...])
    part = nn(gg, wg_ref[...]) + nn(gu, wu_ref[...])

    @pl.when(step == 0)
    def _():
        feed_out_ref[...] = feed
        part_out_ref[...] = part

    @pl.when(step == 1)
    def _():
        feed_keep_ref[...] = feed
        part_keep_ref[...] = part


def run_feed(at, chunk, tokens, gh, mixed, wo, g2, wg, wu, wd):
    t = tokens.shape[0] // 2
    whole = lambda a: pl.BlockSpec(a.shape, lambda s, at: (0,) * a.ndim)
    half = lambda s, at: jnp.bitwise_xor(1 - at[2], s)
    rows = lambda c: pl.BlockSpec((CH, c), lambda s, at: (half(s, at), 0))
    from_all = lambda c: pl.BlockSpec((CH, c), lambda s, at: (2 * chunk + half(s, at), 0))
    once = pl.BlockSpec((CH, 1024), lambda s, at: (0, 0))
    sds = jax.ShapeDtypeStruct
    return pl.pallas_call(
        feed_kernel,
        grid_spec=pltpu.PrefetchScalarGridSpec(
            num_scalar_prefetch=1,
            grid=(t // CH,),
            in_specs=[from_all(1024), from_all(704)] + [rows(256)] * 4 + [whole(wo), whole(g2), whole(wg), whole(wu), whole(wd)],
            out_specs=[rows(1024), rows(1024), rows(704), rows(1408), once, once, once, once],
        ),
        out_shape=[sds((t, 1024), F32), sds((t, 1024), BF16), sds((t, 704), BF16), sds((t, 1408), BF16)] + [sds((CH, 1024), F32)] * 4,
        compiler_params=pltpu.CompilerParams(vmem_limit_bytes=VMEM_BYTES),
        cost_estimate=weight(14),
        name="feed_both_ways",
    )(at, tokens, gh, *mixed, wo, g2, wg, wu, wd)


def mixer_backward(
    at_ref, len_ref, *refs,
):
    gm_refs, gain_ref, refs = refs[:4], refs[4], refs[5:]
    (tok_ref, n_ref, q_ref, k_ref, v_ref, low_ref, logit_ref, cum_ref,
     st_ref, wo_ref, wq_ref, wk_ref, wv_ref, wgd_ref, wgu_ref,
     dqkv_ref, far0_ref, far1_ref, near0_ref, near1_ref, part_keep_ref, ga_ref, small_ref, gup_ref, bias_ref, dstate, whole) = refs
    step = pl.program_id(0)
    steps = pl.num_programs(0)
    rows = tok_ref.shape[0]
    starts = item_starts(len_ref)

    core, z = at_ref[2], at_ref[3]
    here = steps - 1 - step
    mine = jnp.equal(lax.rem(here, 2), core)

    @pl.when(step == 0)
    def _():
        dstate[...] = jnp.zeros_like(dstate)
        small_ref[...] = jnp.zeros_like(small_ref)
        small_ref[17:18, :] = gain_ref[0:1, :]
        gup_ref[...] = jnp.zeros_like(gup_ref)
        bias_ref[...] = jnp.zeros_like(bias_ref)

    first = pl.multiple_of(z * 128, 128)
    second = pl.multiple_of((1 - z) * 128, 128)
    for other in range(2):

        @pl.when(jnp.logical_not(mine) if other else mine)
        def _(other=other):
            ga_ref[pl.ds(first, 128), :] = gm_refs[2 * other][...].astype(BF16)
            ga_ref[pl.ds(second, 128), :] = gm_refs[2 * other + 1][...].astype(BF16)

    ones = causal_ones()
    ds = dstate[...]
    for c in reversed(range(rows // CH)):
        base = here * rows + c * CH
        at = slice(c * CH, (c + 1) * CH)
        g = nt(ga_ref[at, :], wo_ref[...]).astype(BF16)
        q, k, v, cum = q_ref[at, :], k_ref[at, :], v_ref[at, :], cum_ref[at, :]
        visible, carried = chunk_masks(starts, base)
        last, e, en, ef, qf, ksf, kff = scaled_parts(q, k, cum)
        qs, ks = qf.astype(BF16), ksf.astype(BF16)
        scores = jnp.where(visible, nt(qs, ks), 0.0).astype(BF16)
        dscores = jnp.where(visible, nt(g, v), 0.0).astype(BF16)
        dv = tn(scores, g)
        dqs = nn(dscores, ks)
        dks = tn(dscores, qs)
        q_carried = jnp.where(carried, qf, 0.0).astype(BF16)
        dvs, dkfs, dqss, dls = [], [], [], []
        for b in reversed(range(CH // BLK)):
            sl = slice(b * BLK, (b + 1) * BLK)
            keep, tail = block_scalars(starts, base, b)
            dsb = ds.astype(BF16)
            s = st_ref[c * (CH // BLK) + b]
            k_tail = jnp.where(tail, kff[sl], 0.0).astype(BF16)
            dvs.append(dv[sl] + nt(k_tail, dsb))
            dkf = jnp.where(tail, nn(v[sl], dsb), 0.0)
            dkfs.append(dkf)
            dqss.append(dqs[sl] + jnp.where(carried[sl], nn(g[sl], s.astype(BF16)), 0.0))
            grow = keep * jnp.exp(last[b * BLK : b * BLK + 1])
            dlast = grow * jnp.sum(s * ds, axis=0, keepdims=True) + jnp.sum(dkf * kff[sl], axis=0, keepdims=True)
            dls.append(jnp.broadcast_to(dlast, (BLK, 128)))
            ds = grow * ds + tn(g[sl], q_carried[sl])
        join = lambda parts: jnp.concatenate(parts[::-1], axis=0)
        dqs, dkf, dl = join(dqss), join(dkfs), join(dls)
        dq = (dqs * (SCALE * e)).astype(BF16)
        dk = (dks * en + dkf * ef).astype(BF16)
        dv = join(dvs).astype(BF16)
        dqkv_ref[at, 0:128] = dq
        dqkv_ref[at, 128:256] = dk
        dqkv_ref[at, 256:512] = dv
        high, rest = two_parts(dqs * qf - dks * ksf - dkf * kff)
        ddec = tn(ones, high) + tn(ones, rest) + dl
        glog = ddec * jax.nn.sigmoid(-logit_ref[at, :]) * (1.0 / 16.0)
        bias_ref[0:1, :] += jnp.sum(glog, axis=0, keepdims=True)
        high, rest = two_parts(glog)
        gup_ref[...] += tn(low_ref[at, :], high) + tn(low_ref[at, :], rest)
        glr = (nt(high, wgu_ref[...]) + nt(rest, wgu_ref[...])).astype(BF16)
        part = nt(dq, wq_ref[...]) + nt(dk, wk_ref[...]) + nt(dv, wv_ref[...]) + nn(glr, wgd_ref[...])
        @pl.when(mine)
        def _(part=part):
            part_keep_ref[...] = part

        for chunk, (far_ref, near_ref) in enumerate(((far0_ref, near0_ref), (far1_ref, near1_ref))):

            @pl.when(jnp.logical_and(jnp.logical_not(mine), jnp.equal(lax.div(here, 2), chunk)))
            def _(part=part, far_ref=far_ref, near_ref=near_ref):
                whole[...] = part
                far_ref[...] = whole[pl.ds(second, 128), :]
                near_ref[...] = whole[pl.ds(first, 128), :]

        small_ref[0:16, :] += tn(glr, n_ref[at, :])
        x = tok_ref[at, :].astype(F32)
        r = lax.rsqrt(jnp.mean(x * x, axis=-1, keepdims=True) + EPS)
        small_ref[16:17, :] += jnp.sum(part * x * r, axis=0, keepdims=True)
    dstate[...] = ds


def run_mixer_backward(at, lengths, gm, gain, tokens, n, q, k, v, low, logits, cum, st, wo, wq, wk, wv, wgd, wgu):
    t = tokens.shape[0]
    steps = t // CH
    whole = lambda a: pl.BlockSpec(a.shape, lambda i, at: (0,) * a.ndim)
    rows = lambda c: pl.BlockSpec((CH, c), lambda i, at: (steps - 1 - i, 0))
    split = pl.BlockSpec((CH, 1024), lambda i, at: (lax.div(steps - 1 - i, 2), 0))
    nb = CH // BLK
    fixed = lambda s: pl.BlockSpec(s, lambda i, at: (0, 0))
    sds = jax.ShapeDtypeStruct
    return pl.pallas_call(
        mixer_backward,
        grid_spec=pltpu.PrefetchScalarGridSpec(
            num_scalar_prefetch=1,
            grid=(steps,),
            in_specs=[pl.BlockSpec(memory_space=pltpu.SMEM)] + [pl.BlockSpec((128, 1024), lambda i, at: (lax.div(steps - 1 - i, 2), 0))] * 4 + [whole(gain)]
            + [rows(1024), rows(1024), rows(128), rows(128), rows(256), rows(16), rows(128), rows(128),
               pl.BlockSpec((nb, 256, 128), lambda i, at: (steps - 1 - i, 0, 0)),
               whole(wo), whole(wq), whole(wk), whole(wv), whole(wgd), whole(wgu)],
            out_specs=[rows(512)] + [fixed((128, 1024))] * 4 + [split, rows(1024), fixed((24, 1024)), fixed((16, 128)), fixed((8, 128))],
            scratch_shapes=[pltpu.VMEM((256, 128), F32), pltpu.VMEM((CH, 1024), F32)],
        ),
        out_shape=[sds((t, 512), BF16)] + [sds((128, 1024), F32)] * 4 + [sds((t // 2, 1024), F32), sds((t, 1024), BF16),
                   sds((24, 1024), F32), sds((16, 128), F32), sds((8, 128), F32)],
        compiler_params=pltpu.CompilerParams(vmem_limit_bytes=VMEM_BYTES),
        cost_estimate=weight(BACK_US),
        name="mixer_backward",
    )(at, lengths, *gm, gain, tokens, n, q, k, v, low, logits, cum, st, wo, wq, wk, wv, wgd, wgu)


SMALL = dict(
    compiler_params=pltpu.CompilerParams(vmem_limit_bytes=VMEM_BYTES),
    cost_estimate=weight(3),
)


def quarter(v, j, which):
    return rows_of(v, 256 * j + 128 * which, 128)


def norm_gradient(dn, y, gain):
    r = lax.rsqrt(jnp.mean(y * y, axis=-1, keepdims=True) + EPS)
    gd = dn * gain
    dy = r * gd - (r * r * r) * y * jnp.mean(gd * y, axis=-1, keepdims=True)
    return dy, jnp.sum(dn * y * r, axis=0, keepdims=True)


def second_norm_kernel(at_ref, a0_ref, b0_ref, c0_ref, y0_ref, a1_ref, b1_ref, c1_ref, y1_ref, gain_ref, base0_ref, base1_ref, o_ref, s_ref):
    halves = ((a0_ref, b0_ref, c0_ref, y0_ref, base0_ref), (a1_ref, b1_ref, c1_ref, y1_ref, base1_ref))
    total = jnp.zeros((1, 1024), F32)
    for j, (a_ref, b_ref, c_ref, y_ref, base_ref) in enumerate(halves):
        dy, dgain = norm_gradient(a_ref[...] + b_ref[...] + c_ref[...], y_ref[...], gain_ref[...])
        o_ref[128 * j : 128 * (j + 1)] = base_ref[...].astype(F32) + dy
        total = total + dgain
    s_ref[0:1, :] = total


def run_second_norm(at, keep, got, far, middle, gain, cot):
    of_half = pl.BlockSpec((128, 1024), lambda s, at: (at[3], 0))
    of_chunk = pl.BlockSpec((128, 1024), lambda s, at: (2 * at[2] + at[3], 0))
    of_all = lambda j: pl.BlockSpec((128, 1024), lambda s, at: (4 * j + 2 * at[2] + at[3], 0))
    fixed = lambda *s: pl.BlockSpec(s, lambda s, at: (0, 0))
    ops = [v for j in range(2) for v in (keep[j], got[j], far[j], middle[j])]
    return pl.pallas_call(
        second_norm_kernel,
        grid_spec=pltpu.PrefetchScalarGridSpec(
            num_scalar_prefetch=1, grid=(1,),
            in_specs=[of_half, of_half, fixed(128, 1024), of_chunk] * 2 + [fixed(1, 1024), of_all(0), of_all(1)],
            out_specs=[fixed(256, 1024), fixed(8, 1024)]),
        out_shape=[jax.ShapeDtypeStruct((256, 1024), F32), jax.ShapeDtypeStruct((8, 1024), F32)],
        name="second_norm_back",
        **SMALL,
    )(at, *ops, gain, cot, cot)


def first_norm_kernel(at_ref, a_ref, b0_ref, b1_ref, c_ref, y_ref, base_ref, gain_ref, own_ref):
    for j, b_ref in enumerate((b0_ref, b1_ref)):

        @pl.when(pl.program_id(0) == j)
        def _(b_ref=b_ref):
            dy, _ = norm_gradient(a_ref[...] + b_ref[...] + c_ref[...], y_ref[...].astype(F32), gain_ref[...])
            own_ref[...] = dy + base_ref[...]


def run_first_norm(at, keep, got, far, tokens, base, gain):
    of_half = pl.BlockSpec((128, 1024), lambda s, at: (2 * s + at[3], 0))
    of_all = pl.BlockSpec((128, 1024), lambda s, at: (4 * s + 2 * at[2] + at[3], 0))
    own = pl.BlockSpec((128, 1024), lambda s, at: (s, 0))
    fixed = lambda *n: pl.BlockSpec(n, lambda s, at: (0, 0))
    return pl.pallas_call(
        first_norm_kernel,
        grid_spec=pltpu.PrefetchScalarGridSpec(
            num_scalar_prefetch=1, grid=(2,),
            in_specs=[of_half, fixed(128, 1024), fixed(128, 1024), own, of_all, own, fixed(1, 1024)], out_specs=own),
        out_shape=jax.ShapeDtypeStruct((256, 1024), F32),
        name="first_norm_back",
        **SMALL,
    )(at, keep, *got, far, tokens, base, gain)


def place_kernel(at_ref, r0_ref, g0_ref, r1_ref, g1_ref, *rest):
    result_ref, grad_ref = rest[-2:]

    @pl.when(lax.rem(pl.program_id(0), 2) == 0)
    def _():
        result_ref[...] = r0_ref[...].astype(BF16)
        grad_ref[...] = g0_ref[...]

    @pl.when(lax.rem(pl.program_id(0), 2) == 1)
    def _():
        result_ref[...] = r1_ref[...].astype(BF16)
        grad_ref[...] = g1_ref[...]


def run_place(at, odd, pieces, into=()):
    chunk = lambda s: lax.div(s, 2)
    place = lambda s, at: jnp.bitwise_xor(2 * at[2] + at[3], 2 * lax.rem(s, 2) + odd)
    piece = pl.BlockSpec((128, 1024), lambda s, at: (chunk(s), 0))
    placed = pl.BlockSpec((128, 1024), lambda s, at: (4 * chunk(s) + place(s, at), 0))
    return pl.pallas_call(
        place_kernel,
        grid_spec=pltpu.PrefetchScalarGridSpec(
            num_scalar_prefetch=1, grid=(4,),
            in_specs=[piece] * 4 + [pl.BlockSpec(memory_space=pl.ANY)] * len(into),
            out_specs=[placed, placed]),
        out_shape=[jax.ShapeDtypeStruct((1024, 1024), BF16), jax.ShapeDtypeStruct((1024, 1024), F32)],
        input_output_aliases={5: 0, 6: 1} if into else {},
        name="place_rows",
        **SMALL,
    )(at, *pieces, *into)


def feed_grads_kernel(l0_ref, l1_ref, r0_ref, r1_ref, c0_ref, c1_ref, h0_ref, h1_ref, out):
    w1, w2 = r0_ref.shape[1], h0_ref.shape[1]
    first = tn(l0_ref[...], r0_ref[...]) + tn(l1_ref[...], r1_ref[...])
    second = tn(c0_ref[...], h0_ref[...]) + tn(c1_ref[...], h1_ref[...])
    for x in range(4):
        for zh in range(2):
            row = zh * 128 + x * 32
            out[x, 0, zh, :, 0:w1] = first[row : row + 32]
            out[x, 0, zh, :, w1 : w1 + w2] = second[row : row + 32]
            out[x, 0, zh, :, w1 + w2 :] = jnp.zeros((32, out.shape[-1] - w1 - w2), F32)


def run_feed_grads(n2, gg, cot, hid):
    t = cot.shape[0] // 2
    c = gg[0].shape[1] + hid[0].shape[1]
    wide = -(-c // 128) * 128
    cols = lambda j: pl.BlockSpec((t, CH), lambda s: (j, s))
    whole = lambda a: pl.BlockSpec(a.shape, lambda s: (0, 0))
    return pl.pallas_call(
        feed_grads_kernel,
        grid=(4,),
        in_specs=[cols(0), cols(0), whole(gg[0]), whole(gg[1]), cols(0), cols(1), whole(hid[0]), whole(hid[1])],
        out_specs=pl.BlockSpec((4, 1, 2, 32, wide), lambda s: (0, s, 0, 0, 0)),
        out_shape=jax.ShapeDtypeStruct((4, 4, 2, 32, wide), F32),
        compiler_params=pltpu.CompilerParams(vmem_limit_bytes=VMEM_BYTES),
        cost_estimate=weight(12),
        name="feed_weight_grads",
    )(n2[0], n2[1], gg[0], gg[1], cot, cot, hid[0], hid[1])


RING_OUTS = ((0, None, 0), (2, 0, 1), (1, 1, 1), (3, 0, 2), (2, 1, 2), (1, 0, 3), (3, 1, 4))


def mixer_grads_kernel(at_ref, l_ref, r0_ref, a0_ref, m0_ref, m1_ref, small_ref, gup_ref, bias_ref, *outs):
    step = pl.program_id(0)
    w1 = r0_ref.shape[1]

    @pl.when(step < 4)
    def _():
        n = m0_ref.shape[0]
        first = tn(l_ref[...], r0_ref[...])
        second = tn(a0_ref[0:n], m0_ref[...].astype(BF16)) + tn(a0_ref[n:], m1_ref[...].astype(BF16))

        def write(ref, x, to):
            for zh in range(2):
                row = zh * 128 + x * 32
                ref[2 * to + zh, :, 0:w1] = first[row : row + 32]
                ref[2 * to + zh, :, w1:] = second[row : row + 32]

        offset = lax.rem(step - at_ref[1] + 4, 4)

        for k, late, ref in RING_OUTS:

            @pl.when(offset == k)
            def _(late=late, ref=ref):
                for x in range(4):
                    if late is None or late == x // 2:
                        write(outs[ref], x, x if ref < 3 else x % 2)

    @pl.when(step == 4)
    def _():
        small = small_ref[...]
        for out in (outs[0], outs[1], outs[2], outs[4]):
            last = out.shape[0] - 1
            out[last] = jnp.zeros(out.shape[1:], F32)
            out[last, 0:16, :] = small[0:16, 0:768]
            for j in range(3):
                n = min(6, 16 - 6 * j)
                out[last, 16 : 16 + n, 256 * j : 256 * (j + 1)] = small[6 * j : 6 * j + n, 768:1024]
            for j in range(6):
                n = min(3, 16 - 3 * j)
                out[last, 22 : 22 + n, 128 * j : 128 * (j + 1)] = gup_ref[3 * j : 3 * j + n, :]
            out[last, 25:26, :] = small[16:17, 0:768]
            out[last, 26:27, :] = small[17:18, 0:768]
            out[last, 27:28, 0:256] = small[16:17, 768:1024]
            out[last, 27:28, 256:512] = small[17:18, 768:1024]
            out[last, 27:28, 512:640] = bias_ref[0:1, :]


def run_mixer_grads(at, n1, dqkv, ga, mixed, small, gup, bias):
    t, c = n1.shape[0], dqkv.shape[1] + mixed[0].shape[1]
    cols = pl.BlockSpec((t, CH), lambda s, at: (0, jnp.minimum(s, 3)))
    whole = lambda a: pl.BlockSpec(a.shape, lambda s, at: (0, 0))
    rest = [small, gup, bias]
    counts = [9, 9, 9, 4, 5]
    return pl.pallas_call(
        mixer_grads_kernel,
        grid_spec=pltpu.PrefetchScalarGridSpec(
            num_scalar_prefetch=1, grid=(5,),
            in_specs=[cols, whole(dqkv), cols, whole(mixed[0]), whole(mixed[1])] + [whole(a) for a in rest],
            out_specs=[pl.BlockSpec((n, 32, c), lambda s, at: (0, 0, 0)) for n in counts]),
        out_shape=[jax.ShapeDtypeStruct((n, 32, c), F32) for n in counts],
        compiler_params=pltpu.CompilerParams(vmem_limit_bytes=VMEM_BYTES),
        cost_estimate=weight(8),
        name="mixer_weight_grads",
    )(at, n1, dqkv, ga, mixed[0], mixed[1], *rest)


def unpack_kernel(
    own_ref, got_ref, a_ref, b_ref, sums_ref, far_ref,
    g1_ref, down_ref, up_ref, bias_ref, g2_ref, q_ref, k_ref, v_ref, o_ref, gate_ref, mup_ref, mdown_ref,
):
    rows = own_ref[...] + got_ref[...]
    feed = a_ref[...] + b_ref[...]
    own = rows[:, 768:1536]
    sums = sums_ref[...] + far_ref[...]
    wide = jnp.concatenate([sums[16:22, 0:256], sums[16:22, 256:512], sums[16:20, 512:768]], axis=0)
    down_ref[...] = jnp.concatenate([sums[0:16], wide], axis=1)
    for j in range(6):
        n = min(3, 16 - 3 * j)
        up_ref[3 * j : 3 * j + n, :] = own[22 : 22 + n, 128 * j : 128 * (j + 1)]
    g1_ref[:, 0:768] = sums[25:26]
    g1_ref[:, 768:1024] = sums[27:28, 0:256]
    g2_ref[:, 0:768] = sums[26:27]
    g2_ref[:, 768:1024] = sums[27:28, 256:512]
    bias_ref[...] = own[27:28, 512:640]
    q_ref[...] = rows[:, 0:128]
    k_ref[...] = rows[:, 128:256]
    v_ref[...] = rows[:, 256:512]
    o_ref[...] = rows[:, 512:768]
    gate_ref[...] = feed[:, 0:704]
    mup_ref[...] = feed[:, 704:1408]
    mdown_ref[...] = feed[:, 1408:2112]


def unpack(own, got, feed_own, feed_got, sums, far):
    shapes = [(1, 1024), (16, 1024), (16, 128), (1, 128), (1, 1024), (32, 128), (32, 128), (32, 256), (32, 256)] + [(32, 704)] * 3
    return pl.pallas_call(
        unpack_kernel, out_shape=[jax.ShapeDtypeStruct(s, F32) for s in shapes], name="unpack", **SMALL,
    )(own, got, feed_own, feed_got, sums, far)


def after(value, *others):
    return lax.optimization_barrier((value, others))[0]


def send(v, shifts, d):
    return lax.ppermute(v, "dp", shifts[d])


GX = [[(y * 2 + z) * 4 + x for x in range(4)] for y in range(4) for z in range(2)]
GY = [[(y * 2 + z) * 4 + x for y in range(4)] for x in range(4) for z in range(2)]


def scatter_rows(v, groups):
    return lax.psum_scatter(v, "dp", scatter_dimension=0, tiled=True, axis_index_groups=groups)


def ring_first(v, shifts):
    return lax.ppermute(v[1], "dp", shifts[1]), lax.ppermute(v[2], "dp", shifts[3])


def ring_on(v, got):
    n = v[3].shape[0]
    return v[3] + got[0][:n], v[4] + got[1][n:]


def ring_last(on, shifts):
    return lax.ppermute(on[0], "dp", shifts[1]), lax.ppermute(on[1], "dp", shifts[3])


def ring_total(v, got, last):
    n = last[0].shape[0]
    return jnp.concatenate([v[0][:n] + last[0] + got[1][:n], v[0][n:] + got[0][n:] + last[1]], axis=0)


def pick(v, i, dim):
    return lax.dynamic_index_in_dim(v, i, dim, False)


def swap_zh(v, zh, dim):
    return pick(v, zh, dim) + lax.ppermute(pick(v, 1 - zh, dim), "dp", ZH)


def local(tokens, lengths, g1, wq, wk, wv, wgd, wgu, bias, wout, g2, wg, wu, wd, cot):
    mp, dp = lax.axis_index("mp"), lax.axis_index("dp")
    core, z = mp % 2, mp // 2
    ix, zh, iy = dp % 4, (dp // 4) % 2, dp // 8
    at = jnp.stack([ix, iy, core, z]).astype(jnp.int32)
    g1r, g2r, biasr = g1.reshape(1, -1), g2.reshape(1, -1), bias.reshape(1, -1)
    wgd_t, wg_t, wu_t = wgd.T, wg.T, wu.T

    def phase(*values):
        return lax.optimization_barrier(values)

    def across(v, at_here, shifts, take):
        return [take(v, at_here)] + [send(take(v, (at_here + k) % 4), shifts, k) for k in (1, 3, 2)]

    with jax.named_scope("out_weights"):
        wide = wout.astype(F32)
        wout_z = z_swap(wide)
        wout_c = core_swap(wide)
    n1, q, k, v, low, logits, cum, mixed_lo, mixed_hi, st = run_mixer_forward(
        lengths, after(tokens, wide), g1r, wq, wk, wv, wgd_t, wgu, biasr)
    wout_z, wout_c, mixed_lo, mixed_hi = phase(wout_z, wout_c, mixed_lo, mixed_hi)

    with jax.named_scope("heads_one"):
        hi_z = z_swap(mixed_hi)
        hi_c = core_swap(mixed_hi)
        lo_c = core_swap(mixed_lo)
        wout_cz = core_swap(wout_z)
    wo, gh = run_before_feed((wout, wout_z, wout_c, wout_cz), cot, wd)
    hi_z, hi_c, lo_c, mixed_lo, wo, gh = phase(hi_z, hi_c, lo_c, mixed_lo, wo, gh)

    with jax.named_scope("heads_two"):
        lo_z = z_swap(mixed_lo)
        hi_cz = core_swap(hi_z)
    one = run_feed(at, 1, tokens, gh, (mixed_hi, hi_z, hi_c, hi_cz), wo, g2r, wg_t, wu_t, wd)
    lo_z, one = phase(lo_z, one)

    with jax.named_scope("second_norm_core"):
        part_in1 = core_swap(one[6])
        dn2_out1 = quarter(one[7], 0, 1 - z) + quarter(part_in1, 0, 1 - z)
    dn2_out1, part_in1, one, lo_z = phase(dn2_out1, part_in1, one, lo_z)

    with jax.named_scope("second_norm_z"):
        dn2_z1 = z_swap(dn2_out1)
        lo_cz = core_swap(lo_z)
    zero = run_feed(at, 0, tokens, gh, (mixed_lo, lo_z, lo_c, lo_cz), wo, g2r, wg_t, wu_t, wd)
    dn2_z1, zero = phase(dn2_z1, zero)

    with jax.named_scope("second_norm_core"):
        part_in0 = core_swap(zero[6])
        dn2_out0 = quarter(zero[7], 0, 1 - z) + quarter(part_in0, 0, 1 - z)
    dn2_out0, part_in0, one, zero = phase(dn2_out0, part_in0, one, zero)

    middle, n2, hid, gg, feed_out, feed_keep, _, part_keep = zip(zero, one)
    with jax.named_scope("second_norm_z"):
        dn2_z0 = z_swap(dn2_out0)
        feed_in = [core_swap(f) for f in feed_out]
    a = run_feed_grads(n2, gg, cot, hid)
    dn2_z0, feed_in, a = phase(dn2_z0, feed_in, a)

    gm0, gain2 = run_second_norm(at, part_keep, (part_in0, part_in1), (dn2_z0, dn2_z1), middle, g2r, cot)
    gm0, a, feed_in = phase(gm0, a, feed_in)
    with jax.named_scope("second_norm_join"):
        gm1 = z_swap(gm0)
        gm2 = core_swap(gm0)
    with jax.named_scope("feed_grads_x"):
        a = scatter_rows(a.reshape(1024, a.shape[-1]), GX)
    with jax.named_scope("feed_sum"):
        feed_z_out = jnp.concatenate([quarter(feed_keep[j], 0, 1 - z) + quarter(feed_in[j], 0, 1 - z) for j in range(2)], axis=0)
    gm1, gm2, feed_z_out = phase(gm1, gm2, feed_z_out)

    with jax.named_scope("second_norm_join"):
        gm3 = core_swap(gm1)
    gm3, gm1, feed_z_out = phase(gm3, gm1, feed_z_out)

    with jax.named_scope("feed_sum"):
        feed_z = z_swap(feed_z_out)
    gm = (gm0, gm1, gm2, gm3)
    dqkv, *part1_out, part1_keep, ga, small, gup, gbias = run_mixer_backward(
        at, lengths, gm, gain2, tokens, n1, q, k, v, low, logits, cum, st, wout, wq, wk, wv, wgd_t, wgu)
    with jax.named_scope("first_norm_core"):
        part1_in = [core_swap(p) for p in part1_out]
    c = run_mixer_grads(at, n1, dqkv, ga, (mixed_lo, mixed_hi), small, gup, gbias)
    feed_z, part1_in, part1_keep, c = phase(feed_z, part1_in, part1_keep, c)

    dn1_out = jnp.concatenate([quarter(part1_keep, j, 1 - z) + part1_in[j] for j in range(2)], axis=0)
    dn1_out, c = phase(dn1_out, c)
    with jax.named_scope("first_norm_z"):
        dn1_z = z_swap(dn1_out)
    with jax.named_scope("mixer_grads_first"):
        c_got = ring_first(c, YS)
    feed_own = jnp.concatenate([
        quarter(feed_keep[j], 0, z) + quarter(feed_in[j], 0, z) + feed_z[128 * j : 128 * (j + 1)]
        + rows_of(middle[j], 256 * core + 128 * z, 128) for j in range(2)], axis=0)
    with jax.named_scope("result_join"):
        feed1 = z_swap(feed_own)
    grad0 = run_first_norm(at, part1_keep, part1_in[2:], dn1_z, tokens, gm0, g1r)
    with jax.named_scope("mixer_grads_last"):
        c_last = ring_last(ring_on(c, c_got), YS)
        c = ring_total(c, c_got, c_last)
    with jax.named_scope("grad_join"):
        grad2 = core_swap(grad0)
    with jax.named_scope("result_join"):
        feed2 = core_swap(feed_own)
    feed1, feed2, grad0, grad2, c, feed_own, a = phase(feed1, feed2, grad0, grad2, c, feed_own, a)

    with jax.named_scope("grad_join"):
        grad1 = z_swap(grad0)
    with jax.named_scope("feed_grads_y"):
        a = scatter_rows(a, GY).reshape(2, 32, -1)
    with jax.named_scope("mixer_grads_two"):

        def with_small(i):
            return jnp.concatenate([rows_of(c, 2 * (i % 4), 2), c[8:9]], axis=0)

        c_second = [with_small(ix)] + [send(with_small(ix + k), XS, k) for k in (1, 3, 2)]
    placed = run_place(at, 0, (feed_own, grad0, feed2, grad2))
    with jax.named_scope("mixer_grads_two"):
        c = sum(after(c_second, placed))
    with jax.named_scope("rows"):
        c = after(c, (grad1, placed))
        turned = lambda i: jnp.concatenate([pick(c, i, 0), c[2]], axis=1)
        own = turned(zh)
        got = lax.ppermute(turned(1 - zh), "dp", ZH)
        a_own = pick(a, zh, 0)
        a_out = after(pick(a, 1 - zh, 0), c)
        a_got = lax.ppermute(a_out, "dp", ZH)
    with jax.named_scope("result_join"):
        feed3 = core_swap(feed1)
    with jax.named_scope("grad_join"):
        grad3 = core_swap(after(grad1, c))
    result, grad_tokens = run_place(at, 1, after((feed1, grad1, feed3, grad3), a_out), placed)
    with jax.named_scope("small_sums"):
        got = after(got, (result, a_got))
        sums = own[:, 768:1536] + got[:, 768:1536]
        sums = sums + core_swap(sums)
        far = z_swap(sums)
        (gain_one, gate_down, gate_up, gate_bias, gain_two, d_query, d_key, d_value, d_out, d_gate, d_up, d_down) = unpack(
            own, got, a_own, a_got, sums, far)

    return (
        result,
        grad_tokens,
        gain_one.reshape(1024),
        d_query,
        d_key,
        d_value,
        gate_down.T,
        gate_up,
        gate_bias.reshape(128),
        d_out.T,
        gain_two.reshape(1024),
        d_gate,
        d_up,
        d_down.T,
    )


def solution(mesh):
    placed = (
        P("dp", None), P("dp", None), P(), P(None, "mp"), P(None, "mp"), P(None, "mp"), P(), P(None, "mp"),
        P("mp"), P("mp", None), P(), P(None, "mp"), P(None, "mp"), P("mp", None), P("dp", None),
    )
    outs = (
        P("dp", None), P("dp", None), P(), P("dp", "mp"), P("dp", "mp"), P("dp", "mp"), P(), P(None, "mp"),
        P("mp"), P("mp", "dp"), P(), P("dp", "mp"), P("dp", "mp"), P("mp", "dp"),
    )
    return jax.shard_map(local, mesh=mesh, in_specs=placed, out_specs=outs, check_vma=False)
```

```python
import functools

import jax
import jax.numpy as jnp
from jax import lax
from jax.experimental import pallas as pl
from jax.experimental.pallas import tpu as pltpu
from jax.sharding import PartitionSpec as P

BLK = 64
CH = 256
EPS = 1e-6
SCALE = 128 ** -0.5
F32 = jnp.float32
BF16 = jnp.bfloat16
VMEM_BYTES = 63_400_000
BACK_US = 16
FWD_ROWS = 256
BWD_ROWS = 256


def weight(us):
    return pl.CostEstimate(flops=int(us * 1.0e9), bytes_accessed=1024, transcendentals=0)


def nn(a, b, **kw):
    return lax.dot_general(a, b, (((1,), (0,)), ((), ())), preferred_element_type=F32, **kw)


def nt(a, b, **kw):
    return lax.dot_general(a, b, (((1,), (1,)), ((), ())), preferred_element_type=F32, **kw)


def tn(a, b, **kw):
    return lax.dot_general(a, b, (((0,), (0,)), ((), ())), preferred_element_type=F32, **kw)


HIGH = dict(precision=lax.Precision.HIGHEST)


CORE = [(0, 1), (1, 0), (2, 3), (3, 2)]
ZLO = [(0, 2), (2, 0), (1, 3), (3, 1)]


def dp_perm(dy, dz, dx):
    out = []
    for y in range(4):
        for z in range(2):
            for x in range(4):
                out.append(((y * 2 + z) * 4 + x, (((y + dy) % 4) * 2 + (z + dz) % 2) * 4 + (x + dx) % 4))
    return out


XS = {1: dp_perm(0, 0, 1), 3: dp_perm(0, 0, -1), 2: dp_perm(0, 0, 2)}
YS = {1: dp_perm(1, 0, 0), 3: dp_perm(-1, 0, 0), 2: dp_perm(2, 0, 0)}
ZH = dp_perm(0, 1, 0)
Y_PAIR = [((y * 2 + z) * 4 + x, ((y ^ 1) * 2 + z) * 4 + x) for y in range(4) for z in range(2) for x in range(4)]
X_PAIR = [((y * 2 + z) * 4 + x, (y * 2 + z) * 4 + (x ^ 1)) for y in range(4) for z in range(2) for x in range(4)]


def core_swap(v):
    return lax.ppermute(v, "mp", CORE)


def z_swap(v):
    return lax.ppermute(v, "mp", ZLO)


def rows_of(v, start, size):
    return lax.dynamic_slice_in_dim(v, start, size, 0)


def item_starts(len_ref):
    starts, total = [], jnp.int32(0)
    for j in range(8):
        starts.append(total)
        total = total + len_ref[0, j]
    return starts


def start_at(starts, place):
    best = jnp.int32(0)
    for s in starts[1:]:
        best = jnp.where(s <= place, jnp.maximum(best, s), best)
    return best


def chunk_masks(starts, base):
    row = lax.broadcasted_iota(jnp.int32, (CH, CH), 0)
    col = lax.broadcasted_iota(jnp.int32, (CH, CH), 1)
    blk = jnp.bitwise_and(row, -BLK)
    row1 = lax.broadcasted_iota(jnp.int32, (CH, 128), 0)
    place = row1 + base
    low = jnp.zeros_like(place)
    for s in starts[1:]:
        low = jnp.where(place >= s, jnp.maximum(low, s), low)
    low = low - base
    blk1 = jnp.bitwise_and(row1, -BLK)
    carried = low < blk1
    low_wide = jnp.concatenate([low, low], axis=1)
    causal = (col <= row) & (col >= blk)
    visible = causal & (col >= low_wide)
    return visible, carried


def causal_ones():
    row = lax.broadcasted_iota(jnp.int32, (CH, CH), 0)
    col = lax.broadcasted_iota(jnp.int32, (CH, CH), 1)
    return jnp.where((col <= row) & (col >= jnp.bitwise_and(row, -BLK)), 1.0, 0.0).astype(BF16)


def two_parts(v):
    high = v.astype(BF16)
    return high, (v - high.astype(F32)).astype(BF16)


def block_scalars(starts, base, b):
    first = base + b * BLK
    origin = start_at(starts, first + BLK - 1)
    keep = jnp.where(origin < first, 1.0, 0.0).astype(F32)
    place = lax.broadcasted_iota(jnp.int32, (BLK, 128), 0) + first
    return keep, place >= origin


def scaled_parts(q, k, cum):
    last = jnp.broadcast_to(cum.reshape(CH // BLK, BLK, 128)[:, BLK - 1 :, :], (CH // BLK, BLK, 128))
    last = last.reshape(CH, 128)
    e, en, ef = jnp.exp(cum), jnp.exp(-cum), jnp.exp(last - cum)
    qf = q.astype(F32) * SCALE * e
    ks = k.astype(F32) * en
    kf = k.astype(F32) * ef
    return last, e, en, ef, qf, ks, kf


def mixer_forward(
    len_ref, tok_ref, g1_ref, wq_ref, wk_ref, wv_ref, wgd_ref, wgu_ref, bias_ref,
    n_ref, q_ref, k_ref, v_ref, low_ref, logit_ref, cum_ref, mixed_lo_ref, mixed_hi_ref, st_ref, state,
):
    step = pl.program_id(0)
    rows = tok_ref.shape[0]
    starts = item_starts(len_ref)

    @pl.when(step == 0)
    def _():
        state[...] = jnp.zeros_like(state)

    ones = causal_ones()
    s = state[...]
    for c in range(rows // CH):
        base = step * rows + c * CH
        at = slice(c * CH, (c + 1) * CH)
        x = tok_ref[at, :].astype(F32)
        r = lax.rsqrt(jnp.mean(x * x, axis=-1, keepdims=True) + EPS)
        n = (x * r * g1_ref[...]).astype(BF16)
        n_ref[at, :] = n
        low = nt(n, wgd_ref[...]).astype(BF16)
        low_ref[at, :] = low
        logits = nn(low, wgu_ref[...]) + bias_ref[...]
        logit_ref[at, :] = logits
        decays = (jnp.minimum(logits, 0.0) - jnp.log1p(jnp.exp(-jnp.abs(logits)))) * (1.0 / 16.0)
        high, rest = two_parts(decays)
        cum = nn(ones, high) + nn(ones, rest)
        cum_ref[at, :] = cum
        q = nn(n, wq_ref[...]).astype(BF16)
        k = nn(n, wk_ref[...]).astype(BF16)
        v = nn(n, wv_ref[...]).astype(BF16)
        q_ref[at, :] = q
        k_ref[at, :] = k
        v_ref[at, :] = v
        visible, carried = chunk_masks(starts, base)
        last, e, en, ef, qf, ks, kf = scaled_parts(q, k, cum)
        scores = jnp.where(visible, nt(qf.astype(BF16), ks.astype(BF16)), 0.0).astype(BF16)
        out = nn(scores, v)
        q_carried = jnp.where(carried, qf, 0.0).astype(BF16)
        mixed_parts = []
        for b in range(CH // BLK):
            sl = slice(b * BLK, (b + 1) * BLK)
            keep, tail = block_scalars(starts, base, b)
            st_ref[c * (CH // BLK) + b] = s
            inter = nt(q_carried[sl], s.astype(BF16))
            mixed_parts.append((out[sl] + inter).astype(BF16).astype(F32))
            k_tail = jnp.where(tail, kf[sl], 0.0).astype(BF16)
            s = keep * jnp.exp(last[b * BLK : b * BLK + 1]) * s + tn(v[sl], k_tail)
        mixed = jnp.concatenate(mixed_parts, axis=0)

        @pl.when(step < 2)
        def _(mixed=mixed):
            mixed_lo_ref[...] = mixed

        @pl.when(step >= 2)
        def _(mixed=mixed):
            mixed_hi_ref[...] = mixed

    state[...] = s


def run_mixer_forward(lengths, tokens, g1, wq, wk, wv, wgd, wgu, bias):
    t = tokens.shape[0]
    whole = lambda a: pl.BlockSpec(a.shape, lambda i: (0,) * a.ndim)
    rows = lambda c: pl.BlockSpec((CH, c), lambda i: (i, 0))
    nb = CH // BLK
    outs = [
        ((t, 1024), BF16), ((t, 128), BF16), ((t, 128), BF16), ((t, 256), BF16), ((t, 16), BF16), ((t, 128), F32), ((t, 128), F32),
    ]
    sds = jax.ShapeDtypeStruct
    return pl.pallas_call(
        mixer_forward,
        grid=(t // CH,),
        in_specs=[pl.BlockSpec(memory_space=pltpu.SMEM), rows(1024), whole(g1), whole(wq), whole(wk), whole(wv),
                  whole(wgd), whole(wgu), whole(bias)],
        out_specs=[rows(s[1]) for s, _ in outs]
        + [pl.BlockSpec((CH, 256), lambda i: (jnp.minimum(i, 1), 0)), pl.BlockSpec((CH, 256), lambda i: (jnp.maximum(i - 2, 0), 0)),
           pl.BlockSpec((nb, 256, 128), lambda i: (i, 0, 0))],
        out_shape=[sds(s, d) for s, d in outs] + [sds((t // 2, 256), F32)] * 2 + [sds((t // BLK, 256, 128), F32)],
        scratch_shapes=[pltpu.VMEM((256, 128), F32)],
        compiler_params=pltpu.CompilerParams(vmem_limit_bytes=VMEM_BYTES),
        cost_estimate=weight(10),
        name="mixer_forward",
    )(lengths, tokens, g1, wq, wk, wv, wgd, wgu, bias)


def before_feed_kernel(w0_ref, w1_ref, w2_ref, w3_ref, cot_ref, wd_ref, wo_ref, gh_ref):
    for j, w_ref in enumerate((w0_ref, w1_ref, w2_ref, w3_ref)):

        @pl.when(pl.program_id(0) == j)
        def _(w_ref=w_ref):
            wo_ref[...] = w_ref[...].astype(BF16)

    gh_ref[...] = nt(cot_ref[...], wd_ref[...])


def run_before_feed(wo, cot, wd):
    t = cot.shape[0]
    whole = lambda a: pl.BlockSpec(a.shape, lambda s: (0,) * a.ndim)
    rows = lambda c: pl.BlockSpec((CH, c), lambda s: (s, 0))
    return pl.pallas_call(
        before_feed_kernel,
        grid=(t // CH,),
        in_specs=[whole(w) for w in wo] + [rows(1024), whole(wd)],
        out_specs=[rows(1024), rows(704)],
        out_shape=[jax.ShapeDtypeStruct((t, 1024), BF16), jax.ShapeDtypeStruct((t, 704), F32)],
        compiler_params=pltpu.CompilerParams(vmem_limit_bytes=VMEM_BYTES),
        cost_estimate=weight(7),
        name="before_feed",
    )(*wo, cot, wd)


def feed_kernel(
    at_ref, tok_ref, gh_ref, m0_ref, m1_ref, m2_ref, m3_ref, wo_ref, g2_ref, wg_ref, wu_ref, wd_ref,
    mid_ref, n_ref, hid_ref, gg_ref, feed_out_ref, feed_keep_ref, part_out_ref, part_keep_ref,
):
    step = pl.program_id(0)

    mixed = jnp.concatenate([m0_ref[...], m1_ref[...], m2_ref[...], m3_ref[...]], axis=1).astype(BF16)
    mid = tok_ref[...].astype(F32) + nn(mixed, wo_ref[...])
    mid_ref[...] = mid
    r = lax.rsqrt(jnp.mean(mid * mid, axis=-1, keepdims=True) + EPS)
    n = (mid * r * g2_ref[...]).astype(BF16)
    n_ref[...] = n
    pre = nt(n, wg_ref[...])
    up = nt(n, wu_ref[...])
    sg = jax.nn.sigmoid(pre)
    act = pre * sg
    hid = (act * up).astype(BF16)
    hid_ref[...] = hid
    gh = gh_ref[...]
    gg = (gh * up * sg * (1.0 + pre * (1.0 - sg))).astype(BF16)
    gu = (gh * act).astype(BF16)
    gg_ref[:, 0:704] = gg
    gg_ref[:, 704:1408] = gu
    feed = nn(hid, wd_ref[...])
    part = nn(gg, wg_ref[...]) + nn(gu, wu_ref[...])

    @pl.when(step == 0)
    def _():
        feed_out_ref[...] = feed
        part_out_ref[...] = part

    @pl.when(step == 1)
    def _():
        feed_keep_ref[...] = feed
        part_keep_ref[...] = part


def run_feed(at, chunk, tokens, gh, mixed, wo, g2, wg, wu, wd):
    t = tokens.shape[0] // 2
    whole = lambda a: pl.BlockSpec(a.shape, lambda s, at: (0,) * a.ndim)
    half = lambda s, at: jnp.bitwise_xor(1 - at[2], s)
    rows = lambda c: pl.BlockSpec((CH, c), lambda s, at: (half(s, at), 0))
    from_all = lambda c: pl.BlockSpec((CH, c), lambda s, at: (2 * chunk + half(s, at), 0))
    once = pl.BlockSpec((CH, 1024), lambda s, at: (0, 0))
    sds = jax.ShapeDtypeStruct
    return pl.pallas_call(
        feed_kernel,
        grid_spec=pltpu.PrefetchScalarGridSpec(
            num_scalar_prefetch=1,
            grid=(t // CH,),
            in_specs=[from_all(1024), from_all(704)] + [rows(256)] * 4 + [whole(wo), whole(g2), whole(wg), whole(wu), whole(wd)],
            out_specs=[rows(1024), rows(1024), rows(704), rows(1408), once, once, once, once],
        ),
        out_shape=[sds((t, 1024), F32), sds((t, 1024), BF16), sds((t, 704), BF16), sds((t, 1408), BF16)] + [sds((CH, 1024), F32)] * 4,
        compiler_params=pltpu.CompilerParams(vmem_limit_bytes=VMEM_BYTES),
        cost_estimate=weight(14),
        name="feed_both_ways",
    )(at, tokens, gh, *mixed, wo, g2, wg, wu, wd)


def mixer_backward(
    at_ref, len_ref, *refs,
):
    gm_refs, gain_ref, refs = refs[:4], refs[4], refs[5:]
    (tok_ref, n_ref, q_ref, k_ref, v_ref, low_ref, logit_ref, cum_ref,
     st_ref, wo_ref, wq_ref, wk_ref, wv_ref, wgd_ref, wgu_ref,
     dqkv_ref, far0_ref, far1_ref, near0_ref, near1_ref, part_keep_ref, ga_ref, small_ref, gup_ref, bias_ref, dstate, whole) = refs
    step = pl.program_id(0)
    steps = pl.num_programs(0)
    rows = tok_ref.shape[0]
    starts = item_starts(len_ref)

    core, z = at_ref[2], at_ref[3]
    here = steps - 1 - step
    mine = jnp.equal(lax.rem(here, 2), core)

    @pl.when(step == 0)
    def _():
        dstate[...] = jnp.zeros_like(dstate)
        small_ref[...] = jnp.zeros_like(small_ref)
        small_ref[17:18, :] = gain_ref[0:1, :]
        gup_ref[...] = jnp.zeros_like(gup_ref)
        bias_ref[...] = jnp.zeros_like(bias_ref)

    first = pl.multiple_of(z * 128, 128)
    second = pl.multiple_of((1 - z) * 128, 128)
    for other in range(2):

        @pl.when(jnp.logical_not(mine) if other else mine)
        def _(other=other):
            ga_ref[pl.ds(first, 128), :] = gm_refs[2 * other][...].astype(BF16)
            ga_ref[pl.ds(second, 128), :] = gm_refs[2 * other + 1][...].astype(BF16)

    ones = causal_ones()
    ds = dstate[...]
    for c in reversed(range(rows // CH)):
        base = here * rows + c * CH
        at = slice(c * CH, (c + 1) * CH)
        g = nt(ga_ref[at, :], wo_ref[...]).astype(BF16)
        q, k, v, cum = q_ref[at, :], k_ref[at, :], v_ref[at, :], cum_ref[at, :]
        visible, carried = chunk_masks(starts, base)
        last, e, en, ef, qf, ksf, kff = scaled_parts(q, k, cum)
        qs, ks = qf.astype(BF16), ksf.astype(BF16)
        scores = jnp.where(visible, nt(qs, ks), 0.0).astype(BF16)
        dscores = jnp.where(visible, nt(g, v), 0.0).astype(BF16)
        dv = tn(scores, g)
        dqs = nn(dscores, ks)
        dks = tn(dscores, qs)
        q_carried = jnp.where(carried, qf, 0.0).astype(BF16)
        dvs, dkfs, dqss, dls = [], [], [], []
        for b in reversed(range(CH // BLK)):
            sl = slice(b * BLK, (b + 1) * BLK)
            keep, tail = block_scalars(starts, base, b)
            dsb = ds.astype(BF16)
            s = st_ref[c * (CH // BLK) + b]
            k_tail = jnp.where(tail, kff[sl], 0.0).astype(BF16)
            dvs.append(dv[sl] + nt(k_tail, dsb))
            dkf = jnp.where(tail, nn(v[sl], dsb), 0.0)
            dkfs.append(dkf)
            dqss.append(dqs[sl] + jnp.where(carried[sl], nn(g[sl], s.astype(BF16)), 0.0))
            grow = keep * jnp.exp(last[b * BLK : b * BLK + 1])
            dlast = grow * jnp.sum(s * ds, axis=0, keepdims=True) + jnp.sum(dkf * kff[sl], axis=0, keepdims=True)
            dls.append(jnp.broadcast_to(dlast, (BLK, 128)))
            ds = grow * ds + tn(g[sl], q_carried[sl])
        join = lambda parts: jnp.concatenate(parts[::-1], axis=0)
        dqs, dkf, dl = join(dqss), join(dkfs), join(dls)
        dq = (dqs * (SCALE * e)).astype(BF16)
        dk = (dks * en + dkf * ef).astype(BF16)
        dv = join(dvs).astype(BF16)
        dqkv_ref[at, 0:128] = dq
        dqkv_ref[at, 128:256] = dk
        dqkv_ref[at, 256:512] = dv
        high, rest = two_parts(dqs * qf - dks * ksf - dkf * kff)
        ddec = tn(ones, high) + tn(ones, rest) + dl
        glog = ddec * jax.nn.sigmoid(-logit_ref[at, :]) * (1.0 / 16.0)
        bias_ref[0:1, :] += jnp.sum(glog, axis=0, keepdims=True)
        high, rest = two_parts(glog)
        gup_ref[...] += tn(low_ref[at, :], high) + tn(low_ref[at, :], rest)
        glr = (nt(high, wgu_ref[...]) + nt(rest, wgu_ref[...])).astype(BF16)
        part = nt(dq, wq_ref[...]) + nt(dk, wk_ref[...]) + nt(dv, wv_ref[...]) + nn(glr, wgd_ref[...])
        @pl.when(mine)
        def _(part=part):
            part_keep_ref[...] = part

        for chunk, (far_ref, near_ref) in enumerate(((far0_ref, near0_ref), (far1_ref, near1_ref))):

            @pl.when(jnp.logical_and(jnp.logical_not(mine), jnp.equal(lax.div(here, 2), chunk)))
            def _(part=part, far_ref=far_ref, near_ref=near_ref):
                whole[...] = part
                far_ref[...] = whole[pl.ds(second, 128), :]
                near_ref[...] = whole[pl.ds(first, 128), :]

        small_ref[0:16, :] += tn(glr, n_ref[at, :])
        x = tok_ref[at, :].astype(F32)
        r = lax.rsqrt(jnp.mean(x * x, axis=-1, keepdims=True) + EPS)
        small_ref[16:17, :] += jnp.sum(part * x * r, axis=0, keepdims=True)
    dstate[...] = ds


def run_mixer_backward(at, lengths, gm, gain, tokens, n, q, k, v, low, logits, cum, st, wo, wq, wk, wv, wgd, wgu):
    t = tokens.shape[0]
    steps = t // CH
    whole = lambda a: pl.BlockSpec(a.shape, lambda i, at: (0,) * a.ndim)
    rows = lambda c: pl.BlockSpec((CH, c), lambda i, at: (steps - 1 - i, 0))
    split = pl.BlockSpec((CH, 1024), lambda i, at: (lax.div(steps - 1 - i, 2), 0))
    nb = CH // BLK
    fixed = lambda s: pl.BlockSpec(s, lambda i, at: (0, 0))
    sds = jax.ShapeDtypeStruct
    return pl.pallas_call(
        mixer_backward,
        grid_spec=pltpu.PrefetchScalarGridSpec(
            num_scalar_prefetch=1,
            grid=(steps,),
            in_specs=[pl.BlockSpec(memory_space=pltpu.SMEM)] + [pl.BlockSpec((128, 1024), lambda i, at: (lax.div(steps - 1 - i, 2), 0))] * 4 + [whole(gain)]
            + [rows(1024), rows(1024), rows(128), rows(128), rows(256), rows(16), rows(128), rows(128),
               pl.BlockSpec((nb, 256, 128), lambda i, at: (steps - 1 - i, 0, 0)),
               whole(wo), whole(wq), whole(wk), whole(wv), whole(wgd), whole(wgu)],
            out_specs=[rows(512)] + [fixed((128, 1024))] * 4 + [split, rows(1024), fixed((24, 1024)), fixed((16, 128)), fixed((8, 128))],
            scratch_shapes=[pltpu.VMEM((256, 128), F32), pltpu.VMEM((CH, 1024), F32)],
        ),
        out_shape=[sds((t, 512), BF16)] + [sds((128, 1024), F32)] * 4 + [sds((t // 2, 1024), F32), sds((t, 1024), BF16),
                   sds((24, 1024), F32), sds((16, 128), F32), sds((8, 128), F32)],
        compiler_params=pltpu.CompilerParams(vmem_limit_bytes=VMEM_BYTES),
        cost_estimate=weight(BACK_US),
        name="mixer_backward",
    )(at, lengths, *gm, gain, tokens, n, q, k, v, low, logits, cum, st, wo, wq, wk, wv, wgd, wgu)


SMALL = dict(
    compiler_params=pltpu.CompilerParams(vmem_limit_bytes=VMEM_BYTES),
    cost_estimate=weight(3),
)


def quarter(v, j, which):
    return rows_of(v, 256 * j + 128 * which, 128)


def norm_gradient(dn, y, gain):
    r = lax.rsqrt(jnp.mean(y * y, axis=-1, keepdims=True) + EPS)
    gd = dn * gain
    dy = r * gd - (r * r * r) * y * jnp.mean(gd * y, axis=-1, keepdims=True)
    return dy, jnp.sum(dn * y * r, axis=0, keepdims=True)


def second_norm_kernel(at_ref, a0_ref, b0_ref, c0_ref, y0_ref, a1_ref, b1_ref, c1_ref, y1_ref, gain_ref, base0_ref, base1_ref, o_ref, s_ref):
    halves = ((a0_ref, b0_ref, c0_ref, y0_ref, base0_ref), (a1_ref, b1_ref, c1_ref, y1_ref, base1_ref))
    total = jnp.zeros((1, 1024), F32)
    for j, (a_ref, b_ref, c_ref, y_ref, base_ref) in enumerate(halves):
        dy, dgain = norm_gradient(a_ref[...] + b_ref[...] + c_ref[...], y_ref[...], gain_ref[...])
        o_ref[128 * j : 128 * (j + 1)] = base_ref[...].astype(F32) + dy
        total = total + dgain
    s_ref[0:1, :] = total


def run_second_norm(at, keep, got, far, middle, gain, cot):
    of_half = pl.BlockSpec((128, 1024), lambda s, at: (at[3], 0))
    of_chunk = pl.BlockSpec((128, 1024), lambda s, at: (2 * at[2] + at[3], 0))
    of_all = lambda j: pl.BlockSpec((128, 1024), lambda s, at: (4 * j + 2 * at[2] + at[3], 0))
    fixed = lambda *s: pl.BlockSpec(s, lambda s, at: (0, 0))
    ops = [v for j in range(2) for v in (keep[j], got[j], far[j], middle[j])]
    return pl.pallas_call(
        second_norm_kernel,
        grid_spec=pltpu.PrefetchScalarGridSpec(
            num_scalar_prefetch=1, grid=(1,),
            in_specs=[of_half, of_half, fixed(128, 1024), of_chunk] * 2 + [fixed(1, 1024), of_all(0), of_all(1)],
            out_specs=[fixed(256, 1024), fixed(8, 1024)]),
        out_shape=[jax.ShapeDtypeStruct((256, 1024), F32), jax.ShapeDtypeStruct((8, 1024), F32)],
        name="second_norm_back",
        **SMALL,
    )(at, *ops, gain, cot, cot)


def first_norm_kernel(at_ref, a_ref, b0_ref, b1_ref, c_ref, y_ref, base_ref, gain_ref, own_ref):
    for j, b_ref in enumerate((b0_ref, b1_ref)):

        @pl.when(pl.program_id(0) == j)
        def _(b_ref=b_ref):
            dy, _ = norm_gradient(a_ref[...] + b_ref[...] + c_ref[...], y_ref[...].astype(F32), gain_ref[...])
            own_ref[...] = dy + base_ref[...]


def run_first_norm(at, keep, got, far, tokens, base, gain):
    of_half = pl.BlockSpec((128, 1024), lambda s, at: (2 * s + at[3], 0))
    of_all = pl.BlockSpec((128, 1024), lambda s, at: (4 * s + 2 * at[2] + at[3], 0))
    own = pl.BlockSpec((128, 1024), lambda s, at: (s, 0))
    fixed = lambda *n: pl.BlockSpec(n, lambda s, at: (0, 0))
    return pl.pallas_call(
        first_norm_kernel,
        grid_spec=pltpu.PrefetchScalarGridSpec(
            num_scalar_prefetch=1, grid=(2,),
            in_specs=[of_half, fixed(128, 1024), fixed(128, 1024), own, of_all, own, fixed(1, 1024)], out_specs=own),
        out_shape=jax.ShapeDtypeStruct((256, 1024), F32),
        name="first_norm_back",
        **SMALL,
    )(at, keep, *got, far, tokens, base, gain)


def place_kernel(at_ref, r0_ref, g0_ref, r1_ref, g1_ref, *rest):
    result_ref, grad_ref = rest[-2:]

    @pl.when(lax.rem(pl.program_id(0), 2) == 0)
    def _():
        result_ref[...] = r0_ref[...].astype(BF16)
        grad_ref[...] = g0_ref[...]

    @pl.when(lax.rem(pl.program_id(0), 2) == 1)
    def _():
        result_ref[...] = r1_ref[...].astype(BF16)
        grad_ref[...] = g1_ref[...]


def run_place(at, odd, pieces, into=()):
    chunk = lambda s: lax.div(s, 2)
    place = lambda s, at: jnp.bitwise_xor(2 * at[2] + at[3], 2 * lax.rem(s, 2) + odd)
    piece = pl.BlockSpec((128, 1024), lambda s, at: (chunk(s), 0))
    placed = pl.BlockSpec((128, 1024), lambda s, at: (4 * chunk(s) + place(s, at), 0))
    return pl.pallas_call(
        place_kernel,
        grid_spec=pltpu.PrefetchScalarGridSpec(
            num_scalar_prefetch=1, grid=(4,),
            in_specs=[piece] * 4 + [pl.BlockSpec(memory_space=pl.ANY)] * len(into),
            out_specs=[placed, placed]),
        out_shape=[jax.ShapeDtypeStruct((1024, 1024), BF16), jax.ShapeDtypeStruct((1024, 1024), F32)],
        input_output_aliases={5: 0, 6: 1} if into else {},
        name="place_rows",
        **SMALL,
    )(at, *pieces, *into)


def feed_grads_kernel(l0_ref, l1_ref, r0_ref, r1_ref, c0_ref, c1_ref, h0_ref, h1_ref, out):
    w1, w2 = r0_ref.shape[1], h0_ref.shape[1]
    first = tn(l0_ref[...], r0_ref[...]) + tn(l1_ref[...], r1_ref[...])
    second = tn(c0_ref[...], h0_ref[...]) + tn(c1_ref[...], h1_ref[...])
    for x in range(4):
        for zh in range(2):
            row = zh * 128 + x * 32
            out[x, 0, zh, :, 0:w1] = first[row : row + 32]
            out[x, 0, zh, :, w1 : w1 + w2] = second[row : row + 32]
            out[x, 0, zh, :, w1 + w2 :] = jnp.zeros((32, out.shape[-1] - w1 - w2), F32)


def run_feed_grads(n2, gg, cot, hid):
    t = cot.shape[0] // 2
    c = gg[0].shape[1] + hid[0].shape[1]
    wide = -(-c // 128) * 128
    cols = lambda j: pl.BlockSpec((t, CH), lambda s: (j, s))
    whole = lambda a: pl.BlockSpec(a.shape, lambda s: (0, 0))
    return pl.pallas_call(
        feed_grads_kernel,
        grid=(4,),
        in_specs=[cols(0), cols(0), whole(gg[0]), whole(gg[1]), cols(0), cols(1), whole(hid[0]), whole(hid[1])],
        out_specs=pl.BlockSpec((4, 1, 2, 32, wide), lambda s: (0, s, 0, 0, 0)),
        out_shape=jax.ShapeDtypeStruct((4, 4, 2, 32, wide), F32),
        compiler_params=pltpu.CompilerParams(vmem_limit_bytes=VMEM_BYTES),
        cost_estimate=weight(12),
        name="feed_weight_grads",
    )(n2[0], n2[1], gg[0], gg[1], cot, cot, hid[0], hid[1])


RING_OUTS = ((0, None, 0), (2, 0, 1), (1, 1, 1), (3, 0, 2), (2, 1, 2), (1, 0, 3), (3, 1, 4))


def mixer_grads_kernel(at_ref, l_ref, r0_ref, a0_ref, m0_ref, m1_ref, small_ref, gup_ref, bias_ref, *outs):
    step = pl.program_id(0)
    w1 = r0_ref.shape[1]

    @pl.when(step < 4)
    def _():
        n = m0_ref.shape[0]
        first = tn(l_ref[...], r0_ref[...])
        second = tn(a0_ref[0:n], m0_ref[...].astype(BF16)) + tn(a0_ref[n:], m1_ref[...].astype(BF16))

        def write(ref, x, to):
            for zh in range(2):
                row = zh * 128 + x * 32
                ref[2 * to + zh, :, 0:w1] = first[row : row + 32]
                ref[2 * to + zh, :, w1:] = second[row : row + 32]

        offset = lax.rem(step - at_ref[1] + 4, 4)

        for k, late, ref in RING_OUTS:

            @pl.when(offset == k)
            def _(late=late, ref=ref):
                for x in range(4):
                    if late is None or late == x // 2:
                        write(outs[ref], x, x if ref < 3 else x % 2)

    @pl.when(step == 4)
    def _():
        small = small_ref[...]
        for out in (outs[0], outs[1], outs[2], outs[4]):
            last = out.shape[0] - 1
            out[last] = jnp.zeros(out.shape[1:], F32)
            out[last, 0:16, :] = small[0:16, 0:768]
            for j in range(3):
                n = min(6, 16 - 6 * j)
                out[last, 16 : 16 + n, 256 * j : 256 * (j + 1)] = small[6 * j : 6 * j + n, 768:1024]
            for j in range(6):
                n = min(3, 16 - 3 * j)
                out[last, 22 : 22 + n, 128 * j : 128 * (j + 1)] = gup_ref[3 * j : 3 * j + n, :]
            out[last, 25:26, :] = small[16:17, 0:768]
            out[last, 26:27, :] = small[17:18, 0:768]
            out[last, 27:28, 0:256] = small[16:17, 768:1024]
            out[last, 27:28, 256:512] = small[17:18, 768:1024]
            out[last, 27:28, 512:640] = bias_ref[0:1, :]


def run_mixer_grads(at, n1, dqkv, ga, mixed, small, gup, bias):
    t, c = n1.shape[0], dqkv.shape[1] + mixed[0].shape[1]
    cols = pl.BlockSpec((t, CH), lambda s, at: (0, jnp.minimum(s, 3)))
    whole = lambda a: pl.BlockSpec(a.shape, lambda s, at: (0, 0))
    rest = [small, gup, bias]
    counts = [9, 9, 9, 4, 5]
    return pl.pallas_call(
        mixer_grads_kernel,
        grid_spec=pltpu.PrefetchScalarGridSpec(
            num_scalar_prefetch=1, grid=(5,),
            in_specs=[cols, whole(dqkv), cols, whole(mixed[0]), whole(mixed[1])] + [whole(a) for a in rest],
            out_specs=[pl.BlockSpec((n, 32, c), lambda s, at: (0, 0, 0)) for n in counts]),
        out_shape=[jax.ShapeDtypeStruct((n, 32, c), F32) for n in counts],
        compiler_params=pltpu.CompilerParams(vmem_limit_bytes=VMEM_BYTES),
        cost_estimate=weight(8),
        name="mixer_weight_grads",
    )(at, n1, dqkv, ga, mixed[0], mixed[1], *rest)


def unpack_kernel(
    own_ref, got_ref, a_ref, b_ref, sums_ref, far_ref,
    g1_ref, down_ref, up_ref, bias_ref, g2_ref, q_ref, k_ref, v_ref, o_ref, gate_ref, mup_ref, mdown_ref,
):
    rows = own_ref[...] + got_ref[...]
    feed = a_ref[...] + b_ref[...]
    own = rows[:, 768:1536]
    sums = sums_ref[...] + far_ref[...]
    wide = jnp.concatenate([sums[16:22, 0:256], sums[16:22, 256:512], sums[16:20, 512:768]], axis=0)
    down_ref[...] = jnp.concatenate([sums[0:16], wide], axis=1)
    for j in range(6):
        n = min(3, 16 - 3 * j)
        up_ref[3 * j : 3 * j + n, :] = own[22 : 22 + n, 128 * j : 128 * (j + 1)]
    g1_ref[:, 0:768] = sums[25:26]
    g1_ref[:, 768:1024] = sums[27:28, 0:256]
    g2_ref[:, 0:768] = sums[26:27]
    g2_ref[:, 768:1024] = sums[27:28, 256:512]
    bias_ref[...] = own[27:28, 512:640]
    q_ref[...] = rows[:, 0:128]
    k_ref[...] = rows[:, 128:256]
    v_ref[...] = rows[:, 256:512]
    o_ref[...] = rows[:, 512:768]
    gate_ref[...] = feed[:, 0:704]
    mup_ref[...] = feed[:, 704:1408]
    mdown_ref[...] = feed[:, 1408:2112]


def unpack(own, got, feed_own, feed_got, sums, far):
    shapes = [(1, 1024), (16, 1024), (16, 128), (1, 128), (1, 1024), (32, 128), (32, 128), (32, 256), (32, 256)] + [(32, 704)] * 3
    return pl.pallas_call(
        unpack_kernel, out_shape=[jax.ShapeDtypeStruct(s, F32) for s in shapes], name="unpack", **SMALL,
    )(own, got, feed_own, feed_got, sums, far)


def after(value, *others):
    return lax.optimization_barrier((value, others))[0]


def send(v, shifts, d):
    return lax.ppermute(v, "dp", shifts[d])


GX = [[(y * 2 + z) * 4 + x for x in range(4)] for y in range(4) for z in range(2)]
GY = [[(y * 2 + z) * 4 + x for y in range(4)] for x in range(4) for z in range(2)]


def scatter_rows(v, groups):
    return lax.psum_scatter(v, "dp", scatter_dimension=0, tiled=True, axis_index_groups=groups)


def ring_first(v, shifts):
    return lax.ppermute(v[1], "dp", shifts[1]), lax.ppermute(v[2], "dp", shifts[3])


def ring_on(v, got):
    n = v[3].shape[0]
    return v[3] + got[0][:n], v[4] + got[1][n:]


def ring_last(on, shifts):
    return lax.ppermute(on[0], "dp", shifts[1]), lax.ppermute(on[1], "dp", shifts[3])


def ring_total(v, got, last):
    n = last[0].shape[0]
    return jnp.concatenate([v[0][:n] + last[0] + got[1][:n], v[0][n:] + got[0][n:] + last[1]], axis=0)


def pick(v, i, dim):
    return lax.dynamic_index_in_dim(v, i, dim, False)


def swap_zh(v, zh, dim):
    return pick(v, zh, dim) + lax.ppermute(pick(v, 1 - zh, dim), "dp", ZH)


def local(tokens, lengths, g1, wq, wk, wv, wgd, wgu, bias, wout, g2, wg, wu, wd, cot):
    mp, dp = lax.axis_index("mp"), lax.axis_index("dp")
    core, z = mp % 2, mp // 2
    ix, zh, iy = dp % 4, (dp // 4) % 2, dp // 8
    at = jnp.stack([ix, iy, core, z]).astype(jnp.int32)
    g1r, g2r, biasr = g1.reshape(1, -1), g2.reshape(1, -1), bias.reshape(1, -1)
    wgd_t, wg_t, wu_t = wgd.T, wg.T, wu.T

    def phase(*values):
        return lax.optimization_barrier(values)

    def across(v, at_here, shifts, take):
        return [take(v, at_here)] + [send(take(v, (at_here + k) % 4), shifts, k) for k in (1, 3, 2)]

    with jax.named_scope("out_weights"):
        wide = wout.astype(F32)
        wout_z = z_swap(wide)
        wout_c = core_swap(wide)
    n1, q, k, v, low, logits, cum, mixed_lo, mixed_hi, st = run_mixer_forward(
        lengths, after(tokens, wide), g1r, wq, wk, wv, wgd_t, wgu, biasr)
    wout_z, wout_c, mixed_lo, mixed_hi = phase(wout_z, wout_c, mixed_lo, mixed_hi)

    with jax.named_scope("heads_one"):
        hi_z = z_swap(mixed_hi)
        hi_c = core_swap(mixed_hi)
        lo_c = core_swap(mixed_lo)
        wout_cz = core_swap(wout_z)
    wo, gh = run_before_feed((wout, wout_z, wout_c, wout_cz), cot, wd)
    hi_z, hi_c, lo_c, mixed_lo, wo, gh = phase(hi_z, hi_c, lo_c, mixed_lo, wo, gh)

    with jax.named_scope("heads_two"):
        lo_z = z_swap(mixed_lo)
        hi_cz = core_swap(hi_z)
    one = run_feed(at, 1, tokens, gh, (mixed_hi, hi_z, hi_c, hi_cz), wo, g2r, wg_t, wu_t, wd)
    lo_z, one = phase(lo_z, one)

    with jax.named_scope("second_norm_core"):
        part_in1 = core_swap(one[6])
        dn2_out1 = quarter(one[7], 0, 1 - z) + quarter(part_in1, 0, 1 - z)
    dn2_out1, part_in1, one, lo_z = phase(dn2_out1, part_in1, one, lo_z)

    with jax.named_scope("second_norm_z"):
        dn2_z1 = z_swap(dn2_out1)
        lo_cz = core_swap(lo_z)
    zero = run_feed(at, 0, tokens, gh, (mixed_lo, lo_z, lo_c, lo_cz), wo, g2r, wg_t, wu_t, wd)
    dn2_z1, zero = phase(dn2_z1, zero)

    with jax.named_scope("second_norm_core"):
        part_in0 = core_swap(zero[6])
        dn2_out0 = quarter(zero[7], 0, 1 - z) + quarter(part_in0, 0, 1 - z)
    dn2_out0, part_in0, one, zero = phase(dn2_out0, part_in0, one, zero)

    middle, n2, hid, gg, feed_out, feed_keep, _, part_keep = zip(zero, one)
    with jax.named_scope("second_norm_z"):
        dn2_z0 = z_swap(dn2_out0)
        feed_in = [core_swap(f) for f in feed_out]
    a = run_feed_grads(n2, gg, cot, hid)
    dn2_z0, feed_in, a = phase(dn2_z0, feed_in, a)

    gm0, gain2 = run_second_norm(at, part_keep, (part_in0, part_in1), (dn2_z0, dn2_z1), middle, g2r, cot)
    gm0, a, feed_in = phase(gm0, a, feed_in)
    with jax.named_scope("second_norm_join"):
        gm1 = z_swap(gm0)
        gm2 = core_swap(gm0)
    with jax.named_scope("feed_grads_x"):
        a = scatter_rows(a.reshape(1024, a.shape[-1]), GX)
    with jax.named_scope("feed_sum"):
        feed_z_out = jnp.concatenate([quarter(feed_keep[j], 0, 1 - z) + quarter(feed_in[j], 0, 1 - z) for j in range(2)], axis=0)
    gm1, gm2, feed_z_out = phase(gm1, gm2, feed_z_out)

    with jax.named_scope("second_norm_join"):
        gm3 = core_swap(gm1)
    gm3, gm1, feed_z_out = phase(gm3, gm1, feed_z_out)

    with jax.named_scope("feed_sum"):
        feed_z = z_swap(feed_z_out)
    gm = (gm0, gm1, gm2, gm3)
    dqkv, *part1_out, part1_keep, ga, small, gup, gbias = run_mixer_backward(
        at, lengths, gm, gain2, tokens, n1, q, k, v, low, logits, cum, st, wout, wq, wk, wv, wgd_t, wgu)
    with jax.named_scope("first_norm_core"):
        part1_in = [core_swap(p) for p in part1_out]
    c = run_mixer_grads(at, n1, dqkv, ga, (mixed_lo, mixed_hi), small, gup, gbias)
    feed_z, part1_in, part1_keep, c = phase(feed_z, part1_in, part1_keep, c)

    dn1_out = jnp.concatenate([quarter(part1_keep, j, 1 - z) + part1_in[j] for j in range(2)], axis=0)
    dn1_out, c = phase(dn1_out, c)
    with jax.named_scope("first_norm_z"):
        dn1_z = z_swap(dn1_out)
    with jax.named_scope("mixer_grads_first"):
        c_got = ring_first(c, YS)
    feed_own = jnp.concatenate([
        quarter(feed_keep[j], 0, z) + quarter(feed_in[j], 0, z) + feed_z[128 * j : 128 * (j + 1)]
        + rows_of(middle[j], 256 * core + 128 * z, 128) for j in range(2)], axis=0)
    with jax.named_scope("result_join"):
        feed1 = z_swap(feed_own)
    grad0 = run_first_norm(at, part1_keep, part1_in[2:], dn1_z, tokens, gm0, g1r)
    with jax.named_scope("mixer_grads_last"):
        c_last = ring_last(ring_on(c, c_got), YS)
        c = ring_total(c, c_got, c_last)
    with jax.named_scope("grad_join"):
        grad2 = core_swap(grad0)
    with jax.named_scope("result_join"):
        feed2 = core_swap(feed_own)
    feed1, feed2, grad0, grad2, c, feed_own, a = phase(feed1, feed2, grad0, grad2, c, feed_own, a)

    with jax.named_scope("grad_join"):
        grad1 = z_swap(grad0)
    with jax.named_scope("feed_grads_y"):
        a = scatter_rows(a, GY).reshape(2, 32, -1)
    with jax.named_scope("mixer_grads_two"):

        def with_small(i):
            return jnp.concatenate([rows_of(c, 2 * (i % 4), 2), c[8:9]], axis=0)

        c_second = [with_small(ix)] + [send(with_small(ix + k), XS, k) for k in (1, 3, 2)]
    placed = run_place(at, 0, (feed_own, grad0, feed2, grad2))
    with jax.named_scope("mixer_grads_two"):
        c = sum(after(c_second, placed))
    with jax.named_scope("rows"):
        c = after(c, (grad1, placed))
        turned = lambda i: jnp.concatenate([pick(c, i, 0), c[2]], axis=1)
        own = turned(zh)
        got = lax.ppermute(turned(1 - zh), "dp", ZH)
        a_own = pick(a, zh, 0)
        a_out = after(pick(a, 1 - zh, 0), c)
        a_got = lax.ppermute(a_out, "dp", ZH)
    with jax.named_scope("result_join"):
        feed3 = core_swap(feed1)
    with jax.named_scope("grad_join"):
        grad3 = core_swap(after(grad1, c))
    result, grad_tokens = run_place(at, 1, (feed1, grad1, feed3, grad3), placed)
    with jax.named_scope("small_sums"):
        got = after(got, result)
        sums = own[:, 768:1536] + got[:, 768:1536]
        sums = sums + core_swap(sums)
        far = z_swap(sums)
        (gain_one, gate_down, gate_up, gate_bias, gain_two, d_query, d_key, d_value, d_out, d_gate, d_up, d_down) = unpack(
            own, got, a_own, a_got, sums, far)

    return (
        result,
        grad_tokens,
        gain_one.reshape(1024),
        d_query,
        d_key,
        d_value,
        gate_down.T,
        gate_up,
        gate_bias.reshape(128),
        d_out.T,
        gain_two.reshape(1024),
        d_gate,
        d_up,
        d_down.T,
    )


def solution(mesh):
    placed = (
        P("dp", None), P("dp", None), P(), P(None, "mp"), P(None, "mp"), P(None, "mp"), P(), P(None, "mp"),
        P("mp"), P("mp", None), P(), P(None, "mp"), P(None, "mp"), P("mp", None), P("dp", None),
    )
    outs = (
        P("dp", None), P("dp", None), P(), P("dp", "mp"), P("dp", "mp"), P("dp", "mp"), P(), P(None, "mp"),
        P("mp"), P("mp", "dp"), P(), P("dp", "mp"), P("dp", "mp"), P("mp", "dp"),
    )
    return jax.shard_map(local, mesh=mesh, in_specs=placed, out_specs=outs, check_vma=False)
```

```python
import functools

import jax
import jax.numpy as jnp
from jax import lax
from jax.experimental import pallas as pl
from jax.experimental.pallas import tpu as pltpu
from jax.sharding import PartitionSpec as P

BLK = 64
CH = 256
EPS = 1e-6
SCALE = 128 ** -0.5
F32 = jnp.float32
BF16 = jnp.bfloat16
VMEM_BYTES = 63_400_000
BACK_US = 16
FWD_ROWS = 256
BWD_ROWS = 256


def weight(us):
    return pl.CostEstimate(flops=int(us * 1.0e9), bytes_accessed=1024, transcendentals=0)


def nn(a, b, **kw):
    return lax.dot_general(a, b, (((1,), (0,)), ((), ())), preferred_element_type=F32, **kw)


def nt(a, b, **kw):
    return lax.dot_general(a, b, (((1,), (1,)), ((), ())), preferred_element_type=F32, **kw)


def tn(a, b, **kw):
    return lax.dot_general(a, b, (((0,), (0,)), ((), ())), preferred_element_type=F32, **kw)


HIGH = dict(precision=lax.Precision.HIGHEST)


CORE = [(0, 1), (1, 0), (2, 3), (3, 2)]
ZLO = [(0, 2), (2, 0), (1, 3), (3, 1)]


def dp_perm(dy, dz, dx):
    out = []
    for y in range(4):
        for z in range(2):
            for x in range(4):
                out.append(((y * 2 + z) * 4 + x, (((y + dy) % 4) * 2 + (z + dz) % 2) * 4 + (x + dx) % 4))
    return out


XS = {1: dp_perm(0, 0, 1), 3: dp_perm(0, 0, -1), 2: dp_perm(0, 0, 2)}
YS = {1: dp_perm(1, 0, 0), 3: dp_perm(-1, 0, 0), 2: dp_perm(2, 0, 0)}
ZH = dp_perm(0, 1, 0)
Y_PAIR = [((y * 2 + z) * 4 + x, ((y ^ 1) * 2 + z) * 4 + x) for y in range(4) for z in range(2) for x in range(4)]
X_PAIR = [((y * 2 + z) * 4 + x, (y * 2 + z) * 4 + (x ^ 1)) for y in range(4) for z in range(2) for x in range(4)]


def core_swap(v):
    return lax.ppermute(v, "mp", CORE)


def z_swap(v):
    return lax.ppermute(v, "mp", ZLO)


def rows_of(v, start, size):
    return lax.dynamic_slice_in_dim(v, start, size, 0)


def item_starts(len_ref):
    starts, total = [], jnp.int32(0)
    for j in range(8):
        starts.append(total)
        total = total + len_ref[0, j]
    return starts


def start_at(starts, place):
    best = jnp.int32(0)
    for s in starts[1:]:
        best = jnp.where(s <= place, jnp.maximum(best, s), best)
    return best


def chunk_masks(starts, base):
    row = lax.broadcasted_iota(jnp.int32, (CH, CH), 0)
    col = lax.broadcasted_iota(jnp.int32, (CH, CH), 1)
    blk = jnp.bitwise_and(row, -BLK)
    row1 = lax.broadcasted_iota(jnp.int32, (CH, 128), 0)
    place = row1 + base
    low = jnp.zeros_like(place)
    for s in starts[1:]:
        low = jnp.where(place >= s, jnp.maximum(low, s), low)
    low = low - base
    blk1 = jnp.bitwise_and(row1, -BLK)
    carried = low < blk1
    low_wide = jnp.concatenate([low, low], axis=1)
    causal = (col <= row) & (col >= blk)
    visible = causal & (col >= low_wide)
    return visible, carried


def causal_ones():
    row = lax.broadcasted_iota(jnp.int32, (CH, CH), 0)
    col = lax.broadcasted_iota(jnp.int32, (CH, CH), 1)
    return jnp.where((col <= row) & (col >= jnp.bitwise_and(row, -BLK)), 1.0, 0.0).astype(BF16)


def two_parts(v):
    high = v.astype(BF16)
    return high, (v - high.astype(F32)).astype(BF16)


def block_scalars(starts, base, b):
    first = base + b * BLK
    origin = start_at(starts, first + BLK - 1)
    keep = jnp.where(origin < first, 1.0, 0.0).astype(F32)
    place = lax.broadcasted_iota(jnp.int32, (BLK, 128), 0) + first
    return keep, place >= origin


def scaled_parts(q, k, cum):
    last = jnp.broadcast_to(cum.reshape(CH // BLK, BLK, 128)[:, BLK - 1 :, :], (CH // BLK, BLK, 128))
    last = last.reshape(CH, 128)
    e, en, ef = jnp.exp(cum), jnp.exp(-cum), jnp.exp(last - cum)
    qf = q.astype(F32) * SCALE * e
    ks = k.astype(F32) * en
    kf = k.astype(F32) * ef
    return last, e, en, ef, qf, ks, kf


def mixer_forward(
    len_ref, tok_ref, g1_ref, wq_ref, wk_ref, wv_ref, wgd_ref, wgu_ref, bias_ref,
    n_ref, q_ref, k_ref, v_ref, low_ref, logit_ref, cum_ref, mixed_lo_ref, mixed_hi_ref, st_ref, state,
):
    step = pl.program_id(0)
    rows = tok_ref.shape[0]
    starts = item_starts(len_ref)

    @pl.when(step == 0)
    def _():
        state[...] = jnp.zeros_like(state)

    ones = causal_ones()
    s = state[...]
    for c in range(rows // CH):
        base = step * rows + c * CH
        at = slice(c * CH, (c + 1) * CH)
        x = tok_ref[at, :].astype(F32)
        r = lax.rsqrt(jnp.mean(x * x, axis=-1, keepdims=True) + EPS)
        n = (x * r * g1_ref[...]).astype(BF16)
        n_ref[at, :] = n
        low = nt(n, wgd_ref[...]).astype(BF16)
        low_ref[at, :] = low
        logits = nn(low, wgu_ref[...]) + bias_ref[...]
        logit_ref[at, :] = logits
        decays = (jnp.minimum(logits, 0.0) - jnp.log1p(jnp.exp(-jnp.abs(logits)))) * (1.0 / 16.0)
        high, rest = two_parts(decays)
        cum = nn(ones, high) + nn(ones, rest)
        cum_ref[at, :] = cum
        q = nn(n, wq_ref[...]).astype(BF16)
        k = nn(n, wk_ref[...]).astype(BF16)
        v = nn(n, wv_ref[...]).astype(BF16)
        q_ref[at, :] = q
        k_ref[at, :] = k
        v_ref[at, :] = v
        visible, carried = chunk_masks(starts, base)
        last, e, en, ef, qf, ks, kf = scaled_parts(q, k, cum)
        scores = jnp.where(visible, nt(qf.astype(BF16), ks.astype(BF16)), 0.0).astype(BF16)
        out = nn(scores, v)
        q_carried = jnp.where(carried, qf, 0.0).astype(BF16)
        mixed_parts = []
        for b in range(CH // BLK):
            sl = slice(b * BLK, (b + 1) * BLK)
            keep, tail = block_scalars(starts, base, b)
            st_ref[c * (CH // BLK) + b] = s
            inter = nt(q_carried[sl], s.astype(BF16))
            mixed_parts.append((out[sl] + inter).astype(BF16).astype(F32))
            k_tail = jnp.where(tail, kf[sl], 0.0).astype(BF16)
            s = keep * jnp.exp(last[b * BLK : b * BLK + 1]) * s + tn(v[sl], k_tail)
        mixed = jnp.concatenate(mixed_parts, axis=0)

        @pl.when(step < 2)
        def _(mixed=mixed):
            mixed_lo_ref[...] = mixed

        @pl.when(step >= 2)
        def _(mixed=mixed):
            mixed_hi_ref[...] = mixed

    state[...] = s


def run_mixer_forward(lengths, tokens, g1, wq, wk, wv, wgd, wgu, bias):
    t = tokens.shape[0]
    whole = lambda a: pl.BlockSpec(a.shape, lambda i: (0,) * a.ndim)
    rows = lambda c: pl.BlockSpec((CH, c), lambda i: (i, 0))
    nb = CH // BLK
    outs = [
        ((t, 1024), BF16), ((t, 128), BF16), ((t, 128), BF16), ((t, 256), BF16), ((t, 16), BF16), ((t, 128), F32), ((t, 128), F32),
    ]
    sds = jax.ShapeDtypeStruct
    return pl.pallas_call(
        mixer_forward,
        grid=(t // CH,),
        in_specs=[pl.BlockSpec(memory_space=pltpu.SMEM), rows(1024), whole(g1), whole(wq), whole(wk), whole(wv),
                  whole(wgd), whole(wgu), whole(bias)],
        out_specs=[rows(s[1]) for s, _ in outs]
        + [pl.BlockSpec((CH, 256), lambda i: (jnp.minimum(i, 1), 0)), pl.BlockSpec((CH, 256), lambda i: (jnp.maximum(i - 2, 0), 0)),
           pl.BlockSpec((nb, 256, 128), lambda i: (i, 0, 0))],
        out_shape=[sds(s, d) for s, d in outs] + [sds((t // 2, 256), F32)] * 2 + [sds((t // BLK, 256, 128), F32)],
        scratch_shapes=[pltpu.VMEM((256, 128), F32)],
        compiler_params=pltpu.CompilerParams(vmem_limit_bytes=VMEM_BYTES),
        cost_estimate=weight(10),
        name="mixer_forward",
    )(lengths, tokens, g1, wq, wk, wv, wgd, wgu, bias)


def before_feed_kernel(w0_ref, w1_ref, w2_ref, w3_ref, cot_ref, wd_ref, wo_ref, gh_ref):
    for j, w_ref in enumerate((w0_ref, w1_ref, w2_ref, w3_ref)):

        @pl.when(pl.program_id(0) == j)
        def _(w_ref=w_ref):
            wo_ref[...] = w_ref[...].astype(BF16)

    gh_ref[...] = nt(cot_ref[...], wd_ref[...])


def run_before_feed(wo, cot, wd):
    t = cot.shape[0]
    whole = lambda a: pl.BlockSpec(a.shape, lambda s: (0,) * a.ndim)
    rows = lambda c: pl.BlockSpec((CH, c), lambda s: (s, 0))
    return pl.pallas_call(
        before_feed_kernel,
        grid=(t // CH,),
        in_specs=[whole(w) for w in wo] + [rows(1024), whole(wd)],
        out_specs=[rows(1024), rows(704)],
        out_shape=[jax.ShapeDtypeStruct((t, 1024), BF16), jax.ShapeDtypeStruct((t, 704), F32)],
        compiler_params=pltpu.CompilerParams(vmem_limit_bytes=VMEM_BYTES),
        cost_estimate=weight(7),
        name="before_feed",
    )(*wo, cot, wd)


def feed_kernel(
    at_ref, tok_ref, gh_ref, m0_ref, m1_ref, m2_ref, m3_ref, wo_ref, g2_ref, wg_ref, wu_ref, wd_ref,
    mid_ref, n_ref, hid_ref, gg_ref, feed_out_ref, feed_keep_ref, part_out_ref, part_keep_ref,
):
    step = pl.program_id(0)

    mixed = jnp.concatenate([m0_ref[...], m1_ref[...], m2_ref[...], m3_ref[...]], axis=1).astype(BF16)
    mid = tok_ref[...].astype(F32) + nn(mixed, wo_ref[...])
    mid_ref[...] = mid
    r = lax.rsqrt(jnp.mean(mid * mid, axis=-1, keepdims=True) + EPS)
    n = (mid * r * g2_ref[...]).astype(BF16)
    n_ref[...] = n
    pre = nt(n, wg_ref[...])
    up = nt(n, wu_ref[...])
    sg = jax.nn.sigmoid(pre)
    act = pre * sg
    hid = (act * up).astype(BF16)
    hid_ref[...] = hid
    gh = gh_ref[...]
    gg = (gh * up * sg * (1.0 + pre * (1.0 - sg))).astype(BF16)
    gu = (gh * act).astype(BF16)
    gg_ref[:, 0:704] = gg
    gg_ref[:, 704:1408] = gu
    feed = nn(hid, wd_ref[...])
    part = nn(gg, wg_ref[...]) + nn(gu, wu_ref[...])

    @pl.when(step == 0)
    def _():
        feed_out_ref[...] = feed
        part_out_ref[...] = part

    @pl.when(step == 1)
    def _():
        feed_keep_ref[...] = feed
        part_keep_ref[...] = part


def run_feed(at, chunk, tokens, gh, mixed, wo, g2, wg, wu, wd):
    t = tokens.shape[0] // 2
    whole = lambda a: pl.BlockSpec(a.shape, lambda s, at: (0,) * a.ndim)
    half = lambda s, at: jnp.bitwise_xor(1 - at[2], s)
    rows = lambda c: pl.BlockSpec((CH, c), lambda s, at: (half(s, at), 0))
    from_all = lambda c: pl.BlockSpec((CH, c), lambda s, at: (2 * chunk + half(s, at), 0))
    once = pl.BlockSpec((CH, 1024), lambda s, at: (0, 0))
    sds = jax.ShapeDtypeStruct
    return pl.pallas_call(
        feed_kernel,
        grid_spec=pltpu.PrefetchScalarGridSpec(
            num_scalar_prefetch=1,
            grid=(t // CH,),
            in_specs=[from_all(1024), from_all(704)] + [rows(256)] * 4 + [whole(wo), whole(g2), whole(wg), whole(wu), whole(wd)],
            out_specs=[rows(1024), rows(1024), rows(704), rows(1408), once, once, once, once],
        ),
        out_shape=[sds((t, 1024), F32), sds((t, 1024), BF16), sds((t, 704), BF16), sds((t, 1408), BF16)] + [sds((CH, 1024), F32)] * 4,
        compiler_params=pltpu.CompilerParams(vmem_limit_bytes=VMEM_BYTES),
        cost_estimate=weight(14),
        name="feed_both_ways",
    )(at, tokens, gh, *mixed, wo, g2, wg, wu, wd)


def mixer_backward(
    at_ref, len_ref, *refs,
):
    gm_refs, gain_ref, refs = refs[:4], refs[4], refs[5:]
    (tok_ref, n_ref, q_ref, k_ref, v_ref, low_ref, logit_ref, cum_ref,
     st_ref, wo_ref, wq_ref, wk_ref, wv_ref, wgd_ref, wgu_ref,
     dqkv_ref, far0_ref, far1_ref, near0_ref, near1_ref, part_keep_ref, ga_ref, small_ref, gup_ref, bias_ref, dstate, whole) = refs
    step = pl.program_id(0)
    steps = pl.num_programs(0)
    rows = tok_ref.shape[0]
    starts = item_starts(len_ref)

    core, z = at_ref[2], at_ref[3]
    here = steps - 1 - step
    mine = jnp.equal(lax.rem(here, 2), core)

    @pl.when(step == 0)
    def _():
        dstate[...] = jnp.zeros_like(dstate)
        small_ref[...] = jnp.zeros_like(small_ref)
        small_ref[17:18, :] = gain_ref[0:1, :]
        gup_ref[...] = jnp.zeros_like(gup_ref)
        bias_ref[...] = jnp.zeros_like(bias_ref)

    first = pl.multiple_of(z * 128, 128)
    second = pl.multiple_of((1 - z) * 128, 128)
    for other in range(2):

        @pl.when(jnp.logical_not(mine) if other else mine)
        def _(other=other):
            ga_ref[pl.ds(first, 128), :] = gm_refs[2 * other][...].astype(BF16)
            ga_ref[pl.ds(second, 128), :] = gm_refs[2 * other + 1][...].astype(BF16)

    ones = causal_ones()
    ds = dstate[...]
    for c in reversed(range(rows // CH)):
        base = here * rows + c * CH
        at = slice(c * CH, (c + 1) * CH)
        g = nt(ga_ref[at, :], wo_ref[...]).astype(BF16)
        q, k, v, cum = q_ref[at, :], k_ref[at, :], v_ref[at, :], cum_ref[at, :]
        visible, carried = chunk_masks(starts, base)
        last, e, en, ef, qf, ksf, kff = scaled_parts(q, k, cum)
        qs, ks = qf.astype(BF16), ksf.astype(BF16)
        scores = jnp.where(visible, nt(qs, ks), 0.0).astype(BF16)
        dscores = jnp.where(visible, nt(g, v), 0.0).astype(BF16)
        dv = tn(scores, g)
        dqs = nn(dscores, ks)
        dks = tn(dscores, qs)
        q_carried = jnp.where(carried, qf, 0.0).astype(BF16)
        dvs, dkfs, dqss, dls = [], [], [], []
        for b in reversed(range(CH // BLK)):
            sl = slice(b * BLK, (b + 1) * BLK)
            keep, tail = block_scalars(starts, base, b)
            dsb = ds.astype(BF16)
            s = st_ref[c * (CH // BLK) + b]
            k_tail = jnp.where(tail, kff[sl], 0.0).astype(BF16)
            dvs.append(dv[sl] + nt(k_tail, dsb))
            dkf = jnp.where(tail, nn(v[sl], dsb), 0.0)
            dkfs.append(dkf)
            dqss.append(dqs[sl] + jnp.where(carried[sl], nn(g[sl], s.astype(BF16)), 0.0))
            grow = keep * jnp.exp(last[b * BLK : b * BLK + 1])
            dlast = grow * jnp.sum(s * ds, axis=0, keepdims=True) + jnp.sum(dkf * kff[sl], axis=0, keepdims=True)
            dls.append(jnp.broadcast_to(dlast, (BLK, 128)))
            ds = grow * ds + tn(g[sl], q_carried[sl])
        join = lambda parts: jnp.concatenate(parts[::-1], axis=0)
        dqs, dkf, dl = join(dqss), join(dkfs), join(dls)
        dq = (dqs * (SCALE * e)).astype(BF16)
        dk = (dks * en + dkf * ef).astype(BF16)
        dv = join(dvs).astype(BF16)
        dqkv_ref[at, 0:128] = dq
        dqkv_ref[at, 128:256] = dk
        dqkv_ref[at, 256:512] = dv
        high, rest = two_parts(dqs * qf - dks * ksf - dkf * kff)
        ddec = tn(ones, high) + tn(ones, rest) + dl
        glog = ddec * jax.nn.sigmoid(-logit_ref[at, :]) * (1.0 / 16.0)
        bias_ref[0:1, :] += jnp.sum(glog, axis=0, keepdims=True)
        high, rest = two_parts(glog)
        gup_ref[...] += tn(low_ref[at, :], high) + tn(low_ref[at, :], rest)
        glr = (nt(high, wgu_ref[...]) + nt(rest, wgu_ref[...])).astype(BF16)
        part = nt(dq, wq_ref[...]) + nt(dk, wk_ref[...]) + nt(dv, wv_ref[...]) + nn(glr, wgd_ref[...])
        @pl.when(mine)
        def _(part=part):
            part_keep_ref[...] = part

        for chunk, (far_ref, near_ref) in enumerate(((far0_ref, near0_ref), (far1_ref, near1_ref))):

            @pl.when(jnp.logical_and(jnp.logical_not(mine), jnp.equal(lax.div(here, 2), chunk)))
            def _(part=part, far_ref=far_ref, near_ref=near_ref):
                whole[...] = part
                far_ref[...] = whole[pl.ds(second, 128), :]
                near_ref[...] = whole[pl.ds(first, 128), :]

        small_ref[0:16, :] += tn(glr, n_ref[at, :])
        x = tok_ref[at, :].astype(F32)
        r = lax.rsqrt(jnp.mean(x * x, axis=-1, keepdims=True) + EPS)
        small_ref[16:17, :] += jnp.sum(part * x * r, axis=0, keepdims=True)
    dstate[...] = ds


def run_mixer_backward(at, lengths, gm, gain, tokens, n, q, k, v, low, logits, cum, st, wo, wq, wk, wv, wgd, wgu):
    t = tokens.shape[0]
    steps = t // CH
    whole = lambda a: pl.BlockSpec(a.shape, lambda i, at: (0,) * a.ndim)
    rows = lambda c: pl.BlockSpec((CH, c), lambda i, at: (steps - 1 - i, 0))
    split = pl.BlockSpec((CH, 1024), lambda i, at: (lax.div(steps - 1 - i, 2), 0))
    nb = CH // BLK
    fixed = lambda s: pl.BlockSpec(s, lambda i, at: (0, 0))
    sds = jax.ShapeDtypeStruct
    return pl.pallas_call(
        mixer_backward,
        grid_spec=pltpu.PrefetchScalarGridSpec(
            num_scalar_prefetch=1,
            grid=(steps,),
            in_specs=[pl.BlockSpec(memory_space=pltpu.SMEM)] + [pl.BlockSpec((128, 1024), lambda i, at: (lax.div(steps - 1 - i, 2), 0))] * 4 + [whole(gain)]
            + [rows(1024), rows(1024), rows(128), rows(128), rows(256), rows(16), rows(128), rows(128),
               pl.BlockSpec((nb, 256, 128), lambda i, at: (steps - 1 - i, 0, 0)),
               whole(wo), whole(wq), whole(wk), whole(wv), whole(wgd), whole(wgu)],
            out_specs=[rows(512)] + [fixed((128, 1024))] * 4 + [split, rows(1024), fixed((24, 1024)), fixed((16, 128)), fixed((8, 128))],
            scratch_shapes=[pltpu.VMEM((256, 128), F32), pltpu.VMEM((CH, 1024), F32)],
        ),
        out_shape=[sds((t, 512), BF16)] + [sds((128, 1024), F32)] * 4 + [sds((t // 2, 1024), F32), sds((t, 1024), BF16),
                   sds((24, 1024), F32), sds((16, 128), F32), sds((8, 128), F32)],
        compiler_params=pltpu.CompilerParams(vmem_limit_bytes=VMEM_BYTES),
        cost_estimate=weight(BACK_US),
        name="mixer_backward",
    )(at, lengths, *gm, gain, tokens, n, q, k, v, low, logits, cum, st, wo, wq, wk, wv, wgd, wgu)


SMALL = dict(
    compiler_params=pltpu.CompilerParams(vmem_limit_bytes=VMEM_BYTES),
    cost_estimate=weight(3),
)


def quarter(v, j, which):
    return rows_of(v, 256 * j + 128 * which, 128)


def norm_gradient(dn, y, gain):
    r = lax.rsqrt(jnp.mean(y * y, axis=-1, keepdims=True) + EPS)
    gd = dn * gain
    dy = r * gd - (r * r * r) * y * jnp.mean(gd * y, axis=-1, keepdims=True)
    return dy, jnp.sum(dn * y * r, axis=0, keepdims=True)


def second_norm_kernel(at_ref, a0_ref, b0_ref, c0_ref, y0_ref, a1_ref, b1_ref, c1_ref, y1_ref, gain_ref, base0_ref, base1_ref, o_ref, s_ref):
    halves = ((a0_ref, b0_ref, c0_ref, y0_ref, base0_ref), (a1_ref, b1_ref, c1_ref, y1_ref, base1_ref))
    total = jnp.zeros((1, 1024), F32)
    for j, (a_ref, b_ref, c_ref, y_ref, base_ref) in enumerate(halves):
        dy, dgain = norm_gradient(a_ref[...] + b_ref[...] + c_ref[...], y_ref[...], gain_ref[...])
        o_ref[128 * j : 128 * (j + 1)] = base_ref[...].astype(F32) + dy
        total = total + dgain
    s_ref[0:1, :] = total


def run_second_norm(at, keep, got, far, middle, gain, cot):
    of_half = pl.BlockSpec((128, 1024), lambda s, at: (at[3], 0))
    of_chunk = pl.BlockSpec((128, 1024), lambda s, at: (2 * at[2] + at[3], 0))
    of_all = lambda j: pl.BlockSpec((128, 1024), lambda s, at: (4 * j + 2 * at[2] + at[3], 0))
    fixed = lambda *s: pl.BlockSpec(s, lambda s, at: (0, 0))
    ops = [v for j in range(2) for v in (keep[j], got[j], far[j], middle[j])]
    return pl.pallas_call(
        second_norm_kernel,
        grid_spec=pltpu.PrefetchScalarGridSpec(
            num_scalar_prefetch=1, grid=(1,),
            in_specs=[of_half, of_half, fixed(128, 1024), of_chunk] * 2 + [fixed(1, 1024), of_all(0), of_all(1)],
            out_specs=[fixed(256, 1024), fixed(8, 1024)]),
        out_shape=[jax.ShapeDtypeStruct((256, 1024), F32), jax.ShapeDtypeStruct((8, 1024), F32)],
        name="second_norm_back",
        **SMALL,
    )(at, *ops, gain, cot, cot)


def first_norm_kernel(at_ref, a_ref, b0_ref, b1_ref, c_ref, y_ref, base_ref, gain_ref, own_ref):
    for j, b_ref in enumerate((b0_ref, b1_ref)):

        @pl.when(pl.program_id(0) == j)
        def _(b_ref=b_ref):
            dy, _ = norm_gradient(a_ref[...] + b_ref[...] + c_ref[...], y_ref[...].astype(F32), gain_ref[...])
            own_ref[...] = dy + base_ref[...]


def run_first_norm(at, keep, got, far, tokens, base, gain):
    of_half = pl.BlockSpec((128, 1024), lambda s, at: (2 * s + at[3], 0))
    of_all = pl.BlockSpec((128, 1024), lambda s, at: (4 * s + 2 * at[2] + at[3], 0))
    own = pl.BlockSpec((128, 1024), lambda s, at: (s, 0))
    fixed = lambda *n: pl.BlockSpec(n, lambda s, at: (0, 0))
    return pl.pallas_call(
        first_norm_kernel,
        grid_spec=pltpu.PrefetchScalarGridSpec(
            num_scalar_prefetch=1, grid=(2,),
            in_specs=[of_half, fixed(128, 1024), fixed(128, 1024), own, of_all, own, fixed(1, 1024)], out_specs=own),
        out_shape=jax.ShapeDtypeStruct((256, 1024), F32),
        name="first_norm_back",
        **SMALL,
    )(at, keep, *got, far, tokens, base, gain)


def place_kernel(at_ref, r0_ref, g0_ref, r1_ref, g1_ref, *rest):
    result_ref, grad_ref = rest[-2:]

    @pl.when(lax.rem(pl.program_id(0), 2) == 0)
    def _():
        result_ref[...] = r0_ref[...].astype(BF16)
        grad_ref[...] = g0_ref[...]

    @pl.when(lax.rem(pl.program_id(0), 2) == 1)
    def _():
        result_ref[...] = r1_ref[...].astype(BF16)
        grad_ref[...] = g1_ref[...]


def run_place(at, odd, pieces, into=()):
    chunk = lambda s: lax.div(s, 2)
    place = lambda s, at: jnp.bitwise_xor(2 * at[2] + at[3], 2 * lax.rem(s, 2) + odd)
    piece = pl.BlockSpec((128, 1024), lambda s, at: (chunk(s), 0))
    placed = pl.BlockSpec((128, 1024), lambda s, at: (4 * chunk(s) + place(s, at), 0))
    return pl.pallas_call(
        place_kernel,
        grid_spec=pltpu.PrefetchScalarGridSpec(
            num_scalar_prefetch=1, grid=(4,),
            in_specs=[piece] * 4 + [pl.BlockSpec(memory_space=pl.ANY)] * len(into),
            out_specs=[placed, placed]),
        out_shape=[jax.ShapeDtypeStruct((1024, 1024), BF16), jax.ShapeDtypeStruct((1024, 1024), F32)],
        input_output_aliases={5: 0, 6: 1} if into else {},
        name="place_rows",
        **SMALL,
    )(at, *pieces, *into)


def feed_grads_kernel(l0_ref, l1_ref, r0_ref, r1_ref, c0_ref, c1_ref, h0_ref, h1_ref, out):
    w1, w2 = r0_ref.shape[1], h0_ref.shape[1]
    first = tn(l0_ref[...], r0_ref[...]) + tn(l1_ref[...], r1_ref[...])
    second = tn(c0_ref[...], h0_ref[...]) + tn(c1_ref[...], h1_ref[...])
    for x in range(4):
        for zh in range(2):
            row = zh * 128 + x * 32
            out[x, 0, zh, :, 0:w1] = first[row : row + 32]
            out[x, 0, zh, :, w1 : w1 + w2] = second[row : row + 32]
            out[x, 0, zh, :, w1 + w2 :] = jnp.zeros((32, out.shape[-1] - w1 - w2), F32)


def run_feed_grads(n2, gg, cot, hid):
    t = cot.shape[0] // 2
    c = gg[0].shape[1] + hid[0].shape[1]
    wide = -(-c // 128) * 128
    cols = lambda j: pl.BlockSpec((t, CH), lambda s: (j, s))
    whole = lambda a: pl.BlockSpec(a.shape, lambda s: (0, 0))
    return pl.pallas_call(
        feed_grads_kernel,
        grid=(4,),
        in_specs=[cols(0), cols(0), whole(gg[0]), whole(gg[1]), cols(0), cols(1), whole(hid[0]), whole(hid[1])],
        out_specs=pl.BlockSpec((4, 1, 2, 32, wide), lambda s: (0, s, 0, 0, 0)),
        out_shape=jax.ShapeDtypeStruct((4, 4, 2, 32, wide), F32),
        compiler_params=pltpu.CompilerParams(vmem_limit_bytes=VMEM_BYTES),
        cost_estimate=weight(12),
        name="feed_weight_grads",
    )(n2[0], n2[1], gg[0], gg[1], cot, cot, hid[0], hid[1])


RING_OUTS = ((0, None, 0), (2, 0, 1), (1, 1, 1), (3, 0, 2), (2, 1, 2), (1, 0, 3), (3, 1, 4))


def mixer_grads_kernel(at_ref, l_ref, r0_ref, a0_ref, m0_ref, m1_ref, small_ref, gup_ref, bias_ref, *outs):
    step = pl.program_id(0)
    w1 = r0_ref.shape[1]

    @pl.when(step < 4)
    def _():
        n = m0_ref.shape[0]
        first = tn(l_ref[...], r0_ref[...])
        second = tn(a0_ref[0:n], m0_ref[...].astype(BF16)) + tn(a0_ref[n:], m1_ref[...].astype(BF16))

        def write(ref, x, to):
            for zh in range(2):
                row = zh * 128 + x * 32
                ref[2 * to + zh, :, 0:w1] = first[row : row + 32]
                ref[2 * to + zh, :, w1:] = second[row : row + 32]

        offset = lax.rem(step - at_ref[1] + 4, 4)

        for k, late, ref in RING_OUTS:

            @pl.when(offset == k)
            def _(late=late, ref=ref):
                for x in range(4):
                    if late is None or late == x // 2:
                        write(outs[ref], x, x if ref < 3 else x % 2)

    @pl.when(step == 4)
    def _():
        small = small_ref[...]
        for out in (outs[0], outs[1], outs[2], outs[4]):
            last = out.shape[0] - 1
            out[last] = jnp.zeros(out.shape[1:], F32)
            out[last, 0:16, :] = small[0:16, 0:768]
            for j in range(3):
                n = min(6, 16 - 6 * j)
                out[last, 16 : 16 + n, 256 * j : 256 * (j + 1)] = small[6 * j : 6 * j + n, 768:1024]
            for j in range(6):
                n = min(3, 16 - 3 * j)
                out[last, 22 : 22 + n, 128 * j : 128 * (j + 1)] = gup_ref[3 * j : 3 * j + n, :]
            out[last, 25:26, :] = small[16:17, 0:768]
            out[last, 26:27, :] = small[17:18, 0:768]
            out[last, 27:28, 0:256] = small[16:17, 768:1024]
            out[last, 27:28, 256:512] = small[17:18, 768:1024]
            out[last, 27:28, 512:640] = bias_ref[0:1, :]


def run_mixer_grads(at, n1, dqkv, ga, mixed, small, gup, bias):
    t, c = n1.shape[0], dqkv.shape[1] + mixed[0].shape[1]
    cols = pl.BlockSpec((t, CH), lambda s, at: (0, jnp.minimum(s, 3)))
    whole = lambda a: pl.BlockSpec(a.shape, lambda s, at: (0, 0))
    rest = [small, gup, bias]
    counts = [9, 9, 9, 4, 5]
    return pl.pallas_call(
        mixer_grads_kernel,
        grid_spec=pltpu.PrefetchScalarGridSpec(
            num_scalar_prefetch=1, grid=(5,),
            in_specs=[cols, whole(dqkv), cols, whole(mixed[0]), whole(mixed[1])] + [whole(a) for a in rest],
            out_specs=[pl.BlockSpec((n, 32, c), lambda s, at: (0, 0, 0)) for n in counts]),
        out_shape=[jax.ShapeDtypeStruct((n, 32, c), F32) for n in counts],
        compiler_params=pltpu.CompilerParams(vmem_limit_bytes=VMEM_BYTES),
        cost_estimate=weight(8),
        name="mixer_weight_grads",
    )(at, n1, dqkv, ga, mixed[0], mixed[1], *rest)


def unpack_kernel(
    own_ref, got_ref, a_ref, b_ref, sums_ref, far_ref,
    g1_ref, down_ref, up_ref, bias_ref, g2_ref, q_ref, k_ref, v_ref, o_ref, gate_ref, mup_ref, mdown_ref,
):
    rows = own_ref[...] + got_ref[...]
    feed = a_ref[...] + b_ref[...]
    own = rows[:, 768:1536]
    sums = sums_ref[...] + far_ref[...]
    wide = jnp.concatenate([sums[16:22, 0:256], sums[16:22, 256:512], sums[16:20, 512:768]], axis=0)
    down_ref[...] = jnp.concatenate([sums[0:16], wide], axis=1)
    for j in range(6):
        n = min(3, 16 - 3 * j)
        up_ref[3 * j : 3 * j + n, :] = own[22 : 22 + n, 128 * j : 128 * (j + 1)]
    g1_ref[:, 0:768] = sums[25:26]
    g1_ref[:, 768:1024] = sums[27:28, 0:256]
    g2_ref[:, 0:768] = sums[26:27]
    g2_ref[:, 768:1024] = sums[27:28, 256:512]
    bias_ref[...] = own[27:28, 512:640]
    q_ref[...] = rows[:, 0:128]
    k_ref[...] = rows[:, 128:256]
    v_ref[...] = rows[:, 256:512]
    o_ref[...] = rows[:, 512:768]
    gate_ref[...] = feed[:, 0:704]
    mup_ref[...] = feed[:, 704:1408]
    mdown_ref[...] = feed[:, 1408:2112]


def unpack(own, got, feed_own, feed_got, sums, far):
    shapes = [(1, 1024), (16, 1024), (16, 128), (1, 128), (1, 1024), (32, 128), (32, 128), (32, 256), (32, 256)] + [(32, 704)] * 3
    return pl.pallas_call(
        unpack_kernel, out_shape=[jax.ShapeDtypeStruct(s, F32) for s in shapes], name="unpack", **SMALL,
    )(own, got, feed_own, feed_got, sums, far)


def after(value, *others):
    return lax.optimization_barrier((value, others))[0]


def send(v, shifts, d):
    return lax.ppermute(v, "dp", shifts[d])


GX = [[(y * 2 + z) * 4 + x for x in range(4)] for y in range(4) for z in range(2)]
GY = [[(y * 2 + z) * 4 + x for y in range(4)] for x in range(4) for z in range(2)]


def scatter_rows(v, groups):
    return lax.psum_scatter(v, "dp", scatter_dimension=0, tiled=True, axis_index_groups=groups)


def ring_first(v, shifts):
    return lax.ppermute(v[1], "dp", shifts[1]), lax.ppermute(v[2], "dp", shifts[3])


def ring_on(v, got):
    n = v[3].shape[0]
    return v[3] + got[0][:n], v[4] + got[1][n:]


def ring_last(on, shifts):
    return lax.ppermute(on[0], "dp", shifts[1]), lax.ppermute(on[1], "dp", shifts[3])


def ring_total(v, got, last):
    n = last[0].shape[0]
    return jnp.concatenate([v[0][:n] + last[0] + got[1][:n], v[0][n:] + got[0][n:] + last[1]], axis=0)


def pick(v, i, dim):
    return lax.dynamic_index_in_dim(v, i, dim, False)


def swap_zh(v, zh, dim):
    return pick(v, zh, dim) + lax.ppermute(pick(v, 1 - zh, dim), "dp", ZH)


def local(tokens, lengths, g1, wq, wk, wv, wgd, wgu, bias, wout, g2, wg, wu, wd, cot):
    mp, dp = lax.axis_index("mp"), lax.axis_index("dp")
    core, z = mp % 2, mp // 2
    ix, zh, iy = dp % 4, (dp // 4) % 2, dp // 8
    at = jnp.stack([ix, iy, core, z]).astype(jnp.int32)
    g1r, g2r, biasr = g1.reshape(1, -1), g2.reshape(1, -1), bias.reshape(1, -1)
    wgd_t, wg_t, wu_t = wgd.T, wg.T, wu.T

    def phase(*values):
        return lax.optimization_barrier(values)

    def across(v, at_here, shifts, take):
        return [take(v, at_here)] + [send(take(v, (at_here + k) % 4), shifts, k) for k in (1, 3, 2)]

    with jax.named_scope("out_weights"):
        wide = wout.astype(F32)
        wout_z = z_swap(wide)
        wout_c = core_swap(wide)
    n1, q, k, v, low, logits, cum, mixed_lo, mixed_hi, st = run_mixer_forward(
        lengths, after(tokens, wide), g1r, wq, wk, wv, wgd_t, wgu, biasr)
    wout_z, wout_c, mixed_lo, mixed_hi = phase(wout_z, wout_c, mixed_lo, mixed_hi)

    with jax.named_scope("heads_one"):
        hi_z = z_swap(mixed_hi)
        hi_c = core_swap(mixed_hi)
        lo_c = core_swap(mixed_lo)
        wout_cz = core_swap(wout_z)
    wo, gh = run_before_feed((wout, wout_z, wout_c, wout_cz), cot, wd)
    hi_z, hi_c, lo_c, mixed_lo, wo, gh = phase(hi_z, hi_c, lo_c, mixed_lo, wo, gh)

    with jax.named_scope("heads_two"):
        lo_z = z_swap(mixed_lo)
        hi_cz = core_swap(hi_z)
    one = run_feed(at, 1, tokens, gh, (mixed_hi, hi_z, hi_c, hi_cz), wo, g2r, wg_t, wu_t, wd)
    lo_z, one = phase(lo_z, one)

    with jax.named_scope("second_norm_core"):
        part_in1 = core_swap(one[6])
        dn2_out1 = quarter(one[7], 0, 1 - z) + quarter(part_in1, 0, 1 - z)
    dn2_out1, part_in1, one, lo_z = phase(dn2_out1, part_in1, one, lo_z)

    with jax.named_scope("second_norm_z"):
        dn2_z1 = z_swap(dn2_out1)
        lo_cz = core_swap(lo_z)
    zero = run_feed(at, 0, tokens, gh, (mixed_lo, lo_z, lo_c, lo_cz), wo, g2r, wg_t, wu_t, wd)
    dn2_z1, zero = phase(dn2_z1, zero)

    with jax.named_scope("second_norm_core"):
        part_in0 = core_swap(zero[6])
        dn2_out0 = quarter(zero[7], 0, 1 - z) + quarter(part_in0, 0, 1 - z)
    dn2_out0, part_in0, one, zero = phase(dn2_out0, part_in0, one, zero)

    middle, n2, hid, gg, feed_out, feed_keep, _, part_keep = zip(zero, one)
    with jax.named_scope("second_norm_z"):
        dn2_z0 = z_swap(dn2_out0)
        feed_in = [core_swap(f) for f in feed_out]
    a = run_feed_grads(n2, gg, cot, hid)
    dn2_z0, feed_in, a = phase(dn2_z0, feed_in, a)

    gm0, gain2 = run_second_norm(at, part_keep, (part_in0, part_in1), (dn2_z0, dn2_z1), middle, g2r, cot)
    gm0, a, feed_in = phase(gm0, a, feed_in)
    with jax.named_scope("second_norm_join"):
        gm1 = z_swap(gm0)
        gm2 = core_swap(gm0)
    with jax.named_scope("feed_grads_x"):
        a = scatter_rows(a.reshape(1024, a.shape[-1]), GX)
    with jax.named_scope("feed_sum"):
        feed_z_out = jnp.concatenate([quarter(feed_keep[j], 0, 1 - z) + quarter(feed_in[j], 0, 1 - z) for j in range(2)], axis=0)
    gm1, gm2, feed_z_out = phase(gm1, gm2, feed_z_out)

    with jax.named_scope("second_norm_join"):
        gm3 = core_swap(gm1)

    with jax.named_scope("feed_sum"):
        feed_z = z_swap(feed_z_out)
    gm = (gm0, gm1, gm2, gm3)
    dqkv, *part1_out, part1_keep, ga, small, gup, gbias = run_mixer_backward(
        at, lengths, gm, gain2, tokens, n1, q, k, v, low, logits, cum, st, wout, wq, wk, wv, wgd_t, wgu)
    with jax.named_scope("first_norm_core"):
        part1_in = [core_swap(p) for p in part1_out]
    c = run_mixer_grads(at, n1, dqkv, ga, (mixed_lo, mixed_hi), small, gup, gbias)
    feed_z, part1_in, part1_keep, c = phase(feed_z, part1_in, part1_keep, c)

    dn1_out = jnp.concatenate([quarter(part1_keep, j, 1 - z) + part1_in[j] for j in range(2)], axis=0)
    dn1_out, c = phase(dn1_out, c)
    with jax.named_scope("first_norm_z"):
        dn1_z = z_swap(dn1_out)
    with jax.named_scope("mixer_grads_first"):
        c_got = ring_first(c, YS)
    feed_own = jnp.concatenate([
        quarter(feed_keep[j], 0, z) + quarter(feed_in[j], 0, z) + feed_z[128 * j : 128 * (j + 1)]
        + rows_of(middle[j], 256 * core + 128 * z, 128) for j in range(2)], axis=0)
    with jax.named_scope("result_join"):
        feed1 = z_swap(feed_own)
    grad0 = run_first_norm(at, part1_keep, part1_in[2:], dn1_z, tokens, gm0, g1r)
    with jax.named_scope("mixer_grads_last"):
        c_last = ring_last(ring_on(c, c_got), YS)
        c = ring_total(c, c_got, c_last)
    with jax.named_scope("grad_join"):
        grad2 = core_swap(grad0)
    with jax.named_scope("result_join"):
        feed2 = core_swap(feed_own)
    feed1, feed2, grad0, grad2, c, feed_own, a = phase(feed1, feed2, grad0, grad2, c, feed_own, a)

    with jax.named_scope("grad_join"):
        grad1 = z_swap(grad0)
    with jax.named_scope("feed_grads_y"):
        a = scatter_rows(a, GY).reshape(2, 32, -1)
    with jax.named_scope("mixer_grads_two"):

        def with_small(i):
            return jnp.concatenate([rows_of(c, 2 * (i % 4), 2), c[8:9]], axis=0)

        c_second = [with_small(ix)] + [send(with_small(ix + k), XS, k) for k in (1, 3, 2)]
    placed = run_place(at, 0, (feed_own, grad0, feed2, grad2))
    with jax.named_scope("mixer_grads_two"):
        c = sum(after(c_second, placed))
    with jax.named_scope("rows"):
        c = after(c, (grad1, placed))
        turned = lambda i: jnp.concatenate([pick(c, i, 0), c[2]], axis=1)
        own = turned(zh)
        got = lax.ppermute(turned(1 - zh), "dp", ZH)
        a_own = pick(a, zh, 0)
        a_out = after(pick(a, 1 - zh, 0), c)
        a_got = lax.ppermute(a_out, "dp", ZH)
    with jax.named_scope("result_join"):
        feed3 = core_swap(feed1)
    with jax.named_scope("grad_join"):
        grad3 = core_swap(after(grad1, c))
    result, grad_tokens = run_place(at, 1, (feed1, grad1, feed3, grad3), placed)
    with jax.named_scope("small_sums"):
        got = after(got, result)
        sums = own[:, 768:1536] + got[:, 768:1536]
        sums = sums + core_swap(sums)
        far = z_swap(sums)
        (gain_one, gate_down, gate_up, gate_bias, gain_two, d_query, d_key, d_value, d_out, d_gate, d_up, d_down) = unpack(
            own, got, a_own, a_got, sums, far)

    return (
        result,
        grad_tokens,
        gain_one.reshape(1024),
        d_query,
        d_key,
        d_value,
        gate_down.T,
        gate_up,
        gate_bias.reshape(128),
        d_out.T,
        gain_two.reshape(1024),
        d_gate,
        d_up,
        d_down.T,
    )


def solution(mesh):
    placed = (
        P("dp", None), P("dp", None), P(), P(None, "mp"), P(None, "mp"), P(None, "mp"), P(), P(None, "mp"),
        P("mp"), P("mp", None), P(), P(None, "mp"), P(None, "mp"), P("mp", None), P("dp", None),
    )
    outs = (
        P("dp", None), P("dp", None), P(), P("dp", "mp"), P("dp", "mp"), P("dp", "mp"), P(), P(None, "mp"),
        P("mp"), P("mp", "dp"), P(), P("dp", "mp"), P("dp", "mp"), P("mp", "dp"),
    )
    return jax.shard_map(local, mesh=mesh, in_specs=placed, out_specs=outs, check_vma=False)
```
